256 devices in a mesh: ctx: 32 (over z, x), tp: 4 (over y), dp: 2 (over core).
Axes of the slice: x: 4, y: 4, z: 8, core: 2. Of those that a mesh axis runs over, the one named last changes fastest.
Arguments:
- queries: bfloat16 [49152, 2048], P(('dp', 'ctx'), 'tp'), parts along dimension 0, may hold values from -6 to 6
- key_rows: bfloat16 [49152, 2048], P(('dp', 'ctx'), 'tp'), parts along dimension 0, may hold values from -6 to 6
- values: bfloat16 [49152, 2048], P(('dp', 'ctx'), 'tp'), parts along dimension 0, may hold values from -6 to 6
- doc_lengths: int32 [128], P('dp'), parts along dimension 0, may hold values from 1 to 2304, 24576 in all
- in_gate: bfloat16 [49152, 2048], P(('dp', 'ctx'), 'tp'), parts along dimension 0, may hold values from -6 to 6
- out_gate: bfloat16 [49152, 2048], P(('dp', 'ctx'), 'tp'), parts along dimension 0, may hold values from -6 to 6
- filter_taps: float32 [4096, 24576], P(('dp', 'tp'), 'ctx'), parts along dimension 0, may hold values from -0.078125 to 0.078125
Outputs:
- attn_out: bfloat16 [49152, 2048], P(('dp', 'ctx'), 'tp'), parts along dimension 0
- hyena_out: bfloat16 [49152, 2048], P(('dp', 'ctx'), 'tp'), parts along dimension 0
The draws below stay inside these ranges and needn't reach their ends.
There are 2 independent parts, one for each index of `dp`. The reference program is written for one: setup_inputs(seed, part) draws one part's arguments, and reference() takes and returns one part's arrays. A program takes and returns all parts, laid end to end along the dimension named above; each array names one. Nothing has to cross between parts.
Inputs may be any that keep to these rules, and one draw needn't show every extreme that they name: `doc_lengths`: the lengths sum to 24576, and the longest is exactly 2304.
All inputs are finite; a program needn't handle non-finite values.
Results may differ from the reference program's by a relative error of at most 0.012.
Values may be sent and summed in bfloat16 or wider, within the bound.
No kernel may reach another device: no remote copies, remote signals or barrier semaphores. Data moves between devices by JAX's collectives and lax.ppermute only.
A program may use at most 192 MiB of HBM per device.

```python
import math
import jax
import jax.numpy as jnp
import numpy as np
from jax import lax

HEADS = 16
HEAD_DIM = 128
TOK_DEV = 768
KV_REACH = 3
CHANNELS = 2048
SEQ = 24576
DOCS = 64
MOST_DOC = 2304


def paired_rows(key):
    folded = jax.random.fold_in(key, 4217)
    query_seed, key_seed = jax.random.split(folded, 2)
    channels = HEADS * HEAD_DIM
    query_draw = jnp.clip(jax.random.normal(query_seed, (SEQ, channels), jnp.float32), -6.0, 6.0)
    key_draw = jnp.clip(jax.random.normal(key_seed, (SEQ, channels), jnp.float32), -6.0, 6.0)
    return (query_draw, key_draw)


def draw_queries(key, part):
    return paired_rows(key)[0].astype(jnp.bfloat16)


def draw_key_rows(key, part):
    return paired_rows(key)[1].astype(jnp.bfloat16)


def levels(rng, shape, cuts, smallest, high):
    factor_of = 1.0
    for position, blocks in cuts:
        heights = jax.random.uniform(jax.random.fold_in(jax.random.fold_in(rng, 6), position), (blocks,), jnp.float32, smallest / len(cuts), high / len(cuts))
        factor_of = factor_of * jnp.repeat(jnp.exp(heights), shape[position] // blocks).reshape((-1,) + (1,) * (len(shape) - 1 - position))
    return factor_of


def split_up(amount, total, bound, slope):
    portions = [(1 << 20) // math.isqrt(grade ** slope) + 1 for grade in range(2, amount + 1)]
    spare, given = total - bound - (amount - 1), [1] * (amount - 1)
    while spare > 0:
        candidates = [i for i in range(amount - 1) if given[i] < bound]
        whole, budget = sum([portions[i] for i in candidates]), spare
        for i in candidates:
            extra = min(bound - given[i], max(1, budget * portions[i] // whole), spare)
            given[i] = given[i] + extra
            spare = spare - extra
    return np.array([bound] + given)


def ragged(key, number_of, total, most, slope):
    if number_of == 2:
        one = jax.random.randint(key, (), max(1, total - most), min(most, total - 1) + 1)
        return jnp.stack([one, total - one])
    tallies = jnp.asarray(split_up(number_of, total, most, slope), jnp.int32)
    twos = (number_of - 1) // 2
    giver, taker = tallies[1:1 + 2 * twos:2], tallies[2:2 + 2 * twos:2]
    room = jnp.minimum(giver - 1, most - taker)
    shifted = jax.random.randint(jax.random.fold_in(key, 1), (twos,), 0, 1 << 20) % (room + 1)
    tallies = tallies.at[1:1 + 2 * twos:2].set(giver - shifted).at[2:2 + 2 * twos:2].set(taker + shifted)
    return tallies[jax.random.permutation(jax.random.fold_in(key, 2), number_of)]


def noise(stream_key, extent, scale, most, cuts=(), held_as=jnp.bfloat16):
    factor_of = levels(stream_key, extent, cuts, -0.22, 0.18) if cuts else 1.0
    entries = jax.random.normal(stream_key, extent, jnp.float32) * scale * factor_of
    return jnp.minimum(jnp.maximum(entries, -most), most).astype(held_as)


def setup_inputs(seed: int = 0, part: int = 0) -> dict:
    key_list = jax.random.split(jax.random.key(seed), 8)
    part_keys = jax.random.split(jax.random.fold_in(key_list[7], part), 8)
    return {
        "queries": draw_queries(jax.random.fold_in(jax.random.fold_in(key_list[7], part), 71), part),
        "key_rows": draw_key_rows(jax.random.fold_in(jax.random.fold_in(key_list[7], part), 71), part),
        "values": noise(part_keys[2], (SEQ, CHANNELS), 1.0, 6.0, ((0, 32), (1, 4))),
        "doc_lengths": ragged(part_keys[3], DOCS, SEQ, MOST_DOC, 2).astype(jnp.int32),
        "in_gate": noise(part_keys[4], (SEQ, CHANNELS), 1.0, 6.0, ((0, 32), (1, 4))),
        "out_gate": noise(part_keys[5], (SEQ, CHANNELS), 1.0, 6.0, ((0, 32), (1, 4))),
        "filter_taps": noise(part_keys[6], (CHANNELS, SEQ), (SEQ // 4) ** -0.5, 0.078125, ((0, 4), (1, 32)), jnp.float32),
    }


masked_score = -1e+30

def doc_of(positions, doc_lengths):
    starts = jnp.cumsum(doc_lengths) - doc_lengths
    inside = (starts[None, :] <= positions[:, None]).astype(jnp.int32)
    return lax.optimization_barrier(jnp.sum(inside, axis=1)) - 1

def reference(queries, key_rows, values, doc_lengths, in_gate, out_gate, filter_taps):
    channels = queries.shape[1]
    head_count = channels // HEAD_DIM
    positions = jnp.arange(SEQ, dtype=jnp.int32)
    doc_index = doc_of(positions, doc_lengths)
    reach = KV_REACH * TOK_DEV
    window = reach + TOK_DEV
    padded_keys = jnp.concatenate([jnp.zeros((reach, channels), jnp.bfloat16), key_rows], axis=0)
    padded_values = jnp.concatenate([jnp.zeros((reach, channels), jnp.bfloat16), values], axis=0)
    padded_docs = jnp.concatenate([jnp.full((reach,), -1, jnp.int32), doc_index])
    padded_pos = jnp.concatenate([jnp.arange(reach, dtype=jnp.int32) - reach, positions])

    def one_block(block_index):
        block_start = (block_index * TOK_DEV).astype(jnp.int32)
        query_block = lax.dynamic_slice_in_dim(queries, block_start, TOK_DEV, 0).astype(jnp.float32).reshape(TOK_DEV, head_count, HEAD_DIM)
        query_pos = lax.dynamic_slice_in_dim(positions, block_start, TOK_DEV, 0)
        query_doc = lax.dynamic_slice_in_dim(doc_index, block_start, TOK_DEV, 0)
        key_block = lax.dynamic_slice_in_dim(padded_keys, block_start, window, 0).astype(jnp.float32).reshape(window, head_count, HEAD_DIM)
        value_block = lax.dynamic_slice_in_dim(padded_values, block_start, window, 0).astype(jnp.float32).reshape(window, head_count, HEAD_DIM)
        key_doc = lax.dynamic_slice_in_dim(padded_docs, block_start, window, 0)
        key_pos = lax.dynamic_slice_in_dim(padded_pos, block_start, window, 0)
        allowed = (key_doc[None, :] == query_doc[:, None]) & (key_pos[None, :] <= query_pos[:, None])
        scores = jnp.einsum('qhd,khd->hqk', query_block, key_block) / math.sqrt(HEAD_DIM)
        scores = jnp.where(allowed[None], scores, masked_score)
        top_score = lax.optimization_barrier(jnp.max(scores, axis=2, keepdims=True))
        exp_scores = jnp.exp(scores - top_score)
        row_total = lax.optimization_barrier(jnp.sum(exp_scores, axis=2))
        rounded = lax.optimization_barrier(exp_scores.astype(jnp.bfloat16)).astype(jnp.float32)
        attended = jnp.einsum('hqk,khd->qhd', rounded, value_block) / row_total.T[:, :, None]
        return attended.reshape(TOK_DEV, channels).astype(jnp.bfloat16)
    blocks = lax.map(one_block, jnp.arange(SEQ // TOK_DEV, dtype=jnp.int32))
    attn_out = blocks.reshape(SEQ, channels)
    gated = in_gate.astype(jnp.float32) * attn_out.astype(jnp.float32)
    length = 2 * SEQ
    spectrum = jnp.fft.rfft(gated, n=length, axis=0) * jnp.fft.rfft(filter_taps.T, n=length, axis=0)
    mixed = jnp.fft.irfft(spectrum, n=length, axis=0)[:SEQ]
    hyena_out = (out_gate.astype(jnp.float32) * mixed).astype(jnp.bfloat16)
    return (attn_out, hyena_out)
```

```python
import math

import jax
import jax.numpy as jnp
from jax import lax
from jax.sharding import PartitionSpec as P

HEAD_DIM = 128
KV_REACH = 3


masked_score = -1e30


def passed_along(x, axis, by):
    length = lax.axis_size(axis)
    pairs = [(i, i + by) for i in range(length) if 0 <= i + by < length]
    return lax.ppermute(x, axis, pairs)


def doc_of(positions, doc_lengths):
    order = jnp.arange(doc_lengths.shape[0], dtype=jnp.int32)
    before = order[:, None] < order[None, :]
    starts = jnp.sum(jnp.where(before, doc_lengths[:, None], 0), axis=0)
    inside = (starts[None, :] <= positions[:, None]).astype(jnp.int32)
    return jnp.sum(inside, axis=1) - 1


def attend_block(carried, pair, query_heads, allowed):
    running_max, running_sum, weighted = carried
    row_count = query_heads.shape[0]
    key_heads = pair[0].reshape(row_count, -1, HEAD_DIM)
    value_heads = pair[1].reshape(row_count, -1, HEAD_DIM)
    scores = jnp.einsum(
        "qhd,khd->hqk", query_heads, key_heads, preferred_element_type=jnp.float32
    ) / math.sqrt(HEAD_DIM)
    scores = jnp.where(allowed[None], scores, masked_score)
    new_max = jnp.maximum(running_max, jnp.max(scores, axis=2))
    rescale = jnp.exp(running_max - new_max)
    exp_scores = jnp.exp(scores - new_max[:, :, None])
    running_sum = running_sum * rescale + jnp.sum(exp_scores, axis=2)
    weighted = weighted * rescale[:, :, None] + jnp.einsum(
        "hqk,khd->hqd",
        exp_scores.astype(jnp.bfloat16),
        value_heads,
        preferred_element_type=jnp.float32,
    )
    return (new_max, running_sum, weighted)


def split_parts(source):
    high_part = lax.optimization_barrier(source.astype(jnp.bfloat16))
    low_part = (source - high_part.astype(jnp.float32)).astype(jnp.bfloat16)
    return (high_part, low_part)


def split_mul(form, left_parts, right_parts):
    first = jnp.einsum(form, left_parts[0], right_parts[0], preferred_element_type=jnp.float32)
    second = jnp.einsum(form, left_parts[0], right_parts[1], preferred_element_type=jnp.float32)
    third = jnp.einsum(form, left_parts[1], right_parts[0], preferred_element_type=jnp.float32)
    return first + (second + third)


def dft_tables(length):
    inner_len = math.gcd(length, 256)
    outer_len = 2 * length // inner_len
    freq_rows = jnp.arange(outer_len, dtype=jnp.int32)
    time_rows = jnp.arange(outer_len // 2, dtype=jnp.int32)
    inner_index = jnp.arange(inner_len, dtype=jnp.int32)
    angle_outer = (
        2.0
        * math.pi
        / outer_len
        * (freq_rows[:, None] * time_rows[None, :] % outer_len).astype(jnp.float32)
    )
    angle_twist = (
        2.0
        * math.pi
        / (2 * length)
        * (freq_rows[:, None] * inner_index[None, :] % (2 * length)).astype(jnp.float32)
    )
    angle_inner = (
        2.0
        * math.pi
        / inner_len
        * (inner_index[:, None] * inner_index[None, :] % inner_len).astype(jnp.float32)
    )
    return (
        split_parts(jnp.cos(angle_outer)),
        split_parts(-jnp.sin(angle_outer)),
        jnp.cos(angle_twist),
        -jnp.sin(angle_twist),
        split_parts(jnp.cos(angle_inner)),
        split_parts(-jnp.sin(angle_inner)),
    )


def right_mul(left_parts, table_parts):
    return split_mul("cin,nm->cim", left_parts, table_parts)


def forward_dft(samples, tables):
    outer_cos, outer_sin, twist_cos, twist_sin, inner_cos, inner_sin = tables
    item_count = samples.shape[0]
    shaped = split_parts(samples.reshape(item_count, outer_cos[0].shape[1], inner_cos[0].shape[0]))
    section_real = split_mul("ij,cjn->cin", outer_cos, shaped)
    section_imag = split_mul("ij,cjn->cin", outer_sin, shaped)
    turned_real = split_parts(section_real * twist_cos - section_imag * twist_sin)
    turned_imag = split_parts(section_real * twist_sin + section_imag * twist_cos)
    spec_real = right_mul(turned_real, inner_cos) - right_mul(turned_imag, inner_sin)
    spec_imag = right_mul(turned_real, inner_sin) + right_mul(turned_imag, inner_cos)
    return (spec_real, spec_imag)


def inverse_dft(prod_real, prod_imag, tables):
    outer_cos, outer_sin, twist_cos, twist_sin, inner_cos, inner_sin = tables
    item_count = prod_real.shape[0]
    half_len = outer_cos[0].shape[1]
    inner_len = inner_cos[0].shape[0]
    real_parts = split_parts(prod_real)
    imag_parts = split_parts(prod_imag)
    back_real = right_mul(real_parts, inner_cos) + right_mul(imag_parts, inner_sin)
    back_imag = right_mul(imag_parts, inner_cos) - right_mul(real_parts, inner_sin)
    unturn_real = split_parts(back_real * twist_cos + back_imag * twist_sin)
    unturn_imag = split_parts(back_imag * twist_cos - back_real * twist_sin)
    rows_out = split_mul("ij,cin->cjn", outer_cos, unturn_real) + split_mul(
        "ij,cin->cjn", outer_sin, unturn_imag
    )
    return (rows_out * (1.0 / (2 * half_len * inner_len))).reshape(item_count, half_len * inner_len)


def filter_apply(signal, filter_spec, tables):
    sig_real, sig_imag = forward_dft(signal, tables)
    tap_real, tap_imag = filter_spec
    prod_real = sig_real * tap_real - sig_imag * tap_imag
    prod_imag = sig_real * tap_imag + sig_imag * tap_real
    return inverse_dft(prod_real, prod_imag, tables)


def body(queries, key_rows, values, doc_lengths, in_gate, out_gate, filter_taps):
    row_count, channels = queries.shape
    head_count = channels // HEAD_DIM
    group_count = lax.axis_size("ctx")
    per_group = channels // group_count
    seq_len = row_count * group_count
    tables = dft_tables(seq_len)
    taps_grouped = filter_taps.reshape(group_count, per_group, row_count)
    query_pos = lax.axis_index("ctx") * row_count + jnp.arange(row_count, dtype=jnp.int32)
    query_doc = doc_of(query_pos, doc_lengths)
    query_heads = queries.reshape(row_count, head_count, HEAD_DIM)
    carried = (
        jnp.full((head_count, row_count), masked_score, jnp.float32),
        jnp.zeros((head_count, row_count), jnp.float32),
        jnp.zeros((head_count, row_count, HEAD_DIM), jnp.float32),
    )

    def visit(state_now, pair, distance):
        key_pos = query_pos - distance * row_count
        key_doc = doc_of(key_pos, doc_lengths)
        allowed = (key_doc[None, :] == query_doc[:, None]) & (
            key_pos[None, :] <= query_pos[:, None]
        )
        return attend_block(state_now, pair, query_heads, allowed)

    own_pair = jnp.stack((key_rows, values))
    carried = visit(carried, own_pair, 0)
    moving = own_pair
    for distance in range(1, KV_REACH + 1):
        moving = passed_along(moving, "ctx", 1)
        carried = visit(carried, moving, distance)
    running_max, running_sum, weighted = carried
    attended = (
        (weighted / running_sum[:, :, None])
        .transpose(1, 0, 2)
        .reshape(row_count, channels)
        .astype(jnp.bfloat16)
    )
    gated = (in_gate.astype(jnp.float32) * attended.astype(jnp.float32)).T
    gated_grouped = gated.reshape(group_count, per_group, row_count)
    pair = (
        lax.all_to_all(
            gated_grouped.astype(jnp.bfloat16), "ctx", split_axis=0, concat_axis=2, tiled=True
        ).astype(gated_grouped.dtype),
        lax.all_to_all(
            taps_grouped.astype(jnp.bfloat16), "ctx", split_axis=0, concat_axis=2, tiled=True
        ).astype(taps_grouped.dtype),
    )
    item_count = pair[0].shape[1]
    signal = pair[0].reshape(item_count, -1)
    taps = pair[1].reshape(item_count, -1)
    result = filter_apply(signal, forward_dft(taps, tables), tables)
    mixed = result.reshape(1, item_count, -1)
    returned = lax.all_to_all(
        mixed.astype(jnp.bfloat16), "ctx", split_axis=2, concat_axis=0, tiled=True
    ).astype(mixed.dtype)
    hyena_out = (out_gate.astype(jnp.float32) * returned.reshape(channels, row_count).T).astype(
        jnp.bfloat16
    )
    return (attended, hyena_out)


def solution(mesh):
    return jax.shard_map(
        body,
        mesh=mesh,
        in_specs=(
            P(("dp", "ctx"), "tp"),
            P(("dp", "ctx"), "tp"),
            P(("dp", "ctx"), "tp"),
            P("dp"),
            P(("dp", "ctx"), "tp"),
            P(("dp", "ctx"), "tp"),
            P(("dp", "tp"), "ctx"),
        ),
        out_specs=(P(("dp", "ctx"), "tp"), P(("dp", "ctx"), "tp")),
        check_vma=False,
    )
```

```python
import functools
import math

import jax
import jax.numpy as jnp
import ml_dtypes
import numpy as np
from jax import lax
from jax.experimental import pallas as pl
from jax.experimental.pallas import tpu as pltpu
from jax.sharding import PartitionSpec as P

HEAD_DIM = 128
KV_REACH = 3
X_SIZE = 4
Q_BLOCK = 256
K_BLOCK = 256
LANES = 128
masked_score = -1e30


def document_starts(positions, doc_lengths):
    order = jnp.arange(doc_lengths.shape[0], dtype=jnp.int32)
    before = order[:, None] < order[None, :]
    starts = jnp.sum(jnp.where(before, doc_lengths[:, None], 0), axis=0)
    inside = starts[None, :] <= positions[:, None]
    return jnp.max(jnp.where(inside, starts[None, :], 0), axis=1)


def attention_kernel(
    lo_ref, start_ref, q_ref, gate_ref, kp_ref, ko_ref, vp_ref, vo_ref, out_ref, gated_ref, keys, values_t
):
    step = pl.program_id(0)
    reach = kp_ref.shape[0]
    front = keys.shape[0] - reach - ko_ref.shape[0]

    @pl.when(step == 0)
    def _():
        if front:
            keys[0:front] = jnp.zeros((front, HEAD_DIM), jnp.bfloat16)
            values_t[0] = jnp.zeros(values_t.shape[1:], jnp.bfloat16)
        keys[front : front + reach] = kp_ref[...]
        keys[front + reach :] = ko_ref[...]
        for ref, base in ((vp_ref, front), (vo_ref, front + reach)):
            for row in range(0, ref.shape[0], 256):
                block, at = divmod(base + row, K_BLOCK)
                part = ref[row : row + 256].astype(jnp.float32).T
                values_t[block, :, at : at + 256] = part.astype(jnp.bfloat16)

    queries = q_ref[...]
    first = front + reach + step * Q_BLOCK
    start = start_ref[0]
    query_index = first + lax.broadcasted_iota(jnp.int32, (1, Q_BLOCK), 1)
    key_offset = lax.broadcasted_iota(jnp.int32, (K_BLOCK, 1), 0)
    factor = math.log2(math.e) / math.sqrt(HEAD_DIM)

    def visit(block, carried):
        top, total, weighted = carried
        key_rows = keys[pl.ds(pl.multiple_of(block * K_BLOCK, K_BLOCK), K_BLOCK)]
        scores = lax.dot_general(
            key_rows, queries, (((1,), (1,)), ((), ())), preferred_element_type=jnp.float32
        )
        index = block * K_BLOCK + key_offset
        kept = (index >= start) & (index <= query_index)
        scores = jnp.where(kept, scores * factor, masked_score)
        new_top = jnp.maximum(top, jnp.max(scores, axis=0, keepdims=True))
        rescale = jnp.exp2(top - new_top)
        weight = jnp.exp2(scores - new_top)
        total = total * rescale + jnp.sum(weight, axis=0, keepdims=True)
        weighted = weighted * rescale + jnp.dot(
            values_t[block], weight.astype(jnp.bfloat16), preferred_element_type=jnp.float32
        )
        return new_top, total, weighted

    last = (first + Q_BLOCK - 1) // K_BLOCK
    top, total, weighted = lax.fori_loop(
        lo_ref[step],
        last + 1,
        visit,
        (
            jnp.full((1, Q_BLOCK), masked_score, jnp.float32),
            jnp.zeros((1, Q_BLOCK), jnp.float32),
            jnp.zeros((HEAD_DIM, Q_BLOCK), jnp.float32),
        ),
    )
    attended = (weighted * (1.0 / total)).astype(jnp.bfloat16).astype(jnp.float32)
    out_ref[...] = attended.T.astype(jnp.bfloat16)
    gated_ref[...] = (attended * gate_ref[...].astype(jnp.float32).T).astype(jnp.bfloat16)


def attention(queries, gate, keys_before, keys_own, values_before, values_own, start):
    rows = queries.shape[0]
    reach = keys_before.shape[0]
    front = -reach % K_BLOCK
    steps = rows // Q_BLOCK
    start = start + front
    lo = start[::Q_BLOCK] // K_BLOCK
    whole = lambda i, lo: (0, 0)
    by_rows = lambda i, lo: (i, 0)
    key_total = front + reach + rows
    return pl.pallas_call(
        attention_kernel,
        name="attention",
        grid_spec=pltpu.PrefetchScalarGridSpec(
            num_scalar_prefetch=1,
            grid=(steps,),
            in_specs=[
                pl.BlockSpec((1, 1, Q_BLOCK), lambda i, lo: (i, 0, 0)),
                pl.BlockSpec((Q_BLOCK, HEAD_DIM), by_rows),
                pl.BlockSpec((Q_BLOCK, HEAD_DIM), by_rows),
                pl.BlockSpec((reach, HEAD_DIM), whole),
                pl.BlockSpec((rows, HEAD_DIM), whole),
                pl.BlockSpec((reach, HEAD_DIM), whole),
                pl.BlockSpec((rows, HEAD_DIM), whole),
            ],
            out_specs=[
                pl.BlockSpec((Q_BLOCK, HEAD_DIM), by_rows),
                pl.BlockSpec((HEAD_DIM, Q_BLOCK), lambda i, lo: (0, i)),
            ],
            scratch_shapes=[
                pltpu.VMEM((key_total, HEAD_DIM), jnp.bfloat16),
                pltpu.VMEM((key_total // K_BLOCK, HEAD_DIM, K_BLOCK), jnp.bfloat16),
            ],
        ),
        out_shape=[
            jax.ShapeDtypeStruct((rows, HEAD_DIM), jnp.bfloat16),
            jax.ShapeDtypeStruct((HEAD_DIM, rows), jnp.bfloat16),
        ],
        compiler_params=pltpu.CompilerParams(vmem_limit_bytes=40 * 2**20),
        cost_estimate=pl.CostEstimate(
            flops=4 * rows * 1536 * HEAD_DIM, bytes_accessed=10 * rows * HEAD_DIM, transcendentals=rows * 1536
        ),
    )(lo, start.reshape(steps, 1, Q_BLOCK), queries, gate, keys_before, keys_own, values_before, values_own)


def high_low(table):
    high = table.astype(np.float32).astype(ml_dtypes.bfloat16)
    low = (table - high.astype(np.float64)).astype(np.float32).astype(ml_dtypes.bfloat16)
    return np.stack((high, low))


def transform_tables(length, senders, tap_senders):
    outer = length // LANES
    k1 = np.arange(outer)
    per_sender = outer // senders
    a_signal = (np.arange(senders)[None, :] * per_sender + np.arange(per_sender)[:, None]).reshape(-1)
    per_tap = outer // tap_senders
    a_tap = (np.arange(tap_senders)[None, :] * per_tap + np.arange(per_tap)[:, None]).reshape(-1)
    b = np.arange(LANES)

    def angles(a):
        return 2.0 * np.pi * ((4 * k1[:, None] + 1) * a[None, :] % (4 * outer)) / (4 * outer)

    def forward(a):
        angle = angles(a)
        return high_low(np.concatenate((np.cos(angle), -np.sin(angle)), axis=0))

    twist = 2.0 * np.pi * ((4 * k1[:, None] + 1) * b[None, :] % (4 * length)) / (4 * length)
    inner = 2.0 * np.pi * (b[:, None] * b[None, :] % LANES) / LANES
    cos, sin = np.cos(inner), np.sin(inner)
    back = angles(a_tap).T
    return dict(
        signal=forward(a_signal),
        taps=forward(a_tap),
        twist=np.stack((np.cos(twist), -np.sin(twist))).astype(np.float32),
        inner=high_low(np.block([[cos, -sin], [sin, cos]])),
        inner_back=high_low(np.block([[cos, sin], [-sin, cos]])),
        back=high_low(np.concatenate((np.cos(back), -np.sin(back)), axis=1) / length),
    )


def table_dot(table_ref, right):
    return jnp.dot(table_ref[0], right, preferred_element_type=jnp.float32) + jnp.dot(
        table_ref[1], right, preferred_element_type=jnp.float32
    )


def dot_table(left, table_ref):
    return jnp.dot(left, table_ref[0], preferred_element_type=jnp.float32) + jnp.dot(
        left, table_ref[1], preferred_element_type=jnp.float32
    )


def spread(source_ref, spread_ref):
    rows = spread_ref.shape[1]
    for j in range(spread_ref.shape[0]):
        part = source_ref[:, :, j * LANES : (j + 1) * LANES]
        spread_ref[j] = part.reshape(rows, LANES).astype(jnp.float32)


def channel_rows(spread_ref, channel, channels):
    senders = spread_ref.shape[1] // channels
    parts = [spread_ref[j, pl.ds(channel, senders, stride=channels), :] for j in range(spread_ref.shape[0])]
    return jnp.concatenate(parts, axis=0).astype(jnp.bfloat16)


def spectrum(rows, outer_ref, twist_ref, inner_ref):
    outer = rows.shape[0]
    section = table_dot(outer_ref, rows)
    real, imag = section[:outer], section[outer:]
    turned_real = real * twist_ref[0] - imag * twist_ref[1]
    turned_imag = real * twist_ref[1] + imag * twist_ref[0]
    turned = jnp.concatenate((turned_real.astype(jnp.bfloat16), turned_imag.astype(jnp.bfloat16)), axis=1)
    return dot_table(turned, inner_ref)


def taps_kernel(taps_ref, outer_ref, twist_ref, inner_ref, out_ref, spread_ref):
    channels = taps_ref.shape[1]
    spread(taps_ref, spread_ref)
    for c in range(channels):
        out_ref[c] = spectrum(channel_rows(spread_ref, c, channels), outer_ref, twist_ref, inner_ref)


def conv_kernel(
    signal_ref, taps_ref, outer_ref, twist_ref, inner_ref, inner_back_ref, back_ref, out_ref, spread_ref, result_ref
):
    channels = signal_ref.shape[1]
    receivers = out_ref.shape[0]
    spread(signal_ref, spread_ref)
    for c in range(channels):
        signal = spectrum(channel_rows(spread_ref, c, channels), outer_ref, twist_ref, inner_ref)
        taps = taps_ref[c]
        sig_real, sig_imag = signal[:, :LANES], signal[:, LANES:]
        tap_real, tap_imag = taps[:, :LANES], taps[:, LANES:]
        prod_real = sig_real * tap_real - sig_imag * tap_imag
        prod_imag = sig_real * tap_imag + sig_imag * tap_real
        prod = jnp.concatenate((prod_real.astype(jnp.bfloat16), prod_imag.astype(jnp.bfloat16)), axis=1)
        turned = dot_table(prod, inner_back_ref)
        real, imag = turned[:, :LANES], turned[:, LANES:]
        back_real = real * twist_ref[0] + imag * twist_ref[1]
        back_imag = imag * twist_ref[0] - real * twist_ref[1]
        both = jnp.concatenate((back_real.astype(jnp.bfloat16), back_imag.astype(jnp.bfloat16)), axis=0)
        rows = table_dot(back_ref, both)
        for j in range(result_ref.shape[0]):
            result_ref[j, pl.ds(c, receivers, stride=channels), :] = rows[j * receivers : (j + 1) * receivers]
    for j in range(result_ref.shape[0]):
        part = result_ref[j].reshape(receivers, channels, LANES)
        out_ref[:, :, j * LANES : (j + 1) * LANES] = part.astype(jnp.bfloat16)


def finish_kernel(mixed_ref, gate_ref, attended_ref, attn_ref, hyena_ref):
    mixed = mixed_ref[...].reshape(HEAD_DIM, mixed_ref.shape[3]).astype(jnp.float32).T
    hyena_ref[...] = (gate_ref[...].astype(jnp.float32) * mixed).astype(jnp.bfloat16)
    attn_ref[...] = attended_ref[0]


def finish(returned, out_gate, attended):
    rows, channels = out_gate.shape
    z_size = returned.shape[0] // X_SIZE
    returned = returned.reshape(z_size, X_SIZE, returned.shape[1], rows)
    by_columns = pl.BlockSpec((rows, HEAD_DIM), lambda i: (0, i))
    return pl.pallas_call(
        finish_kernel,
        name="finish",
        grid=(channels // HEAD_DIM,),
        in_specs=[
            pl.BlockSpec((z_size, 1, returned.shape[2], rows), lambda i: (0, i, 0, 0)),
            by_columns,
            pl.BlockSpec((1, rows, HEAD_DIM), lambda i: (i, 0, 0)),
        ],
        out_specs=[by_columns, by_columns],
        out_shape=[jax.ShapeDtypeStruct((rows, channels), jnp.bfloat16)] * 2,
        compiler_params=pltpu.CompilerParams(vmem_limit_bytes=40 * 2**20),
    )(returned, out_gate, attended)


def body(queries, key_rows, values, doc_lengths, in_gate, out_gate, filter_taps):
    row_count, channels = queries.shape
    ctx = lax.axis_size("ctx")
    z_size = ctx // X_SIZE
    group_rows = X_SIZE * row_count
    reach = KV_REACH * row_count
    per_device = channels // ctx
    x_groups = [[z * X_SIZE + x for x in range(X_SIZE)] for z in range(z_size)]
    z_groups = [[z * X_SIZE + x for z in range(z_size)] for x in range(X_SIZE)]
    upward = [(i, i + X_SIZE) for i in range(ctx - X_SIZE)]
    tables = transform_tables(row_count * ctx, z_size, ctx)

    def to_heads(x):
        heads = x.reshape(row_count, X_SIZE, HEAD_DIM).transpose(1, 0, 2)
        moved = lax.all_to_all(heads, "ctx", split_axis=0, concat_axis=0, tiled=True, axis_index_groups=x_groups)
        return moved.reshape(group_rows, HEAD_DIM)

    def from_before(x):
        return lax.ppermute(x[group_rows - reach :], "ctx", upward)

    keys_own = to_heads(key_rows)
    keys_before = from_before(keys_own)
    values_own = to_heads(values)
    values_before = from_before(values_own)
    query_heads = to_heads(queries)
    gate_heads = to_heads(in_gate)

    taps = filter_taps.astype(jnp.bfloat16).reshape(X_SIZE, z_size, per_device, row_count)
    taps = taps.transpose(1, 0, 2, 3).reshape(ctx, per_device, row_count)
    taps = lax.all_to_all(taps, "ctx", split_axis=0, concat_axis=0, tiled=True)

    group_first = (lax.axis_index("ctx") // X_SIZE) * group_rows
    positions = group_first + jnp.arange(group_rows, dtype=jnp.int32)
    start = document_starts(positions, doc_lengths) - (group_first - reach)

    outer = row_count * ctx // LANES
    limit = pltpu.CompilerParams(vmem_limit_bytes=48 * 2**20)
    transform_flops = 2 * per_device * outer * LANES * (2 * outer + 4 * LANES) * 2
    taps_spectrum = pl.pallas_call(
        taps_kernel,
        name="taps_spectrum",
        out_shape=jax.ShapeDtypeStruct((per_device, outer, 2 * LANES), jnp.float32),
        scratch_shapes=[pltpu.VMEM((row_count // LANES, ctx * per_device, LANES), jnp.float32)],
        compiler_params=limit,
        cost_estimate=pl.CostEstimate(flops=transform_flops, bytes_accessed=4 * 2**20, transcendentals=0),
    )(taps, tables["taps"], tables["twist"], tables["inner"])

    attended, gated = attention(
        query_heads, gate_heads, keys_before, keys_own, values_before, values_own, start
    )
    attended = lax.all_to_all(
        attended.reshape(X_SIZE, row_count, HEAD_DIM),
        "ctx",
        split_axis=0,
        concat_axis=0,
        tiled=True,
        axis_index_groups=x_groups,
    )
    signal = lax.all_to_all(
        gated.reshape(z_size, per_device, group_rows),
        "ctx",
        split_axis=0,
        concat_axis=0,
        tiled=True,
        axis_index_groups=z_groups,
    )
    mixed = pl.pallas_call(
        conv_kernel,
        name="convolution",
        out_shape=jax.ShapeDtypeStruct((ctx, per_device, row_count), jnp.bfloat16),
        scratch_shapes=[
            pltpu.VMEM((group_rows // LANES, z_size * per_device, LANES), jnp.float32),
            pltpu.VMEM((row_count // LANES, ctx * per_device, LANES), jnp.float32),
        ],
        compiler_params=limit,
        cost_estimate=pl.CostEstimate(flops=2 * transform_flops, bytes_accessed=5 * 2**20, transcendentals=0),
    )(
        signal,
        taps_spectrum,
        tables["signal"],
        tables["twist"],
        tables["inner"],
        tables["inner_back"],
        tables["back"],
    )
    returned = lax.all_to_all(mixed, "ctx", split_axis=0, concat_axis=0, tiled=True)
    return finish(returned, out_gate, attended)


def solution(mesh):
    return jax.shard_map(
        body,
        mesh=mesh,
        in_specs=(
            P(("dp", "ctx"), "tp"),
            P(("dp", "ctx"), "tp"),
            P(("dp", "ctx"), "tp"),
            P("dp"),
            P(("dp", "ctx"), "tp"),
            P(("dp", "ctx"), "tp"),
            P(("dp", "tp"), "ctx"),
        ),
        out_specs=(P(("dp", "ctx"), "tp"), P(("dp", "ctx"), "tp")),
        check_vma=False,
    )
```

```python
import functools
import math

import jax
import jax.numpy as jnp
import ml_dtypes
import numpy as np
from jax import lax
from jax.experimental import pallas as pl
from jax.experimental.pallas import tpu as pltpu
from jax.sharding import PartitionSpec as P

HEAD_DIM = 128
KV_REACH = 3
X_SIZE = 4
Q_BLOCK = 768
K_BLOCK = 384
LANES = 128
masked_score = -1e30


def document_starts(positions, doc_lengths):
    order = jnp.arange(doc_lengths.shape[0], dtype=jnp.int32)
    before = order[:, None] < order[None, :]
    starts = jnp.sum(jnp.where(before, doc_lengths[:, None], 0), axis=0)
    inside = starts[None, :] <= positions[:, None]
    return jnp.max(jnp.where(inside, starts[None, :], 0), axis=1)


def attention_kernel(
    lo_ref, start_ref, q_ref, gate_ref, kp_ref, ko_ref, vp_ref, vo_ref, out_ref, gated_ref, keys, values_t
):
    step = pl.program_id(0)
    reach = kp_ref.shape[0]
    front = keys.shape[0] - reach - ko_ref.shape[0]

    @pl.when(step == 0)
    def _():
        if front:
            keys[0:front] = jnp.zeros((front, HEAD_DIM), jnp.bfloat16)
            values_t[0] = jnp.zeros(values_t.shape[1:], jnp.bfloat16)
        keys[front : front + reach] = kp_ref[...]
        keys[front + reach :] = ko_ref[...]
        for ref, base in ((vp_ref, front), (vo_ref, front + reach)):
            for row in range(0, ref.shape[0], LANES):
                block, at = divmod(base + row, K_BLOCK)
                part = ref[row : row + LANES].astype(jnp.float32).T
                values_t[block, :, at : at + LANES] = part.astype(jnp.bfloat16)

    queries = q_ref[0, 0]
    first = front + reach + step * Q_BLOCK
    start = start_ref[0]
    query_index = first + lax.broadcasted_iota(jnp.int32, (1, Q_BLOCK), 1)
    key_offset = lax.broadcasted_iota(jnp.int32, (K_BLOCK, 1), 0)
    factor = math.log2(math.e) / math.sqrt(HEAD_DIM)

    def visit(block, carried):
        top, total, weighted = carried
        key_rows = keys[pl.ds(pl.multiple_of(block * K_BLOCK, K_BLOCK), K_BLOCK)]
        scores = lax.dot_general(
            key_rows, queries, (((1,), (1,)), ((), ())), preferred_element_type=jnp.float32
        )
        index = block * K_BLOCK + key_offset
        kept = (index >= start) & (index <= query_index)
        scores = jnp.where(kept, scores * factor, masked_score)
        new_top = jnp.maximum(top, jnp.max(scores, axis=0, keepdims=True))
        rescale = jnp.exp2(top - new_top)
        weight = jnp.exp2(scores - new_top)
        total = total * rescale + jnp.sum(weight, axis=0, keepdims=True)
        weighted = weighted * rescale + jnp.dot(
            values_t[block], weight.astype(jnp.bfloat16), preferred_element_type=jnp.float32
        )
        return new_top, total, weighted

    last = (first + Q_BLOCK - 1) // K_BLOCK
    top, total, weighted = lax.fori_loop(
        lo_ref[step],
        last + 1,
        visit,
        (
            jnp.full((1, Q_BLOCK), masked_score, jnp.float32),
            jnp.zeros((1, Q_BLOCK), jnp.float32),
            jnp.zeros((HEAD_DIM, Q_BLOCK), jnp.float32),
        ),
    )
    attended = (weighted * (1.0 / total)).astype(jnp.bfloat16).astype(jnp.float32)
    out_ref[...] = attended.T.astype(jnp.bfloat16)
    gated_ref[...] = (attended * gate_ref[0, 0].astype(jnp.float32).T).astype(jnp.bfloat16)


def attention(queries_gate, keys_before, keys_own, values_before, values_own, start):
    rows = keys_own.shape[0]
    per_block = queries_gate.shape[2] // Q_BLOCK
    reach = keys_before.shape[0]
    front = -reach % K_BLOCK
    steps = rows // Q_BLOCK
    start = start + front
    lo = start[::Q_BLOCK] // K_BLOCK
    whole = lambda i, lo: (0, 0)
    by_rows = lambda i, lo: (i, 0)
    key_total = front + reach + rows
    return pl.pallas_call(
        attention_kernel,
        name="attention",
        grid_spec=pltpu.PrefetchScalarGridSpec(
            num_scalar_prefetch=1,
            grid=(steps,),
            in_specs=[
                pl.BlockSpec((1, 1, Q_BLOCK), lambda i, lo: (i, 0, 0)),
                pl.BlockSpec((1, 1, Q_BLOCK, HEAD_DIM), lambda i, lo: (i // per_block, 0, i % per_block, 0)),
                pl.BlockSpec((1, 1, Q_BLOCK, HEAD_DIM), lambda i, lo: (i // per_block, 1, i % per_block, 0)),
                pl.BlockSpec((reach, HEAD_DIM), whole),
                pl.BlockSpec((rows, HEAD_DIM), whole),
                pl.BlockSpec((reach, HEAD_DIM), whole),
                pl.BlockSpec((rows, HEAD_DIM), whole),
            ],
            out_specs=[
                pl.BlockSpec((Q_BLOCK, HEAD_DIM), by_rows),
                pl.BlockSpec((HEAD_DIM, Q_BLOCK), lambda i, lo: (0, i)),
            ],
            scratch_shapes=[
                pltpu.VMEM((key_total, HEAD_DIM), jnp.bfloat16),
                pltpu.VMEM((key_total // K_BLOCK, HEAD_DIM, K_BLOCK), jnp.bfloat16),
            ],
        ),
        out_shape=[
            jax.ShapeDtypeStruct((rows, HEAD_DIM), jnp.bfloat16),
            jax.ShapeDtypeStruct((HEAD_DIM, rows), jnp.bfloat16),
        ],
        compiler_params=pltpu.CompilerParams(vmem_limit_bytes=40 * 2**20),
        cost_estimate=pl.CostEstimate(
            flops=16 * 10**9, bytes_accessed=10 * rows * HEAD_DIM, transcendentals=rows * 1536
        ),
    )(lo, start.reshape(steps, 1, Q_BLOCK), queries_gate, queries_gate, keys_before, keys_own, values_before, values_own)


def high_low(table):
    high = table.astype(np.float32).astype(ml_dtypes.bfloat16)
    low = (table - high.astype(np.float64)).astype(np.float32).astype(ml_dtypes.bfloat16)
    return np.stack((high, low))


def transform_tables(length, senders, tap_senders):
    outer = length // LANES
    k1 = np.arange(outer)
    per_sender = outer // senders
    a_signal = (np.arange(senders)[None, :] * per_sender + np.arange(per_sender)[:, None]).reshape(-1)
    per_tap = outer // tap_senders
    a_tap = (np.arange(tap_senders)[None, :] * per_tap + np.arange(per_tap)[:, None]).reshape(-1)
    b = np.arange(LANES)

    def angles(a):
        return 2.0 * np.pi * ((4 * k1[:, None] + 1) * a[None, :] % (4 * outer)) / (4 * outer)

    def forward(a):
        angle = angles(a)
        return high_low(np.concatenate((np.cos(angle), -np.sin(angle)), axis=0))

    twist = 2.0 * np.pi * ((4 * k1[:, None] + 1) * b[None, :] % (4 * length)) / (4 * length)
    inner = 2.0 * np.pi * (b[:, None] * b[None, :] % LANES) / LANES
    cos, sin = np.cos(inner), np.sin(inner)
    back = angles(a_tap).T
    return dict(
        signal=forward(a_signal),
        taps=forward(a_tap),
        twist=np.stack((np.cos(twist), -np.sin(twist))).astype(np.float32),
        inner=high_low(np.block([[cos, -sin], [sin, cos]])),
        inner_back=high_low(np.block([[cos, sin], [-sin, cos]])),
        back=high_low(np.concatenate((np.cos(back), -np.sin(back)), axis=1) / length),
    )


def table_dot(table_ref, right):
    return jnp.dot(table_ref[0], right, preferred_element_type=jnp.float32) + jnp.dot(
        table_ref[1], right, preferred_element_type=jnp.float32
    )


def dot_table(left, table_ref):
    return jnp.dot(left, table_ref[0], preferred_element_type=jnp.float32) + jnp.dot(
        left, table_ref[1], preferred_element_type=jnp.float32
    )


def spread(source_ref, spread_ref):
    rows = spread_ref.shape[1]
    for j in range(spread_ref.shape[0]):
        part = source_ref[:, :, j * LANES : (j + 1) * LANES]
        spread_ref[j] = part.reshape(rows, LANES).astype(jnp.float32)


def channel_rows(spread_ref, channel, channels):
    senders = spread_ref.shape[1] // channels
    parts = [spread_ref[j, pl.ds(channel, senders, stride=channels), :] for j in range(spread_ref.shape[0])]
    return jnp.concatenate(parts, axis=0).astype(jnp.bfloat16)


def spectrum(rows, outer_ref, twist_ref, inner_ref):
    outer = rows.shape[0]
    section = table_dot(outer_ref, rows)
    real, imag = section[:outer], section[outer:]
    turned_real = real * twist_ref[0] - imag * twist_ref[1]
    turned_imag = real * twist_ref[1] + imag * twist_ref[0]
    turned = jnp.concatenate((turned_real.astype(jnp.bfloat16), turned_imag.astype(jnp.bfloat16)), axis=1)
    return dot_table(turned, inner_ref)


def taps_kernel(taps_ref, outer_ref, twist_ref, inner_ref, out_ref, spread_ref):
    channels = taps_ref.shape[1]
    spread(taps_ref, spread_ref)
    for c in range(channels):
        out_ref[c] = spectrum(channel_rows(spread_ref, c, channels), outer_ref, twist_ref, inner_ref)


def conv_kernel(
    signal_ref, taps_ref, outer_ref, twist_ref, inner_ref, inner_back_ref, back_ref, out_ref, spread_ref, result_ref
):
    channels = signal_ref.shape[1]
    receivers = out_ref.shape[0]
    spread(signal_ref, spread_ref)
    for c in range(channels):
        signal = spectrum(channel_rows(spread_ref, c, channels), outer_ref, twist_ref, inner_ref)
        taps = taps_ref[c]
        sig_real, sig_imag = signal[:, :LANES], signal[:, LANES:]
        tap_real, tap_imag = taps[:, :LANES], taps[:, LANES:]
        prod_real = sig_real * tap_real - sig_imag * tap_imag
        prod_imag = sig_real * tap_imag + sig_imag * tap_real
        prod = jnp.concatenate((prod_real.astype(jnp.bfloat16), prod_imag.astype(jnp.bfloat16)), axis=1)
        turned = dot_table(prod, inner_back_ref)
        real, imag = turned[:, :LANES], turned[:, LANES:]
        back_real = real * twist_ref[0] + imag * twist_ref[1]
        back_imag = imag * twist_ref[0] - real * twist_ref[1]
        both = jnp.concatenate((back_real.astype(jnp.bfloat16), back_imag.astype(jnp.bfloat16)), axis=0)
        rows = table_dot(back_ref, both)
        for j in range(result_ref.shape[0]):
            result_ref[j, pl.ds(c, receivers, stride=channels), :] = rows[j * receivers : (j + 1) * receivers]
    for j in range(result_ref.shape[0]):
        part = result_ref[j].reshape(receivers, channels, LANES)
        out_ref[:, :, j * LANES : (j + 1) * LANES] = part.astype(jnp.bfloat16)


def finish_kernel(mixed_ref, gate_ref, attended_ref, attn_ref, hyena_ref):
    mixed = mixed_ref[...].reshape(HEAD_DIM, mixed_ref.shape[3]).astype(jnp.float32).T
    hyena_ref[...] = (gate_ref[...].astype(jnp.float32) * mixed).astype(jnp.bfloat16)
    attn_ref[...] = attended_ref[0]


def finish(returned, out_gate, attended):
    rows, channels = out_gate.shape
    z_size = returned.shape[0] // X_SIZE
    returned = returned.reshape(z_size, X_SIZE, returned.shape[1], rows)
    by_columns = pl.BlockSpec((rows, HEAD_DIM), lambda i: (0, i))
    return pl.pallas_call(
        finish_kernel,
        name="finish",
        grid=(channels // HEAD_DIM,),
        in_specs=[
            pl.BlockSpec((z_size, 1, returned.shape[2], rows), lambda i: (0, i, 0, 0)),
            by_columns,
            pl.BlockSpec((1, rows, HEAD_DIM), lambda i: (i, 0, 0)),
        ],
        out_specs=[by_columns, by_columns],
        out_shape=[jax.ShapeDtypeStruct((rows, channels), jnp.bfloat16)] * 2,
        compiler_params=pltpu.CompilerParams(vmem_limit_bytes=40 * 2**20),
    )(returned, out_gate, attended)


def body(queries, key_rows, values, doc_lengths, in_gate, out_gate, filter_taps):
    row_count, channels = queries.shape
    ctx = lax.axis_size("ctx")
    z_size = ctx // X_SIZE
    group_rows = X_SIZE * row_count
    reach = KV_REACH * row_count
    per_device = channels // ctx
    x_groups = [[z * X_SIZE + x for x in range(X_SIZE)] for z in range(z_size)]
    z_groups = [[z * X_SIZE + x for z in range(z_size)] for x in range(X_SIZE)]
    upward = [(i, i + X_SIZE) for i in range(ctx - X_SIZE)]
    tables = transform_tables(row_count * ctx, z_size, ctx)

    def by_head(x):
        return x.reshape(row_count, X_SIZE, HEAD_DIM).transpose(1, 0, 2)

    def exchanged(x, groups=None):
        return lax.all_to_all(x, "ctx", split_axis=0, concat_axis=0, tiled=True, axis_index_groups=groups)

    def from_before(x):
        return lax.ppermute(x.reshape(group_rows, HEAD_DIM)[group_rows - reach :], "ctx", upward)

    taps = filter_taps.astype(jnp.bfloat16).reshape(X_SIZE, z_size, per_device, row_count)
    taps = taps.transpose(1, 0, 2, 3).reshape(ctx, per_device, row_count)

    keys_own = exchanged(by_head(key_rows), x_groups)
    keys_own, value_heads = lax.optimization_barrier((keys_own, by_head(values)))
    keys_before = from_before(keys_own)
    values_own = exchanged(value_heads, x_groups)
    queries_gate = jnp.stack((by_head(queries), by_head(in_gate)), axis=1)
    values_own, keys_before, queries_gate = lax.optimization_barrier((values_own, keys_before, queries_gate))
    values_before = from_before(values_own)
    queries_gate = exchanged(queries_gate, x_groups)
    queries_gate, values_before, taps = lax.optimization_barrier((queries_gate, values_before, taps))
    taps = exchanged(taps)
    keys_own = keys_own.reshape(group_rows, HEAD_DIM)
    values_own = values_own.reshape(group_rows, HEAD_DIM)

    group_first = (lax.axis_index("ctx") // X_SIZE) * group_rows
    positions = group_first + jnp.arange(group_rows, dtype=jnp.int32)
    start = document_starts(positions, doc_lengths) - (group_first - reach)

    outer = row_count * ctx // LANES
    limit = pltpu.CompilerParams(vmem_limit_bytes=48 * 2**20)
    attended, gated = attention(queries_gate, keys_before, keys_own, values_before, values_own, start)
    gated, taps = lax.optimization_barrier((gated, taps))
    taps_spectrum = pl.pallas_call(
        taps_kernel,
        name="taps_spectrum",
        out_shape=jax.ShapeDtypeStruct((per_device, outer, 2 * LANES), jnp.float32),
        scratch_shapes=[pltpu.VMEM((row_count // LANES, ctx * per_device, LANES), jnp.float32)],
        compiler_params=limit,
        cost_estimate=pl.CostEstimate(flops=6 * 10**9, bytes_accessed=4 * 2**20, transcendentals=0),
    )(taps, tables["taps"], tables["twist"], tables["inner"])
    signal = exchanged(gated.reshape(z_size, per_device, group_rows), z_groups)
    signal, attended = lax.optimization_barrier((signal, attended.reshape(X_SIZE, row_count, HEAD_DIM)))
    attended = exchanged(attended, x_groups)
    mixed = pl.pallas_call(
        conv_kernel,
        name="convolution",
        out_shape=jax.ShapeDtypeStruct((ctx, per_device, row_count), jnp.bfloat16),
        scratch_shapes=[
            pltpu.VMEM((group_rows // LANES, z_size * per_device, LANES), jnp.float32),
            pltpu.VMEM((row_count // LANES, ctx * per_device, LANES), jnp.float32),
        ],
        compiler_params=limit,
        cost_estimate=pl.CostEstimate(flops=9 * 10**9, bytes_accessed=5 * 2**20, transcendentals=0),
    )(
        signal,
        taps_spectrum,
        tables["signal"],
        tables["twist"],
        tables["inner"],
        tables["inner_back"],
        tables["back"],
    )
    mixed, attended = lax.optimization_barrier((mixed, attended))
    returned = exchanged(mixed)
    return finish(returned, out_gate, attended)


def solution(mesh):
    return jax.shard_map(
        body,
        mesh=mesh,
        in_specs=(
            P(("dp", "ctx"), "tp"),
            P(("dp", "ctx"), "tp"),
            P(("dp", "ctx"), "tp"),
            P("dp"),
            P(("dp", "ctx"), "tp"),
            P(("dp", "ctx"), "tp"),
            P(("dp", "tp"), "ctx"),
        ),
        out_specs=(P(("dp", "ctx"), "tp"), P(("dp", "ctx"), "tp")),
        check_vma=False,
    )
```

```python
import functools
import math

import jax
import jax.numpy as jnp
import ml_dtypes
import numpy as np
from jax import lax
from jax.experimental import pallas as pl
from jax.experimental.pallas import tpu as pltpu
from jax.sharding import PartitionSpec as P

HEAD_DIM = 128
X_SIZE = 4
Q_BLOCK = 768
K_BLOCK = 384
LANES = 128
VMEM_LIMIT = 62 * 2**20
PAIRS = 4
masked_score = -1e30


def document_starts(positions, doc_lengths):
    order = jnp.arange(doc_lengths.shape[0], dtype=jnp.int32)
    before = order[:, None] < order[None, :]
    starts = jnp.sum(jnp.where(before, doc_lengths[:, None], 0), axis=0)
    inside = starts[None, :] <= positions[:, None]
    return jnp.max(jnp.where(inside, starts[None, :], 0), axis=1)


def identity(size):
    row = lax.broadcasted_iota(jnp.int32, (size, size), 0)
    column = lax.broadcasted_iota(jnp.int32, (size, size), 1)
    return jnp.where(row == column, 1.0, 0.0).astype(jnp.bfloat16)


def transposed(x, eye):
    return lax.dot_general(eye, x, (((1,), (1,)), ((), ())), preferred_element_type=jnp.float32)


def pieces_kernel(x_ref, first_ref, second_ref, *rest):
    outs, sems = rest[:X_SIZE], rest[X_SIZE]
    copies = []
    for k, out in enumerate(outs):
        column = pl.multiple_of(lax.rem(x_ref[0] + k, X_SIZE) * HEAD_DIM, HEAD_DIM)
        for which, ref in enumerate((first_ref, second_ref)):
            copy = pltpu.make_async_copy(ref.at[:, pl.ds(column, HEAD_DIM)], out.at[which], sems.at[k, which])
            copy.start()
            copies.append(copy)
    for copy in copies:
        copy.wait()


def pieces_of(x_index, first, second):
    anywhere = pl.BlockSpec(memory_space=pl.ANY)
    return pl.pallas_call(
        pieces_kernel,
        name="pieces",
        in_specs=[pl.BlockSpec(memory_space=pltpu.SMEM), anywhere, anywhere],
        out_specs=[anywhere] * X_SIZE,
        out_shape=[jax.ShapeDtypeStruct((2, first.shape[0], HEAD_DIM), jnp.bfloat16)] * X_SIZE,
        scratch_shapes=[pltpu.SemaphoreType.DMA((X_SIZE, 2))],
    )(x_index, first, second)


def attention_kernel(lo_ref, mid_ref, x_ref, start_ref, *rest):
    own, before, asked = rest[:X_SIZE], rest[X_SIZE : 2 * X_SIZE], rest[2 * X_SIZE : 3 * X_SIZE]
    out_ref, gated_ref, keys, values, values_t, queries_all, gate_all, sems = rest[3 * X_SIZE :]
    step = pl.program_id(0)
    group = queries_all.shape[0]
    piece = group // X_SIZE
    eye = identity(HEAD_DIM)

    @pl.when(step == 0)
    def _():
        copies = []
        for k in range(X_SIZE):
            at = pl.multiple_of(lax.rem(x_ref[0] + X_SIZE - k, X_SIZE) * piece, piece)
            early, late = pl.ds(at, piece), pl.ds(at + group, piece)
            for n, (source, target) in enumerate(
                (
                    (own[k].at[0], keys.at[late]),
                    (own[k].at[1], values.at[late]),
                    (before[k].at[0], keys.at[early]),
                    (before[k].at[1], values.at[early]),
                    (asked[k].at[0], queries_all.at[early]),
                    (asked[k].at[1], gate_all.at[early]),
                )
            ):
                copy = pltpu.make_async_copy(source, target, sems.at[k, n])
                copy.start()
                copies.append(copy)
        for copy in copies:
            copy.wait()

        def turn(block, _):
            rows = values[pl.ds(pl.multiple_of(block * K_BLOCK, K_BLOCK), K_BLOCK)]
            values_t[block] = transposed(rows, eye).astype(jnp.bfloat16)
            return 0

        lax.fori_loop(lo_ref[0], values_t.shape[0], turn, 0)

    here = pl.ds(pl.multiple_of(step * Q_BLOCK, Q_BLOCK), Q_BLOCK)
    queries = transposed(queries_all[here], eye).astype(jnp.bfloat16)
    first = group + step * Q_BLOCK
    start = start_ref[0]
    query_index = first + lax.broadcasted_iota(jnp.int32, (1, Q_BLOCK), 1)
    key_offset = lax.broadcasted_iota(jnp.int32, (K_BLOCK, 1), 0)
    factor = math.log2(math.e) / math.sqrt(HEAD_DIM)

    def visit(masked, block, carried):
        top, total, weighted = carried
        key_rows = keys[pl.ds(pl.multiple_of(block * K_BLOCK, K_BLOCK), K_BLOCK)]
        scores = jnp.dot(key_rows, queries, preferred_element_type=jnp.float32) * factor
        if masked:
            index = block * K_BLOCK + key_offset
            scores = jnp.where((index >= start) & (index <= query_index), scores, masked_score)
        new_top = jnp.maximum(top, jnp.max(scores, axis=0, keepdims=True))
        rescale = jnp.exp2(top - new_top)
        weight = jnp.exp2(scores - new_top)
        total = total * rescale + jnp.sum(weight, axis=0, keepdims=True)
        weighted = weighted * rescale + jnp.dot(
            values_t[block], weight.astype(jnp.bfloat16), preferred_element_type=jnp.float32
        )
        return new_top, total, weighted

    diagonal = first // K_BLOCK
    last = (first + Q_BLOCK - 1) // K_BLOCK
    middle = jnp.minimum(mid_ref[step], diagonal)
    carried = (
        jnp.full((1, Q_BLOCK), masked_score, jnp.float32),
        jnp.zeros((1, Q_BLOCK), jnp.float32),
        jnp.zeros((HEAD_DIM, Q_BLOCK), jnp.float32),
    )
    edge, inside = functools.partial(visit, True), functools.partial(visit, False)
    carried = lax.fori_loop(lo_ref[step], middle, edge, carried)
    carried = lax.fori_loop(middle, diagonal, inside, carried)
    top, total, weighted = lax.fori_loop(diagonal, last + 1, edge, carried)
    rounded = (weighted * (1.0 / total)).astype(jnp.bfloat16)
    wide = identity(2 * LANES)
    for at in range(0, Q_BLOCK, 2 * LANES):
        part = transposed(rounded[:, at : at + 2 * LANES], wide)
        out_ref[at : at + 2 * LANES] = part.astype(jnp.bfloat16)
    gated_ref[...] = (rounded.astype(jnp.float32) * transposed(gate_all[here], eye)).astype(jnp.bfloat16)


def attention(x_index, own, before, asked, start):
    rows = X_SIZE * own[0].shape[1]
    steps = rows // Q_BLOCK
    lo = start[::Q_BLOCK] // K_BLOCK
    middle = start[Q_BLOCK - 1 :: Q_BLOCK] // K_BLOCK + 1
    anywhere = pl.BlockSpec(memory_space=pl.ANY)
    return pl.pallas_call(
        attention_kernel,
        name="attention",
        grid_spec=pltpu.PrefetchScalarGridSpec(
            num_scalar_prefetch=3,
            grid=(steps,),
            in_specs=[pl.BlockSpec((1, 1, Q_BLOCK), lambda i, *_: (i, 0, 0))] + [anywhere] * (3 * X_SIZE),
            out_specs=[
                pl.BlockSpec((Q_BLOCK, HEAD_DIM), lambda i, *_: (i, 0)),
                pl.BlockSpec((HEAD_DIM, Q_BLOCK), lambda i, *_: (0, i)),
            ],
            scratch_shapes=[
                pltpu.VMEM((2 * rows, HEAD_DIM), jnp.bfloat16),
                pltpu.VMEM((2 * rows, HEAD_DIM), jnp.bfloat16),
                pltpu.VMEM((2 * rows // K_BLOCK, HEAD_DIM, K_BLOCK), jnp.bfloat16),
                pltpu.VMEM((rows, HEAD_DIM), jnp.bfloat16),
                pltpu.VMEM((rows, HEAD_DIM), jnp.bfloat16),
                pltpu.SemaphoreType.DMA((X_SIZE, 6)),
            ],
        ),
        out_shape=[
            jax.ShapeDtypeStruct((rows, HEAD_DIM), jnp.bfloat16),
            jax.ShapeDtypeStruct((HEAD_DIM, rows), jnp.bfloat16),
        ],
        compiler_params=pltpu.CompilerParams(vmem_limit_bytes=VMEM_LIMIT),
        cost_estimate=pl.CostEstimate(
            flops=16 * 10**9, bytes_accessed=10 * rows * HEAD_DIM, transcendentals=rows * 1536
        ),
    )(lo, middle, x_index, start.reshape(steps, 1, Q_BLOCK), *own, *before, *asked)


def high_low(table):
    high = table.astype(np.float32).astype(ml_dtypes.bfloat16)
    low = (table - high.astype(np.float64)).astype(np.float32).astype(ml_dtypes.bfloat16)
    return high, low


def transform_tables(length, senders, tap_senders):
    outer = length // LANES
    k1 = np.arange(outer)
    per_sender = outer // senders
    a_signal = (np.arange(senders)[None, :] * per_sender + np.arange(per_sender)[:, None]).reshape(-1)
    per_tap = outer // tap_senders
    a_tap = (np.arange(tap_senders)[None, :] * per_tap + np.arange(per_tap)[:, None]).reshape(-1)
    b = np.arange(LANES)

    def angles(a):
        return 2.0 * np.pi * ((4 * k1[:, None] + 1) * a[None, :] % (4 * outer)) / (4 * outer)

    def left(table):
        return np.concatenate(high_low(table), axis=1)

    def right(table):
        return np.concatenate(high_low(table), axis=0)

    def forward(a):
        angle = angles(a)
        return left(np.concatenate((np.cos(angle), -np.sin(angle)), axis=0))

    twist = 2.0 * np.pi * ((4 * k1[:, None] + 1) * b[None, :] % (4 * length)) / (4 * length)
    inner = 2.0 * np.pi * (b[:, None] * b[None, :] % LANES) / LANES
    cos, sin = np.cos(inner), np.sin(inner)
    back = angles(a_tap).T
    return dict(
        signal=forward(a_signal),
        taps=forward(a_tap),
        twist=np.stack((np.cos(twist), -np.sin(twist))).astype(np.float32),
        inner=right(np.block([[cos, -sin], [sin, cos]])),
        inner_back=right(np.block([[cos, sin], [-sin, cos]])),
        back=left(np.concatenate((np.cos(back), -np.sin(back)), axis=1) / length),
    )


def table_dot(table_ref, right):
    return jnp.dot(table_ref[...], jnp.concatenate((right, right), axis=0), preferred_element_type=jnp.float32)


def dot_table(left, table_ref):
    return jnp.dot(jnp.concatenate((left, left), axis=1), table_ref[...], preferred_element_type=jnp.float32)


def spread(source_ref, spread_ref):
    rows = spread_ref.shape[1]
    for j in range(spread_ref.shape[0]):
        part = source_ref[:, :, j * LANES : (j + 1) * LANES]
        spread_ref[j] = part.reshape(rows, LANES).astype(jnp.float32)


def channel_rows(spread_ref, channel, channels):
    senders = spread_ref.shape[1] // channels
    pair = []
    for c in (channel, channel + 1):
        parts = [spread_ref[j, pl.ds(c, senders, stride=channels), :] for j in range(spread_ref.shape[0])]
        pair.append(jnp.concatenate(parts, axis=0).astype(jnp.bfloat16))
    return jnp.concatenate(pair, axis=1)


def spectrum(rows, outer_ref, twist_ref, inner_ref):
    outer = rows.shape[0]
    section = table_dot(outer_ref, rows)
    turned = []
    for lane in (0, LANES):
        real, imag = section[:outer, lane : lane + LANES], section[outer:, lane : lane + LANES]
        turned_real = real * twist_ref[0] - imag * twist_ref[1]
        turned_imag = real * twist_ref[1] + imag * twist_ref[0]
        turned.append(jnp.concatenate((turned_real.astype(jnp.bfloat16), turned_imag.astype(jnp.bfloat16)), axis=1))
    return dot_table(jnp.concatenate(turned, axis=0), inner_ref)


def taps_kernel(taps_ref, outer_ref, twist_ref, inner_ref, out_ref, spread_ref):
    step = pl.program_id(0)
    channels = taps_ref.shape[1]

    @pl.when(step == 0)
    def _():
        spread(taps_ref, spread_ref)

    for pair in range(out_ref.shape[0]):
        channel = step * 2 * out_ref.shape[0] + 2 * pair
        out_ref[pair] = spectrum(channel_rows(spread_ref, channel, channels), outer_ref, twist_ref, inner_ref)


def conv_kernel(
    signal_ref, taps_ref, outer_ref, twist_ref, inner_ref, inner_back_ref, back_ref, out_ref, spread_ref, result_ref
):
    step = pl.program_id(0)
    channels = signal_ref.shape[1]
    receivers = out_ref.shape[0]
    outer = twist_ref.shape[1]

    @pl.when(step == 0)
    def _():
        spread(signal_ref, spread_ref)

    for pair in range(taps_ref.shape[0]):
        channel = step * 2 * taps_ref.shape[0] + 2 * pair
        signal = spectrum(channel_rows(spread_ref, channel, channels), outer_ref, twist_ref, inner_ref)
        taps = taps_ref[pair]
        sig_real, sig_imag = signal[:, :LANES], signal[:, LANES:]
        tap_real, tap_imag = taps[:, :LANES], taps[:, LANES:]
        prod_real = sig_real * tap_real - sig_imag * tap_imag
        prod_imag = sig_real * tap_imag + sig_imag * tap_real
        prod = jnp.concatenate((prod_real.astype(jnp.bfloat16), prod_imag.astype(jnp.bfloat16)), axis=1)
        turned = dot_table(prod, inner_back_ref)
        both = []
        for row in (0, outer):
            real, imag = turned[row : row + outer, :LANES], turned[row : row + outer, LANES:]
            back_real = real * twist_ref[0] + imag * twist_ref[1]
            back_imag = imag * twist_ref[0] - real * twist_ref[1]
            both.append(jnp.concatenate((back_real.astype(jnp.bfloat16), back_imag.astype(jnp.bfloat16)), axis=0))
        rows = table_dot(back_ref, jnp.concatenate(both, axis=1))
        for n in range(2):
            for j in range(result_ref.shape[0]):
                part = rows[j * receivers : (j + 1) * receivers, n * LANES : (n + 1) * LANES]
                result_ref[j, pl.ds(channel + n, receivers, stride=channels), :] = part

    @pl.when(step == pl.num_programs(0) - 1)
    def _():
        for j in range(result_ref.shape[0]):
            part = result_ref[j].reshape(receivers, channels, LANES)
            out_ref[:, :, j * LANES : (j + 1) * LANES] = part.astype(jnp.bfloat16)


def whole(array):
    return pl.BlockSpec(array.shape, lambda i: (0,) * array.ndim)


def transform_taps(taps, tables):
    senders, channels, rows = taps.shape
    outer = tables["twist"].shape[1]
    operands = (taps, tables["taps"], tables["twist"], tables["inner"])
    return pl.pallas_call(
        taps_kernel,
        name="taps_spectrum",
        grid=(channels // (2 * PAIRS),),
        in_specs=[whole(x) for x in operands],
        out_specs=pl.BlockSpec((PAIRS, 2 * outer, 2 * LANES), lambda i: (i, 0, 0)),
        out_shape=jax.ShapeDtypeStruct((channels // 2, 2 * outer, 2 * LANES), jnp.float32),
        scratch_shapes=[pltpu.VMEM((rows // LANES, senders * channels, LANES), jnp.float32)],
        compiler_params=pltpu.CompilerParams(vmem_limit_bytes=VMEM_LIMIT),
        cost_estimate=pl.CostEstimate(flops=5 * 10**9, bytes_accessed=4 * 2**20, transcendentals=0),
    )(*operands)


def convolve(signal, spectra, tables, receivers):
    senders, channels, rows = signal.shape
    out_rows = senders * rows // receivers
    operands = [tables[n] for n in ("signal", "twist", "inner", "inner_back", "back")]
    return pl.pallas_call(
        conv_kernel,
        name="convolution",
        grid=(channels // (2 * PAIRS),),
        in_specs=[whole(signal), pl.BlockSpec((PAIRS,) + spectra.shape[1:], lambda i: (i, 0, 0))]
        + [whole(x) for x in operands],
        out_specs=pl.BlockSpec((receivers, channels, out_rows), lambda i: (0, 0, 0)),
        out_shape=jax.ShapeDtypeStruct((receivers, channels, out_rows), jnp.bfloat16),
        scratch_shapes=[
            pltpu.VMEM((rows // LANES, senders * channels, LANES), jnp.float32),
            pltpu.VMEM((out_rows // LANES, receivers * channels, LANES), jnp.float32),
        ],
        compiler_params=pltpu.CompilerParams(vmem_limit_bytes=VMEM_LIMIT),
        cost_estimate=pl.CostEstimate(flops=7 * 10**9, bytes_accessed=5 * 2**20, transcendentals=0),
    )(signal, spectra, *operands)


def finish_kernel(mixed_ref, gate_ref, attended_ref, attn_ref, hyena_ref):
    mixed = mixed_ref[...].reshape(HEAD_DIM, mixed_ref.shape[3]).astype(jnp.float32).T
    hyena_ref[...] = (gate_ref[...].astype(jnp.float32) * mixed).astype(jnp.bfloat16)
    attn_ref[...] = attended_ref[0]


def finish(returned, out_gate, attended):
    rows, channels = out_gate.shape
    z_size = returned.shape[0] // X_SIZE
    returned = returned.reshape(z_size, X_SIZE, returned.shape[1], rows)
    by_columns = pl.BlockSpec((rows, HEAD_DIM), lambda i: (0, i))
    return pl.pallas_call(
        finish_kernel,
        name="finish",
        grid=(channels // HEAD_DIM,),
        in_specs=[
            pl.BlockSpec((z_size, 1, returned.shape[2], rows), lambda i: (0, i, 0, 0)),
            by_columns,
            pl.BlockSpec((1, rows, HEAD_DIM), lambda i: (i, 0, 0)),
        ],
        out_specs=[by_columns, by_columns],
        out_shape=[jax.ShapeDtypeStruct((rows, channels), jnp.bfloat16)] * 2,
        compiler_params=pltpu.CompilerParams(vmem_limit_bytes=VMEM_LIMIT),
    )(returned, out_gate, attended)


def body(queries, key_rows, values, doc_lengths, in_gate, out_gate, filter_taps):
    row_count, channels = queries.shape
    ctx = lax.axis_size("ctx")
    z_size = ctx // X_SIZE
    group_rows = X_SIZE * row_count
    per_device = channels // ctx
    x_groups = [[z * X_SIZE + x for x in range(X_SIZE)] for z in range(z_size)]
    z_groups = [[z * X_SIZE + x for z in range(z_size)] for x in range(X_SIZE)]
    tables = transform_tables(row_count * ctx, z_size, ctx)
    me = lax.axis_index("ctx").astype(jnp.int32)
    x_index = lax.rem(me, X_SIZE).reshape(1)

    def exchanged(x, groups=None):
        return lax.all_to_all(x, "ctx", split_axis=0, concat_axis=0, tiled=True, axis_index_groups=groups)

    def along_x(piece, k):
        pairs = [(z * X_SIZE + x, z * X_SIZE + (x + k) % X_SIZE) for z in range(z_size) for x in range(X_SIZE)]
        return lax.ppermute(piece, "ctx", pairs)

    def along_z(piece, k):
        pairs = [(i, i + X_SIZE) for i in range(ctx - X_SIZE) if i % X_SIZE != k]
        return lax.ppermute(piece, "ctx", pairs)

    def arrived(pieces):
        return [pieces[0]] + [along_x(pieces[k], k) for k in range(1, X_SIZE)]

    taps = filter_taps.astype(jnp.bfloat16).reshape(X_SIZE, z_size, per_device, row_count)
    taps = taps.transpose(1, 0, 2, 3).reshape(ctx, per_device, row_count)
    own = arrived(pieces_of(x_index, key_rows, values))
    taps = exchanged(taps)
    before = [along_z(own[k], k) for k in range(X_SIZE)]
    taps, queries, in_gate = lax.optimization_barrier((taps, queries, in_gate))
    asked = arrived(pieces_of(x_index, queries, in_gate))

    group_first = (me // X_SIZE) * group_rows
    positions = group_first + jnp.arange(group_rows, dtype=jnp.int32)
    start = document_starts(positions, doc_lengths) - (group_first - group_rows)

    attended, gated = attention(x_index, own, before, asked, start)
    gated, taps = lax.optimization_barrier((gated, taps))
    signal = exchanged(gated.reshape(z_size, per_device, group_rows), z_groups)
    spectra = transform_taps(taps, tables)
    signal, attended = lax.optimization_barrier((signal, attended.reshape(X_SIZE, row_count, HEAD_DIM)))
    attended = exchanged(attended, x_groups)
    mixed = convolve(signal, spectra, tables, ctx)
    mixed, attended = lax.optimization_barrier((mixed, attended))
    returned = exchanged(mixed)
    return finish(returned, out_gate, attended)


def solution(mesh):
    return jax.shard_map(
        body,
        mesh=mesh,
        in_specs=(
            P(("dp", "ctx"), "tp"),
            P(("dp", "ctx"), "tp"),
            P(("dp", "ctx"), "tp"),
            P("dp"),
            P(("dp", "ctx"), "tp"),
            P(("dp", "ctx"), "tp"),
            P(("dp", "tp"), "ctx"),
        ),
        out_specs=(P(("dp", "ctx"), "tp"), P(("dp", "ctx"), "tp")),
        check_vma=False,
    )
```

```python
import functools
import math

import jax
import jax.numpy as jnp
import ml_dtypes
import numpy as np
from jax import lax
from jax.experimental import pallas as pl
from jax.experimental.pallas import tpu as pltpu
from jax.sharding import PartitionSpec as P

HEAD_DIM = 128
X_SIZE = 4
Q_BLOCK = 768
K_BLOCK = 384
Q_SUB = 768
LANES = 128
VMEM_LIMIT = 62 * 2**20
PAIRS = 4
masked_score = -1e30


def document_starts(positions, doc_lengths):
    order = jnp.arange(doc_lengths.shape[0], dtype=jnp.int32)
    before = order[:, None] < order[None, :]
    starts = jnp.sum(jnp.where(before, doc_lengths[:, None], 0), axis=0)
    inside = starts[None, :] <= positions[:, None]
    return jnp.max(jnp.where(inside, starts[None, :], 0), axis=1)


def pieces_kernel(x_ref, first_ref, second_ref, *rest):
    outs, (held, in_sems, out_sems) = rest[:X_SIZE], rest[X_SIZE:]
    arriving, leaving = [], []
    for k in range(X_SIZE):
        column = pl.multiple_of(lax.rem(x_ref[0] + k, X_SIZE) * HEAD_DIM, HEAD_DIM)
        for which, ref in enumerate((first_ref, second_ref)):
            copy = pltpu.make_async_copy(ref.at[:, pl.ds(column, HEAD_DIM)], held.at[k, which], in_sems.at[k, which])
            copy.start()
            arriving.append((k, which, copy))
    for k, which, copy in arriving:
        copy.wait()
        out = pltpu.make_async_copy(held.at[k, which], outs[k].at[which], out_sems.at[k, which])
        out.start()
        leaving.append(out)
    for out in leaving:
        out.wait()


def pieces_of(x_index, first, second):
    rows = first.shape[0]
    anywhere = pl.BlockSpec(memory_space=pl.ANY)
    return pl.pallas_call(
        pieces_kernel,
        name="pieces",
        in_specs=[pl.BlockSpec(memory_space=pltpu.SMEM), anywhere, anywhere],
        out_specs=[anywhere] * X_SIZE,
        out_shape=[jax.ShapeDtypeStruct((2, rows, HEAD_DIM), jnp.bfloat16)] * X_SIZE,
        scratch_shapes=[
            pltpu.VMEM((X_SIZE, 2, rows, HEAD_DIM), jnp.bfloat16),
            pltpu.SemaphoreType.DMA((X_SIZE, 2)),
            pltpu.SemaphoreType.DMA((X_SIZE, 2)),
        ],
    )(x_index, first, second)


def attention_kernel(lo_ref, mid_ref, x_ref, start_ref, *rest):
    own, before, asked = rest[:X_SIZE], rest[X_SIZE : 2 * X_SIZE], rest[2 * X_SIZE : 3 * X_SIZE]
    out_ref, gated_ref, keys, values, values_t, queries_all, gate_all, sems = rest[3 * X_SIZE :]
    step = pl.program_id(0)
    group = queries_all.shape[0]
    piece = group // X_SIZE
    group_blocks = group // K_BLOCK
    piece_blocks = piece // K_BLOCK

    def copies_of(k, chosen, sources):
        at = pl.multiple_of(lax.rem(x_ref[0] + X_SIZE - k, X_SIZE) * piece, piece)
        early, late = pl.ds(at, piece), pl.ds(at + group, piece)
        targets = (keys.at[early], values.at[early], keys.at[late], values.at[late], queries_all.at[early], gate_all.at[early])
        return [pltpu.make_async_copy(sources[n // 2].at[n % 2], targets[n], sems.at[k, n]) for n in chosen]

    def reached(k):
        position = lax.rem(x_ref[0] + X_SIZE - k, X_SIZE)
        return jnp.logical_and(position > 0, (position + 1) * piece_blocks > lo_ref[0])

    def turn(block, _):
        rows = values[pl.ds(pl.multiple_of(block * K_BLOCK, K_BLOCK), K_BLOCK)]
        values_t[block] = rows.T
        return 0

    @pl.when(step == 0)
    def _():
        for k in range(X_SIZE):
            sources = (before[k], own[k], asked[k])

            @pl.when(reached(k))
            def _():
                for copy in copies_of(k, (0, 1), sources):
                    copy.start()

            for copy in copies_of(k, (2, 3, 4, 5), sources):
                copy.start()
        for k in range(X_SIZE):

            @pl.when(reached(k))
            def _():
                for copy in copies_of(k, (0, 1), (before[k], own[k], asked[k])):
                    copy.wait()

        lax.fori_loop(lo_ref[0], group_blocks, turn, 0)

    now = lax.rem(x_ref[0] + X_SIZE - step, X_SIZE)
    for copy in copies_of(now, (2, 3, 4, 5), (before[0], own[0], asked[0])):
        copy.wait()
    first = group + step * Q_BLOCK
    diagonal = first // K_BLOCK
    last = (first + Q_BLOCK - 1) // K_BLOCK
    lax.fori_loop(diagonal, last + 1, turn, 0)

    here = pl.ds(pl.multiple_of(step * Q_BLOCK, Q_BLOCK), Q_BLOCK)
    queries = queries_all[here].T
    start = start_ref[0]
    query_index = first + lax.broadcasted_iota(jnp.int32, (1, Q_BLOCK), 1)
    key_offset = lax.broadcasted_iota(jnp.int32, (K_BLOCK, 1), 0)
    factor = math.log2(math.e) / math.sqrt(HEAD_DIM)
    subs = [slice(at, at + Q_SUB) for at in range(0, Q_BLOCK, Q_SUB)]

    def visit(kind, block, carried):
        key_rows = keys[pl.ds(pl.multiple_of(block * K_BLOCK, K_BLOCK), K_BLOCK)]
        block_values = values_t[block]
        index = block * K_BLOCK + key_offset
        result = []
        for sub, (top, total, weighted) in zip(subs, carried):
            scores = jnp.dot(key_rows, queries[:, sub], preferred_element_type=jnp.float32) * factor
            if kind == "before":
                scores = jnp.where(index >= start[:, sub], scores, masked_score)
            if kind == "diagonal":
                kept = (index >= start[:, sub]) & (index <= query_index[:, sub])
                scores = jnp.where(kept, scores, masked_score)
            new_top = jnp.maximum(top, jnp.max(scores, axis=0, keepdims=True))
            rescale = jnp.exp2(top - new_top)
            weight = jnp.exp2(scores - new_top)
            total = total * rescale + jnp.sum(weight, axis=0, keepdims=True)
            weighted = weighted * rescale + jnp.dot(
                block_values, weight.astype(jnp.bfloat16), preferred_element_type=jnp.float32
            )
            result.append((new_top, total, weighted))
        return tuple(result)

    middle = jnp.minimum(mid_ref[step], diagonal)
    carried = tuple(
        (
            jnp.full((1, Q_SUB), masked_score, jnp.float32),
            jnp.zeros((1, Q_SUB), jnp.float32),
            jnp.zeros((HEAD_DIM, Q_SUB), jnp.float32),
        )
        for _ in subs
    )
    carried = lax.fori_loop(lo_ref[step], middle, functools.partial(visit, "before"), carried)
    carried = lax.fori_loop(middle, diagonal, functools.partial(visit, "inside"), carried)
    carried = lax.fori_loop(diagonal, last + 1, functools.partial(visit, "diagonal"), carried)
    gate = gate_all[here].T
    for sub, (top, total, weighted) in zip(subs, carried):
        rounded = (weighted * (1.0 / total)).astype(jnp.bfloat16)
        out_ref[0, sub] = rounded.T
        gated_ref[:, sub] = (rounded.astype(jnp.float32) * gate[:, sub].astype(jnp.float32)).astype(jnp.bfloat16)


def attention(x_index, own, before, asked, start):
    rows = X_SIZE * own[0].shape[1]
    steps = rows // Q_BLOCK
    lo = start[::Q_BLOCK] // K_BLOCK
    middle = start[Q_BLOCK - 1 :: Q_BLOCK] // K_BLOCK + 1
    anywhere = pl.BlockSpec(memory_space=pl.ANY)
    return pl.pallas_call(
        attention_kernel,
        name="attention",
        grid_spec=pltpu.PrefetchScalarGridSpec(
            num_scalar_prefetch=3,
            grid=(steps,),
            in_specs=[pl.BlockSpec((1, 1, Q_BLOCK), lambda i, *_: (i, 0, 0))] + [anywhere] * (3 * X_SIZE),
            out_specs=[
                pl.BlockSpec((1, Q_BLOCK, HEAD_DIM), lambda i, lo, mid, x: (lax.rem(i - x[0] + X_SIZE, X_SIZE), 0, 0)),
                pl.BlockSpec((HEAD_DIM, Q_BLOCK), lambda i, *_: (0, i)),
            ],
            scratch_shapes=[
                pltpu.VMEM((2 * rows, HEAD_DIM), jnp.bfloat16),
                pltpu.VMEM((2 * rows, HEAD_DIM), jnp.bfloat16),
                pltpu.VMEM((2 * rows // K_BLOCK, HEAD_DIM, K_BLOCK), jnp.bfloat16),
                pltpu.VMEM((rows, HEAD_DIM), jnp.bfloat16),
                pltpu.VMEM((rows, HEAD_DIM), jnp.bfloat16),
                pltpu.SemaphoreType.DMA((X_SIZE, 6)),
            ],
        ),
        out_shape=[
            jax.ShapeDtypeStruct((X_SIZE, rows // X_SIZE, HEAD_DIM), jnp.bfloat16),
            jax.ShapeDtypeStruct((HEAD_DIM, rows), jnp.bfloat16),
        ],
        compiler_params=pltpu.CompilerParams(vmem_limit_bytes=VMEM_LIMIT),
        cost_estimate=pl.CostEstimate(
            flops=16 * 10**9, bytes_accessed=10 * rows * HEAD_DIM, transcendentals=rows * 1536
        ),
    )(lo, middle, x_index, start.reshape(steps, 1, Q_BLOCK), *own, *before, *asked)


def high_low(table):
    high = table.astype(np.float32).astype(ml_dtypes.bfloat16)
    low = (table - high.astype(np.float64)).astype(np.float32).astype(ml_dtypes.bfloat16)
    return high, low


def transform_tables(length, senders, tap_senders):
    outer = length // LANES
    k1 = np.arange(outer)
    per_sender = outer // senders
    a_signal = (np.arange(senders)[None, :] * per_sender + np.arange(per_sender)[:, None]).reshape(-1)
    per_tap = outer // tap_senders
    a_tap = (np.arange(tap_senders)[None, :] * per_tap + np.arange(per_tap)[:, None]).reshape(-1)
    b = np.arange(LANES)

    def angles(a):
        return 2.0 * np.pi * ((4 * k1[:, None] + 1) * a[None, :] % (4 * outer)) / (4 * outer)

    def left(table):
        return np.concatenate(high_low(table), axis=1)

    def right(table):
        return np.concatenate(high_low(table), axis=0)

    def forward(a):
        angle = angles(a)
        return left(np.concatenate((np.cos(angle), -np.sin(angle)), axis=0))

    twist = 2.0 * np.pi * ((4 * k1[:, None] + 1) * b[None, :] % (4 * length)) / (4 * length)
    inner = 2.0 * np.pi * (b[:, None] * b[None, :] % LANES) / LANES
    cos, sin = np.cos(inner), np.sin(inner)
    back = angles(a_tap).T
    return dict(
        signal=forward(a_signal),
        taps=forward(a_tap),
        twist=np.stack((np.cos(twist), -np.sin(twist))).astype(np.float32),
        inner=right(np.block([[cos, -sin], [sin, cos]])),
        inner_back=right(np.block([[cos, sin], [-sin, cos]])),
        back=left(np.concatenate((np.cos(back), -np.sin(back)), axis=1) / length),
    )


def table_dot(table_ref, right):
    return jnp.dot(table_ref[...], jnp.concatenate((right, right), axis=0), preferred_element_type=jnp.float32)


def dot_table(left, table_ref):
    return jnp.dot(jnp.concatenate((left, left), axis=1), table_ref[...], preferred_element_type=jnp.float32)


def spread(source_ref, spread_ref):
    rows = spread_ref.shape[1]
    for j in range(spread_ref.shape[0]):
        part = source_ref[:, :, j * LANES : (j + 1) * LANES]
        spread_ref[j] = part.reshape(rows, LANES).astype(jnp.float32)


def channel_rows(spread_ref, channel, channels):
    senders = spread_ref.shape[1] // channels
    pair = []
    for c in (channel, channel + 1):
        parts = [spread_ref[j, pl.ds(c, senders, stride=channels), :] for j in range(spread_ref.shape[0])]
        pair.append(jnp.concatenate(parts, axis=0).astype(jnp.bfloat16))
    return jnp.concatenate(pair, axis=1)


def spectrum(rows, outer_ref, twist_ref, inner_ref):
    outer = rows.shape[0]
    section = table_dot(outer_ref, rows)
    turned = []
    for lane in (0, LANES):
        real, imag = section[:outer, lane : lane + LANES], section[outer:, lane : lane + LANES]
        turned_real = real * twist_ref[0] - imag * twist_ref[1]
        turned_imag = real * twist_ref[1] + imag * twist_ref[0]
        turned.append(jnp.concatenate((turned_real.astype(jnp.bfloat16), turned_imag.astype(jnp.bfloat16)), axis=1))
    return dot_table(jnp.concatenate(turned, axis=0), inner_ref)


def taps_kernel(taps_ref, outer_ref, twist_ref, inner_ref, out_ref, spread_ref):
    step = pl.program_id(0)
    channels = taps_ref.shape[1]

    @pl.when(step == 0)
    def _():
        spread(taps_ref, spread_ref)

    for pair in range(out_ref.shape[0]):
        channel = step * 2 * out_ref.shape[0] + 2 * pair
        out_ref[pair] = spectrum(channel_rows(spread_ref, channel, channels), outer_ref, twist_ref, inner_ref)


def conv_kernel(
    signal_ref, taps_ref, outer_ref, twist_ref, inner_ref, inner_back_ref, back_ref, out_ref, spread_ref, result_ref
):
    step = pl.program_id(0)
    channels = signal_ref.shape[1]
    receivers = out_ref.shape[0]
    outer = twist_ref.shape[1]

    @pl.when(step == 0)
    def _():
        spread(signal_ref, spread_ref)

    for pair in range(taps_ref.shape[0]):
        channel = step * 2 * taps_ref.shape[0] + 2 * pair
        signal = spectrum(channel_rows(spread_ref, channel, channels), outer_ref, twist_ref, inner_ref)
        taps = taps_ref[pair]
        sig_real, sig_imag = signal[:, :LANES], signal[:, LANES:]
        tap_real, tap_imag = taps[:, :LANES], taps[:, LANES:]
        prod_real = sig_real * tap_real - sig_imag * tap_imag
        prod_imag = sig_real * tap_imag + sig_imag * tap_real
        prod = jnp.concatenate((prod_real.astype(jnp.bfloat16), prod_imag.astype(jnp.bfloat16)), axis=1)
        turned = dot_table(prod, inner_back_ref)
        both = []
        for row in (0, outer):
            real, imag = turned[row : row + outer, :LANES], turned[row : row + outer, LANES:]
            back_real = real * twist_ref[0] + imag * twist_ref[1]
            back_imag = imag * twist_ref[0] - real * twist_ref[1]
            both.append(jnp.concatenate((back_real.astype(jnp.bfloat16), back_imag.astype(jnp.bfloat16)), axis=0))
        rows = table_dot(back_ref, jnp.concatenate(both, axis=1))
        for n in range(2):
            for j in range(result_ref.shape[0]):
                part = rows[j * receivers : (j + 1) * receivers, n * LANES : (n + 1) * LANES]
                result_ref[j, pl.ds(channel + n, receivers, stride=channels), :] = part

    @pl.when(step == pl.num_programs(0) - 1)
    def _():
        for j in range(result_ref.shape[0]):
            part = result_ref[j].reshape(receivers, channels, LANES)
            out_ref[:, :, j * LANES : (j + 1) * LANES] = part.astype(jnp.bfloat16)


def whole(array):
    return pl.BlockSpec(array.shape, lambda i: (0,) * array.ndim)


def transform_taps(taps, tables):
    senders, channels, rows = taps.shape
    outer = tables["twist"].shape[1]
    operands = (taps, tables["taps"], tables["twist"], tables["inner"])
    return pl.pallas_call(
        taps_kernel,
        name="taps_spectrum",
        grid=(channels // (2 * PAIRS),),
        in_specs=[whole(x) for x in operands],
        out_specs=pl.BlockSpec((PAIRS, 2 * outer, 2 * LANES), lambda i: (i, 0, 0)),
        out_shape=jax.ShapeDtypeStruct((channels // 2, 2 * outer, 2 * LANES), jnp.float32),
        scratch_shapes=[pltpu.VMEM((rows // LANES, senders * channels, LANES), jnp.float32)],
        compiler_params=pltpu.CompilerParams(vmem_limit_bytes=VMEM_LIMIT),
        cost_estimate=pl.CostEstimate(flops=5 * 10**9, bytes_accessed=4 * 2**20, transcendentals=0),
    )(*operands)


def convolve(signal, spectra, tables, receivers):
    senders, channels, rows = signal.shape
    out_rows = senders * rows // receivers
    operands = [tables[n] for n in ("signal", "twist", "inner", "inner_back", "back")]
    return pl.pallas_call(
        conv_kernel,
        name="convolution",
        grid=(channels // (2 * PAIRS),),
        in_specs=[whole(signal), pl.BlockSpec((PAIRS,) + spectra.shape[1:], lambda i: (i, 0, 0))]
        + [whole(x) for x in operands],
        out_specs=pl.BlockSpec((receivers, channels, out_rows), lambda i: (0, 0, 0)),
        out_shape=jax.ShapeDtypeStruct((receivers, channels, out_rows), jnp.bfloat16),
        scratch_shapes=[
            pltpu.VMEM((rows // LANES, senders * channels, LANES), jnp.float32),
            pltpu.VMEM((out_rows // LANES, receivers * channels, LANES), jnp.float32),
        ],
        compiler_params=pltpu.CompilerParams(vmem_limit_bytes=VMEM_LIMIT),
        cost_estimate=pl.CostEstimate(flops=7 * 10**9, bytes_accessed=5 * 2**20, transcendentals=0),
    )(signal, spectra, *operands)


def assemble_kernel(x_ref, *rest):
    pieces, (out, held, in_sems, out_sems) = rest[:X_SIZE], rest[X_SIZE:]
    arriving = [pltpu.make_async_copy(pieces[k], held.at[k], in_sems.at[k]) for k in range(X_SIZE)]
    for copy in arriving:
        copy.start()
    leaving = []
    for k, copy in enumerate(arriving):
        column = pl.multiple_of(lax.rem(x_ref[0] + X_SIZE - k, X_SIZE) * HEAD_DIM, HEAD_DIM)
        copy.wait()
        out_copy = pltpu.make_async_copy(held.at[k], out.at[:, pl.ds(column, HEAD_DIM)], out_sems.at[k])
        out_copy.start()
        leaving.append(out_copy)
    for copy in leaving:
        copy.wait()


def assembled(x_index, pieces):
    rows = pieces[0].shape[0]
    anywhere = pl.BlockSpec(memory_space=pl.ANY)
    return pl.pallas_call(
        assemble_kernel,
        name="assemble",
        in_specs=[pl.BlockSpec(memory_space=pltpu.SMEM)] + [anywhere] * X_SIZE,
        out_specs=anywhere,
        out_shape=jax.ShapeDtypeStruct((rows, X_SIZE * HEAD_DIM), jnp.bfloat16),
        scratch_shapes=[
            pltpu.VMEM((X_SIZE, rows, HEAD_DIM), jnp.bfloat16),
            pltpu.SemaphoreType.DMA((X_SIZE,)),
            pltpu.SemaphoreType.DMA((X_SIZE,)),
        ],
        cost_estimate=pl.CostEstimate(flops=2 * 10**9, bytes_accessed=2**20, transcendentals=0),
    )(x_index, *pieces)


def finish_kernel(mixed_ref, gate_ref, hyena_ref):
    mixed = mixed_ref[...].reshape(HEAD_DIM, mixed_ref.shape[3]).T
    hyena_ref[...] = (gate_ref[...].astype(jnp.float32) * mixed.astype(jnp.float32)).astype(jnp.bfloat16)


def finish(returned, out_gate):
    rows, channels = out_gate.shape
    z_size = returned.shape[0] // X_SIZE
    returned = returned.reshape(z_size, X_SIZE, returned.shape[1], rows)
    by_columns = pl.BlockSpec((rows, HEAD_DIM), lambda i: (0, i))
    return pl.pallas_call(
        finish_kernel,
        name="finish",
        grid=(channels // HEAD_DIM,),
        in_specs=[pl.BlockSpec((z_size, 1, returned.shape[2], rows), lambda i: (0, i, 0, 0)), by_columns],
        out_specs=by_columns,
        out_shape=jax.ShapeDtypeStruct((rows, channels), jnp.bfloat16),
        compiler_params=pltpu.CompilerParams(vmem_limit_bytes=16 * 2**20),
    )(returned, out_gate)


def body(queries, key_rows, values, doc_lengths, in_gate, out_gate, filter_taps):
    row_count, channels = queries.shape
    ctx = lax.axis_size("ctx")
    z_size = ctx // X_SIZE
    group_rows = X_SIZE * row_count
    per_device = channels // ctx
    z_groups = [[z * X_SIZE + x for z in range(z_size)] for x in range(X_SIZE)]
    tables = transform_tables(row_count * ctx, z_size, ctx)
    me = lax.axis_index("ctx").astype(jnp.int32)
    x_index = lax.rem(me, X_SIZE).reshape(1)

    def exchanged(x, groups=None):
        return lax.all_to_all(x, "ctx", split_axis=0, concat_axis=0, tiled=True, axis_index_groups=groups)

    def along_x(piece, k):
        pairs = [(z * X_SIZE + x, z * X_SIZE + (x + k) % X_SIZE) for z in range(z_size) for x in range(X_SIZE)]
        return lax.ppermute(piece, "ctx", pairs)

    def along_z(piece, k):
        pairs = [(i, i + X_SIZE) for i in range(ctx - X_SIZE) if i % X_SIZE != k]
        return lax.ppermute(piece, "ctx", pairs)

    def arrived(pieces):
        return [pieces[0]] + [along_x(pieces[k], k) for k in range(1, X_SIZE)]

    taps = filter_taps.astype(jnp.bfloat16).reshape(X_SIZE, z_size, per_device, row_count)
    taps = taps.transpose(1, 0, 2, 3).reshape(ctx, per_device, row_count)
    pieces = pieces_of(x_index, key_rows, values)
    own = arrived(pieces)
    taps, _ = lax.optimization_barrier((taps, pieces[0]))
    taps = exchanged(taps)
    before = [along_z(own[k], k) for k in range(X_SIZE)]
    own[1], queries, in_gate = lax.optimization_barrier((own[1], queries, in_gate))
    asked = arrived(pieces_of(x_index, queries, in_gate))

    group_first = (me // X_SIZE) * group_rows
    positions = group_first + jnp.arange(group_rows, dtype=jnp.int32)
    start = document_starts(positions, doc_lengths) - (group_first - group_rows)

    attended, gated = attention(x_index, own, before, asked, start)
    gated, taps = lax.optimization_barrier((gated, taps))
    signal = exchanged(gated.reshape(z_size, per_device, group_rows), z_groups)
    spectra = transform_taps(taps, tables)
    spectra, attended = lax.optimization_barrier((spectra, attended))
    attended = arrived([attended[k] for k in range(X_SIZE)])
    mixed = convolve(signal, spectra, tables, ctx)
    mixed, *attended = lax.optimization_barrier((mixed, *attended))
    returned = exchanged(mixed)
    return assembled(x_index, attended), finish(returned, out_gate)


def solution(mesh):
    return jax.shard_map(
        body,
        mesh=mesh,
        in_specs=(
            P(("dp", "ctx"), "tp"),
            P(("dp", "ctx"), "tp"),
            P(("dp", "ctx"), "tp"),
            P("dp"),
            P(("dp", "ctx"), "tp"),
            P(("dp", "ctx"), "tp"),
            P(("dp", "tp"), "ctx"),
        ),
        out_specs=(P(("dp", "ctx"), "tp"), P(("dp", "ctx"), "tp")),
        check_vma=False,
    )
```

```python
import functools
import math

import jax
import jax.numpy as jnp
import ml_dtypes
import numpy as np
from jax import lax
from jax.experimental import pallas as pl
from jax.experimental.pallas import tpu as pltpu
from jax.sharding import PartitionSpec as P

HEAD_DIM = 128
X_SIZE = 4
Q_BLOCK = 768
K_BLOCK = 384
Q_SUB = 768
LANES = 128
VMEM_LIMIT = 62 * 2**20
PAIRS = 4
masked_score = -1e30


def document_starts(positions, doc_lengths):
    order = jnp.arange(doc_lengths.shape[0], dtype=jnp.int32)
    before = order[:, None] < order[None, :]
    starts = jnp.sum(jnp.where(before, doc_lengths[:, None], 0), axis=0)
    inside = starts[None, :] <= positions[:, None]
    return jnp.max(jnp.where(inside, starts[None, :], 0), axis=1)


def pieces_kernel(x_ref, first_ref, second_ref, *rest):
    outs, (held, in_sems, out_sems) = rest[:X_SIZE], rest[X_SIZE:]
    arriving, leaving = [], []
    for k in range(X_SIZE):
        column = pl.multiple_of(lax.rem(x_ref[0] + k, X_SIZE) * HEAD_DIM, HEAD_DIM)
        for which, ref in enumerate((first_ref, second_ref)):
            copy = pltpu.make_async_copy(ref.at[:, pl.ds(column, HEAD_DIM)], held.at[k, which], in_sems.at[k, which])
            copy.start()
            arriving.append((k, which, copy))
    for k, which, copy in arriving:
        copy.wait()
        out = pltpu.make_async_copy(held.at[k, which], outs[k].at[which], out_sems.at[k, which])
        out.start()
        leaving.append(out)
    for out in leaving:
        out.wait()


def pieces_of(x_index, first, second):
    rows = first.shape[0]
    anywhere = pl.BlockSpec(memory_space=pl.ANY)
    return pl.pallas_call(
        pieces_kernel,
        name="pieces",
        in_specs=[pl.BlockSpec(memory_space=pltpu.SMEM), anywhere, anywhere],
        out_specs=[anywhere] * X_SIZE,
        out_shape=[jax.ShapeDtypeStruct((2, rows, HEAD_DIM), jnp.bfloat16)] * X_SIZE,
        scratch_shapes=[
            pltpu.VMEM((X_SIZE, 2, rows, HEAD_DIM), jnp.bfloat16),
            pltpu.SemaphoreType.DMA((X_SIZE, 2)),
            pltpu.SemaphoreType.DMA((X_SIZE, 2)),
        ],
    )(x_index, first, second)


def attention_kernel(lo_ref, mid_ref, x_ref, start_ref, *rest):
    own, before, asked = rest[:X_SIZE], rest[X_SIZE : 2 * X_SIZE], rest[2 * X_SIZE : 3 * X_SIZE]
    out_ref, gated_ref, keys, values, values_t, queries_all, gate_all, sems = rest[3 * X_SIZE :]
    step = pl.program_id(0)
    group = queries_all.shape[0]
    piece = group // X_SIZE
    group_blocks = group // K_BLOCK
    piece_blocks = piece // K_BLOCK

    def copies_of(k, chosen, sources):
        at = pl.multiple_of(lax.rem(x_ref[0] + X_SIZE - k, X_SIZE) * piece, piece)
        early, late = pl.ds(at, piece), pl.ds(at + group, piece)
        targets = (keys.at[early], values.at[early], keys.at[late], values.at[late], queries_all.at[early], gate_all.at[early])
        return [pltpu.make_async_copy(sources[n // 2].at[n % 2], targets[n], sems.at[k, n]) for n in chosen]

    def reached(k):
        position = lax.rem(x_ref[0] + X_SIZE - k, X_SIZE)
        return jnp.logical_and(position > 0, (position + 1) * piece_blocks > lo_ref[0])

    def turn(block, _):
        rows = values[pl.ds(pl.multiple_of(block * K_BLOCK, K_BLOCK), K_BLOCK)]
        values_t[block] = rows.T
        return 0

    @pl.when(step == 0)
    def _():
        for k in range(X_SIZE):
            sources = (before[k], own[k], asked[k])

            @pl.when(reached(k))
            def _():
                for copy in copies_of(k, (0, 1), sources):
                    copy.start()

            for copy in copies_of(k, (2, 3, 4, 5), sources):
                copy.start()
        for k in range(X_SIZE):

            @pl.when(reached(k))
            def _():
                for copy in copies_of(k, (0, 1), (before[k], own[k], asked[k])):
                    copy.wait()

        lax.fori_loop(lo_ref[0], group_blocks, turn, 0)

    now = lax.rem(x_ref[0] + X_SIZE - step, X_SIZE)
    for copy in copies_of(now, (2, 3, 4, 5), (before[0], own[0], asked[0])):
        copy.wait()
    first = group + step * Q_BLOCK
    diagonal = first // K_BLOCK
    last = (first + Q_BLOCK - 1) // K_BLOCK
    lax.fori_loop(diagonal, last + 1, turn, 0)

    here = pl.ds(pl.multiple_of(step * Q_BLOCK, Q_BLOCK), Q_BLOCK)
    queries = queries_all[here].T
    start = start_ref[0]
    query_index = first + lax.broadcasted_iota(jnp.int32, (1, Q_BLOCK), 1)
    key_offset = lax.broadcasted_iota(jnp.int32, (K_BLOCK, 1), 0)
    factor = math.log2(math.e) / math.sqrt(HEAD_DIM)
    subs = [slice(at, at + Q_SUB) for at in range(0, Q_BLOCK, Q_SUB)]

    def visit(kind, block, carried):
        key_rows = keys[pl.ds(pl.multiple_of(block * K_BLOCK, K_BLOCK), K_BLOCK)]
        block_values = values_t[block]
        index = block * K_BLOCK + key_offset
        result = []
        for sub, (top, total, weighted) in zip(subs, carried):
            scores = jnp.dot(key_rows, queries[:, sub], preferred_element_type=jnp.float32) * factor
            if kind == "before":
                scores = jnp.where(index >= start[:, sub], scores, masked_score)
            if kind == "diagonal":
                kept = (index >= start[:, sub]) & (index <= query_index[:, sub])
                scores = jnp.where(kept, scores, masked_score)
            new_top = jnp.maximum(top, jnp.max(scores, axis=0, keepdims=True))
            rescale = jnp.exp2(top - new_top)
            weight = jnp.exp2(scores - new_top)
            total = total * rescale + jnp.sum(weight, axis=0, keepdims=True)
            weighted = weighted * rescale + jnp.dot(
                block_values, weight.astype(jnp.bfloat16), preferred_element_type=jnp.float32
            )
            result.append((new_top, total, weighted))
        return tuple(result)

    middle = jnp.minimum(mid_ref[step], diagonal)
    carried = tuple(
        (
            jnp.full((1, Q_SUB), masked_score, jnp.float32),
            jnp.zeros((1, Q_SUB), jnp.float32),
            jnp.zeros((HEAD_DIM, Q_SUB), jnp.float32),
        )
        for _ in subs
    )
    carried = lax.fori_loop(lo_ref[step], middle, functools.partial(visit, "before"), carried)
    carried = lax.fori_loop(middle, diagonal, functools.partial(visit, "inside"), carried)
    carried = lax.fori_loop(diagonal, last + 1, functools.partial(visit, "diagonal"), carried)
    gate = gate_all[here].T
    for sub, (top, total, weighted) in zip(subs, carried):
        rounded = (weighted * (1.0 / total)).astype(jnp.bfloat16)
        out_ref[0, sub] = rounded.T
        gated_ref[:, sub] = (rounded.astype(jnp.float32) * gate[:, sub].astype(jnp.float32)).astype(jnp.bfloat16)


def attention(x_index, own, before, asked, start):
    rows = X_SIZE * own[0].shape[1]
    steps = rows // Q_BLOCK
    lo = start[::Q_BLOCK] // K_BLOCK
    middle = start[Q_BLOCK - 1 :: Q_BLOCK] // K_BLOCK + 1
    anywhere = pl.BlockSpec(memory_space=pl.ANY)
    return pl.pallas_call(
        attention_kernel,
        name="attention",
        grid_spec=pltpu.PrefetchScalarGridSpec(
            num_scalar_prefetch=3,
            grid=(steps,),
            in_specs=[pl.BlockSpec((1, 1, Q_BLOCK), lambda i, *_: (i, 0, 0))] + [anywhere] * (3 * X_SIZE),
            out_specs=[
                pl.BlockSpec((1, Q_BLOCK, HEAD_DIM), lambda i, lo, mid, x: (lax.rem(i - x[0] + X_SIZE, X_SIZE), 0, 0)),
                pl.BlockSpec((HEAD_DIM, Q_BLOCK), lambda i, *_: (0, i)),
            ],
            scratch_shapes=[
                pltpu.VMEM((2 * rows, HEAD_DIM), jnp.bfloat16),
                pltpu.VMEM((2 * rows, HEAD_DIM), jnp.bfloat16),
                pltpu.VMEM((2 * rows // K_BLOCK, HEAD_DIM, K_BLOCK), jnp.bfloat16),
                pltpu.VMEM((rows, HEAD_DIM), jnp.bfloat16),
                pltpu.VMEM((rows, HEAD_DIM), jnp.bfloat16),
                pltpu.SemaphoreType.DMA((X_SIZE, 6)),
            ],
        ),
        out_shape=[
            jax.ShapeDtypeStruct((X_SIZE, rows // X_SIZE, HEAD_DIM), jnp.bfloat16),
            jax.ShapeDtypeStruct((HEAD_DIM, rows), jnp.bfloat16),
        ],
        compiler_params=pltpu.CompilerParams(vmem_limit_bytes=VMEM_LIMIT),
        cost_estimate=pl.CostEstimate(
            flops=16 * 10**9, bytes_accessed=10 * rows * HEAD_DIM, transcendentals=rows * 1536
        ),
    )(lo, middle, x_index, start.reshape(steps, 1, Q_BLOCK), *own, *before, *asked)


def high_low(table):
    high = table.astype(np.float32).astype(ml_dtypes.bfloat16)
    low = (table - high.astype(np.float64)).astype(np.float32).astype(ml_dtypes.bfloat16)
    return high, low


def transform_tables(length, senders, tap_senders):
    outer = length // LANES
    k1 = np.arange(outer)
    per_sender = outer // senders
    a_signal = (np.arange(senders)[None, :] * per_sender + np.arange(per_sender)[:, None]).reshape(-1)
    per_tap = outer // tap_senders
    a_tap = (np.arange(tap_senders)[None, :] * per_tap + np.arange(per_tap)[:, None]).reshape(-1)
    b = np.arange(LANES)

    def angles(a):
        return 2.0 * np.pi * ((4 * k1[:, None] + 1) * a[None, :] % (4 * outer)) / (4 * outer)

    def left(table):
        return np.concatenate(high_low(table), axis=1)

    def right(table):
        return np.concatenate(high_low(table), axis=0)

    def forward(a):
        angle = angles(a)
        return left(np.concatenate((np.cos(angle), -np.sin(angle)), axis=0))

    twist = 2.0 * np.pi * ((4 * k1[:, None] + 1) * b[None, :] % (4 * length)) / (4 * length)
    inner = 2.0 * np.pi * (b[:, None] * b[None, :] % LANES) / LANES
    cos, sin = np.cos(inner), np.sin(inner)
    back = angles(a_tap).T
    return dict(
        signal=forward(a_signal),
        taps=forward(a_tap),
        twist=np.stack((np.cos(twist), -np.sin(twist))).astype(np.float32),
        inner=right(np.block([[cos, -sin], [sin, cos]])),
        inner_back=right(np.block([[cos, sin], [-sin, cos]])),
        back=left(np.concatenate((np.cos(back), -np.sin(back)), axis=1) / length),
    )


def table_dot(table_ref, right):
    return jnp.dot(table_ref[...], jnp.concatenate((right, right), axis=0), preferred_element_type=jnp.float32)


def dot_table(left, table_ref):
    return jnp.dot(jnp.concatenate((left, left), axis=1), table_ref[...], preferred_element_type=jnp.float32)


def spread(source_ref, spread_ref):
    rows = spread_ref.shape[1]
    for j in range(spread_ref.shape[0]):
        part = source_ref[:, :, j * LANES : (j + 1) * LANES]
        spread_ref[j] = part.reshape(rows, LANES).astype(jnp.float32)


def channel_rows(spread_ref, channel, channels):
    senders = spread_ref.shape[1] // channels
    pair = []
    for c in (channel, channel + 1):
        parts = [spread_ref[j, pl.ds(c, senders, stride=channels), :] for j in range(spread_ref.shape[0])]
        pair.append(jnp.concatenate(parts, axis=0).astype(jnp.bfloat16))
    return jnp.concatenate(pair, axis=1)


def spectrum(rows, outer_ref, twist_ref, inner_ref):
    outer = rows.shape[0]
    section = table_dot(outer_ref, rows)
    turned = []
    for lane in (0, LANES):
        real, imag = section[:outer, lane : lane + LANES], section[outer:, lane : lane + LANES]
        turned_real = real * twist_ref[0] - imag * twist_ref[1]
        turned_imag = real * twist_ref[1] + imag * twist_ref[0]
        turned.append(jnp.concatenate((turned_real.astype(jnp.bfloat16), turned_imag.astype(jnp.bfloat16)), axis=1))
    return dot_table(jnp.concatenate(turned, axis=0), inner_ref)


def taps_kernel(taps_ref, outer_ref, twist_ref, inner_ref, out_ref, spread_ref):
    step = pl.program_id(0)
    channels = taps_ref.shape[1]

    @pl.when(step == 0)
    def _():
        spread(taps_ref, spread_ref)

    for pair in range(out_ref.shape[0]):
        channel = step * 2 * out_ref.shape[0] + 2 * pair
        out_ref[pair] = spectrum(channel_rows(spread_ref, channel, channels), outer_ref, twist_ref, inner_ref)


def conv_kernel(
    signal_ref, taps_ref, outer_ref, twist_ref, inner_ref, inner_back_ref, back_ref, out_ref, spread_ref, result_ref
):
    step = pl.program_id(0)
    channels = signal_ref.shape[1]
    receivers = out_ref.shape[0]
    outer = twist_ref.shape[1]

    @pl.when(step == 0)
    def _():
        spread(signal_ref, spread_ref)

    for pair in range(taps_ref.shape[0]):
        channel = step * 2 * taps_ref.shape[0] + 2 * pair
        signal = spectrum(channel_rows(spread_ref, channel, channels), outer_ref, twist_ref, inner_ref)
        taps = taps_ref[pair]
        sig_real, sig_imag = signal[:, :LANES], signal[:, LANES:]
        tap_real, tap_imag = taps[:, :LANES], taps[:, LANES:]
        prod_real = sig_real * tap_real - sig_imag * tap_imag
        prod_imag = sig_real * tap_imag + sig_imag * tap_real
        prod = jnp.concatenate((prod_real.astype(jnp.bfloat16), prod_imag.astype(jnp.bfloat16)), axis=1)
        turned = dot_table(prod, inner_back_ref)
        both = []
        for row in (0, outer):
            real, imag = turned[row : row + outer, :LANES], turned[row : row + outer, LANES:]
            back_real = real * twist_ref[0] + imag * twist_ref[1]
            back_imag = imag * twist_ref[0] - real * twist_ref[1]
            both.append(jnp.concatenate((back_real.astype(jnp.bfloat16), back_imag.astype(jnp.bfloat16)), axis=0))
        rows = table_dot(back_ref, jnp.concatenate(both, axis=1))
        for n in range(2):
            for j in range(result_ref.shape[0]):
                part = rows[j * receivers : (j + 1) * receivers, n * LANES : (n + 1) * LANES]
                result_ref[j, pl.ds(channel + n, receivers, stride=channels), :] = part

    @pl.when(step == pl.num_programs(0) - 1)
    def _():
        for j in range(result_ref.shape[0]):
            part = result_ref[j].reshape(receivers, channels, LANES)
            out_ref[:, :, j * LANES : (j + 1) * LANES] = part.astype(jnp.bfloat16)


def whole(array):
    return pl.BlockSpec(array.shape, lambda i: (0,) * array.ndim)


def transform_taps(taps, tables):
    senders, channels, rows = taps.shape
    outer = tables["twist"].shape[1]
    operands = (taps, tables["taps"], tables["twist"], tables["inner"])
    return pl.pallas_call(
        taps_kernel,
        name="taps_spectrum",
        grid=(channels // (2 * PAIRS),),
        in_specs=[whole(x) for x in operands],
        out_specs=pl.BlockSpec((PAIRS, 2 * outer, 2 * LANES), lambda i: (i, 0, 0)),
        out_shape=jax.ShapeDtypeStruct((channels // 2, 2 * outer, 2 * LANES), jnp.float32),
        scratch_shapes=[pltpu.VMEM((rows // LANES, senders * channels, LANES), jnp.float32)],
        compiler_params=pltpu.CompilerParams(vmem_limit_bytes=VMEM_LIMIT),
        cost_estimate=pl.CostEstimate(flops=5 * 10**9, bytes_accessed=4 * 2**20, transcendentals=0),
    )(*operands)


def convolve(signal, spectra, tables, receivers):
    senders, channels, rows = signal.shape
    out_rows = senders * rows // receivers
    operands = [tables[n] for n in ("signal", "twist", "inner", "inner_back", "back")]
    return pl.pallas_call(
        conv_kernel,
        name="convolution",
        grid=(channels // (2 * PAIRS),),
        in_specs=[whole(signal), pl.BlockSpec((PAIRS,) + spectra.shape[1:], lambda i: (i, 0, 0))]
        + [whole(x) for x in operands],
        out_specs=pl.BlockSpec((receivers, channels, out_rows), lambda i: (0, 0, 0)),
        out_shape=jax.ShapeDtypeStruct((receivers, channels, out_rows), jnp.bfloat16),
        scratch_shapes=[
            pltpu.VMEM((rows // LANES, senders * channels, LANES), jnp.float32),
            pltpu.VMEM((out_rows // LANES, receivers * channels, LANES), jnp.float32),
        ],
        compiler_params=pltpu.CompilerParams(vmem_limit_bytes=VMEM_LIMIT),
        cost_estimate=pl.CostEstimate(flops=7 * 10**9, bytes_accessed=5 * 2**20, transcendentals=0),
    )(signal, spectra, *operands)


def assemble_kernel(x_ref, *rest):
    pieces, (out, held, in_sems, out_sems) = rest[:X_SIZE], rest[X_SIZE:]
    arriving = [pltpu.make_async_copy(pieces[k], held.at[k], in_sems.at[k]) for k in range(X_SIZE)]
    for copy in arriving:
        copy.start()
    leaving = []
    for k, copy in enumerate(arriving):
        column = pl.multiple_of(lax.rem(x_ref[0] + X_SIZE - k, X_SIZE) * HEAD_DIM, HEAD_DIM)
        copy.wait()
        out_copy = pltpu.make_async_copy(held.at[k], out.at[:, pl.ds(column, HEAD_DIM)], out_sems.at[k])
        out_copy.start()
        leaving.append(out_copy)
    for copy in leaving:
        copy.wait()


def assembled(x_index, pieces):
    rows = pieces[0].shape[0]
    anywhere = pl.BlockSpec(memory_space=pl.ANY)
    return pl.pallas_call(
        assemble_kernel,
        name="assemble",
        in_specs=[pl.BlockSpec(memory_space=pltpu.SMEM)] + [anywhere] * X_SIZE,
        out_specs=anywhere,
        out_shape=jax.ShapeDtypeStruct((rows, X_SIZE * HEAD_DIM), jnp.bfloat16),
        scratch_shapes=[
            pltpu.VMEM((X_SIZE, rows, HEAD_DIM), jnp.bfloat16),
            pltpu.SemaphoreType.DMA((X_SIZE,)),
            pltpu.SemaphoreType.DMA((X_SIZE,)),
        ],
        cost_estimate=pl.CostEstimate(flops=2 * 10**9, bytes_accessed=2**20, transcendentals=0),
    )(x_index, *pieces)


def finish_kernel(mixed_ref, gate_ref, hyena_ref):
    mixed = mixed_ref[...].reshape(HEAD_DIM, mixed_ref.shape[3]).T
    hyena_ref[...] = (gate_ref[...].astype(jnp.float32) * mixed.astype(jnp.float32)).astype(jnp.bfloat16)


def finish(returned, out_gate):
    rows, channels = out_gate.shape
    z_size = returned.shape[0] // X_SIZE
    returned = returned.reshape(z_size, X_SIZE, returned.shape[1], rows)
    by_columns = pl.BlockSpec((rows, HEAD_DIM), lambda i: (0, i))
    return pl.pallas_call(
        finish_kernel,
        name="finish",
        grid=(channels // HEAD_DIM,),
        in_specs=[pl.BlockSpec((z_size, 1, returned.shape[2], rows), lambda i: (0, i, 0, 0)), by_columns],
        out_specs=by_columns,
        out_shape=jax.ShapeDtypeStruct((rows, channels), jnp.bfloat16),
        compiler_params=pltpu.CompilerParams(vmem_limit_bytes=16 * 2**20),
    )(returned, out_gate)


def body(queries, key_rows, values, doc_lengths, in_gate, out_gate, filter_taps):
    row_count, channels = queries.shape
    ctx = lax.axis_size("ctx")
    z_size = ctx // X_SIZE
    group_rows = X_SIZE * row_count
    per_device = channels // ctx
    z_groups = [[z * X_SIZE + x for z in range(z_size)] for x in range(X_SIZE)]
    tables = transform_tables(row_count * ctx, z_size, ctx)
    me = lax.axis_index("ctx").astype(jnp.int32)
    x_index = lax.rem(me, X_SIZE).reshape(1)

    def exchanged(x, groups=None):
        return lax.all_to_all(x, "ctx", split_axis=0, concat_axis=0, tiled=True, axis_index_groups=groups)

    def along_x(piece, k):
        pairs = [(z * X_SIZE + x, z * X_SIZE + (x + k) % X_SIZE) for z in range(z_size) for x in range(X_SIZE)]
        return lax.ppermute(piece, "ctx", pairs)

    def along_z(piece, k):
        pairs = [(i, i + X_SIZE) for i in range(ctx - X_SIZE) if i % X_SIZE != k]
        return lax.ppermute(piece, "ctx", pairs)

    def arrived(pieces):
        return [pieces[0]] + [along_x(pieces[k], k) for k in range(1, X_SIZE)]

    taps = filter_taps.astype(jnp.bfloat16).reshape(X_SIZE, z_size, per_device, row_count)
    taps = taps.transpose(1, 0, 2, 3).reshape(ctx, per_device, row_count)
    own = arrived(pieces_of(x_index, key_rows, values))
    before = [along_z(own[k], k) for k in range(X_SIZE)]
    own[1], queries, in_gate = lax.optimization_barrier((own[1], queries, in_gate))
    asked = pieces_of(x_index, queries, in_gate)
    taps, *_ = lax.optimization_barrier((taps, *own, *asked))
    asked = arrived(asked)
    taps = exchanged(taps)

    group_first = (me // X_SIZE) * group_rows
    positions = group_first + jnp.arange(group_rows, dtype=jnp.int32)
    start = document_starts(positions, doc_lengths) - (group_first - group_rows)

    attended, gated = attention(x_index, own, before, asked, start)
    gated, taps = lax.optimization_barrier((gated, taps))
    signal = exchanged(gated.reshape(z_size, per_device, group_rows), z_groups)
    spectra = transform_taps(taps, tables)
    spectra, attended = lax.optimization_barrier((spectra, attended))
    attended = arrived([attended[k] for k in range(X_SIZE)])
    mixed = convolve(signal, spectra, tables, ctx)
    mixed, *attended = lax.optimization_barrier((mixed, *attended))
    returned = exchanged(mixed)
    return assembled(x_index, attended), finish(returned, out_gate)


def solution(mesh):
    return jax.shard_map(
        body,
        mesh=mesh,
        in_specs=(
            P(("dp", "ctx"), "tp"),
            P(("dp", "ctx"), "tp"),
            P(("dp", "ctx"), "tp"),
            P("dp"),
            P(("dp", "ctx"), "tp"),
            P(("dp", "ctx"), "tp"),
            P(("dp", "tp"), "ctx"),
        ),
        out_specs=(P(("dp", "ctx"), "tp"), P(("dp", "ctx"), "tp")),
        check_vma=False,
    )
```

```python
import functools
import math

import jax
import jax.numpy as jnp
import ml_dtypes
import numpy as np
from jax import lax
from jax.experimental import pallas as pl
from jax.experimental.pallas import tpu as pltpu
from jax.sharding import PartitionSpec as P

HEAD_DIM = 128
X_SIZE = 4
NEAR_FIRST = (0, 1, 3, 2)
Q_BLOCK = 768
K_BLOCK = 384
LANES = 128
VMEM_LIMIT = 63 * 2**20
PAIRS = 4
masked_score = -1e30


def document_starts(positions, doc_lengths):
    order = jnp.arange(doc_lengths.shape[0], dtype=jnp.int32)
    before = order[:, None] < order[None, :]
    starts = jnp.sum(jnp.where(before, doc_lengths[:, None], 0), axis=0)
    inside = starts[None, :] <= positions[:, None]
    return jnp.max(jnp.where(inside, starts[None, :], 0), axis=1)


def pieces_kernel(x_ref, first_ref, second_ref, *rest):
    outs, (held, in_sems, out_sems) = rest[:X_SIZE], rest[X_SIZE:]
    arriving, leaving = [], []
    for k in range(X_SIZE):
        column = pl.multiple_of(lax.rem(x_ref[0] + k, X_SIZE) * HEAD_DIM, HEAD_DIM)
        for which, ref in enumerate((first_ref, second_ref)):
            copy = pltpu.make_async_copy(ref.at[:, pl.ds(column, HEAD_DIM)], held.at[k, which], in_sems.at[k, which])
            copy.start()
            arriving.append((k, which, copy))
    for k, which, copy in arriving:
        copy.wait()
        out = pltpu.make_async_copy(held.at[k, which], outs[k].at[which], out_sems.at[k, which])
        out.start()
        leaving.append(out)
    for out in leaving:
        out.wait()


def pieces_of(x_index, first, second):
    rows = first.shape[0]
    anywhere = pl.BlockSpec(memory_space=pl.ANY)
    return pl.pallas_call(
        pieces_kernel,
        name="pieces",
        in_specs=[pl.BlockSpec(memory_space=pltpu.SMEM), anywhere, anywhere],
        out_specs=[anywhere] * X_SIZE,
        out_shape=[jax.ShapeDtypeStruct((2, rows, HEAD_DIM), jnp.bfloat16)] * X_SIZE,
        scratch_shapes=[
            pltpu.VMEM((X_SIZE, 2, rows, HEAD_DIM), jnp.bfloat16),
            pltpu.SemaphoreType.DMA((X_SIZE, 2)),
            pltpu.SemaphoreType.DMA((X_SIZE, 2)),
        ],
    )(x_index, first, second)


def attention_kernel(lo_ref, mid_ref, x_ref, start_ref, *rest):
    own, before, asked = rest[:X_SIZE], rest[X_SIZE : 2 * X_SIZE], rest[2 * X_SIZE : 3 * X_SIZE]
    out_ref, gated_ref, keys, values, values_t, queries_all, gate_all, weighted_ref, sems = rest[3 * X_SIZE :]
    step = pl.program_id(0)
    group = queries_all.shape[0]
    piece = group // X_SIZE
    group_blocks = group // K_BLOCK
    piece_blocks = piece // K_BLOCK

    def copies_of(k, chosen, sources):
        at = pl.multiple_of(lax.rem(x_ref[0] + X_SIZE - k, X_SIZE) * piece, piece)
        early, late = pl.ds(at, piece), pl.ds(at + group, piece)
        targets = (keys.at[early], values.at[early], keys.at[late], values.at[late], queries_all.at[early], gate_all.at[early])
        return [pltpu.make_async_copy(sources[n // 2].at[n % 2], targets[n], sems.at[k, n]) for n in chosen]

    def reached(k):
        position = lax.rem(x_ref[0] + X_SIZE - k, X_SIZE)
        return jnp.logical_and(position > 0, (position + 1) * piece_blocks > lo_ref[0])

    def turn(block, _):
        rows = values[pl.ds(pl.multiple_of(block * K_BLOCK, K_BLOCK), K_BLOCK)]
        values_t[block] = rows.T
        return 0

    @pl.when(step == 0)
    def _():
        for k in range(X_SIZE):
            sources = (before[k], own[k], asked[k])

            @pl.when(reached(k))
            def _():
                for copy in copies_of(k, (0, 1), sources):
                    copy.start()

            for copy in copies_of(k, (2, 3, 4, 5), sources):
                copy.start()
        for k in range(X_SIZE):

            @pl.when(reached(k))
            def _():
                for copy in copies_of(k, (0, 1), (before[k], own[k], asked[k])):
                    copy.wait()

        lax.fori_loop(lo_ref[0], group_blocks, turn, 0)

    now = lax.rem(x_ref[0] + X_SIZE - step, X_SIZE)
    for copy in copies_of(now, (2, 3, 4, 5), (before[0], own[0], asked[0])):
        copy.wait()
    first = group + step * Q_BLOCK
    diagonal = first // K_BLOCK
    last = (first + Q_BLOCK - 1) // K_BLOCK
    lax.fori_loop(diagonal, last + 1, turn, 0)

    here = pl.ds(pl.multiple_of(step * Q_BLOCK, Q_BLOCK), Q_BLOCK)
    queries = queries_all[here].T
    start = start_ref[0]
    query_index = first + lax.broadcasted_iota(jnp.int32, (1, Q_BLOCK), 1)
    key_offset = lax.broadcasted_iota(jnp.int32, (K_BLOCK, 1), 0)
    factor = math.log2(math.e) / math.sqrt(HEAD_DIM)
    weighted_ref[...] = jnp.zeros_like(weighted_ref)

    def visit(kind, block, carried):
        top, total = carried
        key_rows = keys[pl.ds(pl.multiple_of(block * K_BLOCK, K_BLOCK), K_BLOCK)]
        scores = jnp.dot(key_rows, queries, preferred_element_type=jnp.float32) * factor
        index = block * K_BLOCK + key_offset
        if kind == "before":
            scores = jnp.where(index >= start, scores, masked_score)
        if kind == "diagonal":
            scores = jnp.where((index >= start) & (index <= query_index), scores, masked_score)
        new_top = jnp.maximum(top, jnp.max(scores, axis=0, keepdims=True))
        rescale = jnp.exp2(top - new_top)
        weight = jnp.exp2(scores - new_top)
        total = total * rescale + jnp.sum(weight, axis=0, keepdims=True)
        weighted_ref[...] = weighted_ref[...] * rescale + jnp.dot(
            values_t[block], weight.astype(jnp.bfloat16), preferred_element_type=jnp.float32
        )
        return new_top, total

    middle = jnp.minimum(mid_ref[step], diagonal)
    carried = (
        jnp.full((1, Q_BLOCK), masked_score, jnp.float32),
        jnp.zeros((1, Q_BLOCK), jnp.float32),
    )
    carried = lax.fori_loop(lo_ref[step], middle, functools.partial(visit, "before"), carried)
    carried = lax.fori_loop(middle, diagonal, functools.partial(visit, "inside"), carried)
    _, total = lax.fori_loop(diagonal, last + 1, functools.partial(visit, "diagonal"), carried)
    rounded = (weighted_ref[...] * (1.0 / total)).astype(jnp.bfloat16)
    out_ref[0] = rounded.T
    gated = rounded.astype(jnp.float32) * gate_all[here].T.astype(jnp.float32)
    gated_ref[...] = gated.astype(jnp.bfloat16)


def attention(x_index, own, before, asked, start):
    rows = X_SIZE * own[0].shape[1]
    steps = rows // Q_BLOCK
    lo = start[::Q_BLOCK] // K_BLOCK
    middle = start[Q_BLOCK - 1 :: Q_BLOCK] // K_BLOCK + 1
    anywhere = pl.BlockSpec(memory_space=pl.ANY)
    return pl.pallas_call(
        attention_kernel,
        name="attention",
        grid_spec=pltpu.PrefetchScalarGridSpec(
            num_scalar_prefetch=3,
            grid=(steps,),
            in_specs=[pl.BlockSpec((1, 1, Q_BLOCK), lambda i, *_: (i, 0, 0))] + [anywhere] * (3 * X_SIZE),
            out_specs=[
                pl.BlockSpec((1, Q_BLOCK, HEAD_DIM), lambda i, lo, mid, x: (lax.rem(i - x[0] + X_SIZE, X_SIZE), 0, 0)),
                pl.BlockSpec((HEAD_DIM, Q_BLOCK), lambda i, *_: (0, i)),
            ],
            scratch_shapes=[
                pltpu.VMEM((2 * rows, HEAD_DIM), jnp.bfloat16),
                pltpu.VMEM((2 * rows, HEAD_DIM), jnp.bfloat16),
                pltpu.VMEM((2 * rows // K_BLOCK, HEAD_DIM, K_BLOCK), jnp.bfloat16),
                pltpu.VMEM((rows, HEAD_DIM), jnp.bfloat16),
                pltpu.VMEM((rows, HEAD_DIM), jnp.bfloat16),
                pltpu.VMEM((HEAD_DIM, Q_BLOCK), jnp.float32),
                pltpu.SemaphoreType.DMA((X_SIZE, 6)),
            ],
        ),
        out_shape=[
            jax.ShapeDtypeStruct((X_SIZE, rows // X_SIZE, HEAD_DIM), jnp.bfloat16),
            jax.ShapeDtypeStruct((HEAD_DIM, rows), jnp.bfloat16),
        ],
        compiler_params=pltpu.CompilerParams(vmem_limit_bytes=VMEM_LIMIT),
        cost_estimate=pl.CostEstimate(
            flops=16 * 10**9, bytes_accessed=10 * rows * HEAD_DIM, transcendentals=rows * 1536
        ),
    )(lo, middle, x_index, start.reshape(steps, 1, Q_BLOCK), *own, *before, *asked)


def high_low(table):
    high = table.astype(np.float32).astype(ml_dtypes.bfloat16)
    low = (table - high.astype(np.float64)).astype(np.float32).astype(ml_dtypes.bfloat16)
    return np.stack((high, low))


def transform_tables(length, senders, tap_senders):
    outer = length // LANES
    k1 = np.arange(outer)
    per_sender = outer // senders
    a_signal = (np.arange(senders)[None, :] * per_sender + np.arange(per_sender)[:, None]).reshape(-1)
    per_tap = outer // tap_senders
    a_tap = (np.arange(tap_senders)[None, :] * per_tap + np.arange(per_tap)[:, None]).reshape(-1)
    b = np.arange(LANES)

    def angles(a):
        return 2.0 * np.pi * ((4 * k1[:, None] + 1) * a[None, :] % (4 * outer)) / (4 * outer)

    def forward(a):
        angle = angles(a)
        return high_low(np.concatenate((np.cos(angle), -np.sin(angle)), axis=0))

    twist = 2.0 * np.pi * ((4 * k1[:, None] + 1) * b[None, :] % (4 * length)) / (4 * length)
    inner = 2.0 * np.pi * (b[:, None] * b[None, :] % LANES) / LANES
    cos, sin = np.cos(inner), np.sin(inner)
    back = angles(a_tap).T
    return dict(
        signal=forward(a_signal),
        taps=forward(a_tap),
        twist=np.stack((np.cos(twist), -np.sin(twist))).astype(np.float32),
        inner=high_low(np.block([[cos, -sin], [sin, cos]])),
        inner_back=high_low(np.block([[cos, sin], [-sin, cos]])),
        back=high_low(np.concatenate((np.cos(back), -np.sin(back)), axis=1) / length),
    )


def table_dot(table_ref, right):
    return jnp.dot(table_ref[0], right, preferred_element_type=jnp.float32) + jnp.dot(
        table_ref[1], right, preferred_element_type=jnp.float32
    )


def dot_table(left, table_ref):
    return jnp.dot(left, table_ref[0], preferred_element_type=jnp.float32) + jnp.dot(
        left, table_ref[1], preferred_element_type=jnp.float32
    )


def spread(source_ref, spread_ref):
    rows = spread_ref.shape[1]
    for j in range(spread_ref.shape[0]):
        part = source_ref[:, :, j * LANES : (j + 1) * LANES]
        spread_ref[j] = part.reshape(rows, LANES).astype(jnp.float32)


def channel_rows(spread_ref, channel, channels):
    senders = spread_ref.shape[1] // channels
    pair = []
    for c in (channel, channel + 1):
        parts = [spread_ref[j, pl.ds(c, senders, stride=channels), :] for j in range(spread_ref.shape[0])]
        pair.append(jnp.concatenate(parts, axis=0).astype(jnp.bfloat16))
    return jnp.concatenate(pair, axis=1)


def spectra_of(pairs, outer_ref, twist_ref, inner_ref):
    outer = twist_ref.shape[1]
    turned = []
    for rows in pairs:
        section = table_dot(outer_ref, rows)
        for lane in (0, LANES):
            real, imag = section[:outer, lane : lane + LANES], section[outer:, lane : lane + LANES]
            turned_real = real * twist_ref[0] - imag * twist_ref[1]
            turned_imag = real * twist_ref[1] + imag * twist_ref[0]
            turned.append(jnp.concatenate((turned_real.astype(jnp.bfloat16), turned_imag.astype(jnp.bfloat16)), axis=1))
    return dot_table(jnp.concatenate(turned, axis=0), inner_ref)


def taps_kernel(taps_ref, outer_ref, twist_ref, inner_ref, out_ref, spread_ref):
    step = pl.program_id(0)
    channels = taps_ref.shape[1]

    @pl.when(step == 0)
    def _():
        spread(taps_ref, spread_ref)

    first = step * 2 * PAIRS
    pairs = [channel_rows(spread_ref, first + 2 * pair, channels) for pair in range(PAIRS)]
    out_ref[...] = spectra_of(pairs, outer_ref, twist_ref, inner_ref)


def conv_kernel(
    signal_ref, taps_ref, outer_ref, twist_ref, inner_ref, inner_back_ref, back_ref, out_ref, spread_ref, result_ref
):
    step = pl.program_id(0)
    channels = signal_ref.shape[1]
    receivers = out_ref.shape[0]
    outer = twist_ref.shape[1]

    @pl.when(step == 0)
    def _():
        spread(signal_ref, spread_ref)

    first = step * 2 * PAIRS
    pairs = [channel_rows(spread_ref, first + 2 * pair, channels) for pair in range(PAIRS)]
    signal = spectra_of(pairs, outer_ref, twist_ref, inner_ref)
    sig_real, sig_imag = signal[:, :LANES], signal[:, LANES:]
    tap_real, tap_imag = taps_ref[:, :LANES], taps_ref[:, LANES:]
    prod_real = sig_real * tap_real - sig_imag * tap_imag
    prod_imag = sig_real * tap_imag + sig_imag * tap_real
    prod = jnp.concatenate((prod_real.astype(jnp.bfloat16), prod_imag.astype(jnp.bfloat16)), axis=1)
    turned = dot_table(prod, inner_back_ref)
    for pair in range(PAIRS):
        channel = first + 2 * pair
        both = []
        for row in (2 * pair * outer, (2 * pair + 1) * outer):
            real, imag = turned[row : row + outer, :LANES], turned[row : row + outer, LANES:]
            back_real = real * twist_ref[0] + imag * twist_ref[1]
            back_imag = imag * twist_ref[0] - real * twist_ref[1]
            both.append(jnp.concatenate((back_real.astype(jnp.bfloat16), back_imag.astype(jnp.bfloat16)), axis=0))
        rows = table_dot(back_ref, jnp.concatenate(both, axis=1))
        for n in range(2):
            for j in range(result_ref.shape[0]):
                part = rows[j * receivers : (j + 1) * receivers, n * LANES : (n + 1) * LANES]
                result_ref[j, pl.ds(channel + n, receivers, stride=channels), :] = part

    @pl.when(step == pl.num_programs(0) - 1)
    def _():
        for j in range(result_ref.shape[0]):
            part = result_ref[j].reshape(receivers, channels, LANES)
            out_ref[:, :, j * LANES : (j + 1) * LANES] = part.astype(jnp.bfloat16)


def whole(array):
    return pl.BlockSpec(array.shape, lambda i: (0,) * array.ndim)


def transform_taps(taps, tables):
    senders, channels, rows = taps.shape
    outer = tables["twist"].shape[1]
    operands = (taps, tables["taps"], tables["twist"], tables["inner"])
    return pl.pallas_call(
        taps_kernel,
        name="taps_spectrum",
        grid=(channels // (2 * PAIRS),),
        in_specs=[whole(x) for x in operands],
        out_specs=pl.BlockSpec((PAIRS * 2 * outer, 2 * LANES), lambda i: (i, 0)),
        out_shape=jax.ShapeDtypeStruct((channels * outer, 2 * LANES), jnp.float32),
        scratch_shapes=[pltpu.VMEM((rows // LANES, senders * channels, LANES), jnp.float32)],
        compiler_params=pltpu.CompilerParams(vmem_limit_bytes=VMEM_LIMIT),
        cost_estimate=pl.CostEstimate(flops=5 * 10**9, bytes_accessed=4 * 2**20, transcendentals=0),
    )(*operands)


def convolve(signal, spectra, tables, receivers):
    senders, channels, rows = signal.shape
    out_rows = senders * rows // receivers
    outer = tables["twist"].shape[1]
    operands = [tables[n] for n in ("signal", "twist", "inner", "inner_back", "back")]
    return pl.pallas_call(
        conv_kernel,
        name="convolution",
        grid=(channels // (2 * PAIRS),),
        in_specs=[whole(signal), pl.BlockSpec((PAIRS * 2 * outer, 2 * LANES), lambda i: (i, 0))]
        + [whole(x) for x in operands],
        out_specs=pl.BlockSpec((receivers, channels, out_rows), lambda i: (0, 0, 0)),
        out_shape=jax.ShapeDtypeStruct((receivers, channels, out_rows), jnp.bfloat16),
        scratch_shapes=[
            pltpu.VMEM((rows // LANES, senders * channels, LANES), jnp.float32),
            pltpu.VMEM((out_rows // LANES, receivers * channels, LANES), jnp.float32),
        ],
        compiler_params=pltpu.CompilerParams(vmem_limit_bytes=VMEM_LIMIT),
        cost_estimate=pl.CostEstimate(flops=7 * 10**9, bytes_accessed=5 * 2**20, transcendentals=0),
    )(signal, spectra, *operands)


def assemble_kernel(x_ref, *rest):
    pieces, (out, held, in_sems, out_sems) = rest[:X_SIZE], rest[X_SIZE:]
    arriving = [pltpu.make_async_copy(pieces[k], held.at[k], in_sems.at[k]) for k in range(X_SIZE)]
    for copy in arriving:
        copy.start()
    leaving = []
    for k, copy in enumerate(arriving):
        column = pl.multiple_of(lax.rem(x_ref[0] + X_SIZE - k, X_SIZE) * HEAD_DIM, HEAD_DIM)
        copy.wait()
        out_copy = pltpu.make_async_copy(held.at[k], out.at[:, pl.ds(column, HEAD_DIM)], out_sems.at[k])
        out_copy.start()
        leaving.append(out_copy)
    for copy in leaving:
        copy.wait()


def assembled(x_index, pieces):
    rows = pieces[0].shape[0]
    anywhere = pl.BlockSpec(memory_space=pl.ANY)
    return pl.pallas_call(
        assemble_kernel,
        name="assemble",
        in_specs=[pl.BlockSpec(memory_space=pltpu.SMEM)] + [anywhere] * X_SIZE,
        out_specs=anywhere,
        out_shape=jax.ShapeDtypeStruct((rows, X_SIZE * HEAD_DIM), jnp.bfloat16),
        scratch_shapes=[
            pltpu.VMEM((X_SIZE, rows, HEAD_DIM), jnp.bfloat16),
            pltpu.SemaphoreType.DMA((X_SIZE,)),
            pltpu.SemaphoreType.DMA((X_SIZE,)),
        ],
        cost_estimate=pl.CostEstimate(flops=2 * 10**9, bytes_accessed=2**20, transcendentals=0),
    )(x_index, *pieces)


def finish_kernel(mixed_ref, gate_ref, hyena_ref):
    mixed = mixed_ref[...].reshape(HEAD_DIM, mixed_ref.shape[3]).T
    hyena_ref[...] = (gate_ref[...].astype(jnp.float32) * mixed.astype(jnp.float32)).astype(jnp.bfloat16)


def finish(returned, out_gate):
    rows, channels = out_gate.shape
    z_size = returned.shape[0] // X_SIZE
    returned = returned.reshape(z_size, X_SIZE, returned.shape[1], rows)
    by_columns = pl.BlockSpec((rows, HEAD_DIM), lambda i: (0, i))
    return pl.pallas_call(
        finish_kernel,
        name="finish",
        grid=(channels // HEAD_DIM,),
        in_specs=[pl.BlockSpec((z_size, 1, returned.shape[2], rows), lambda i: (0, i, 0, 0)), by_columns],
        out_specs=by_columns,
        out_shape=jax.ShapeDtypeStruct((rows, channels), jnp.bfloat16),
        compiler_params=pltpu.CompilerParams(vmem_limit_bytes=16 * 2**20),
    )(returned, out_gate)


def body(queries, key_rows, values, doc_lengths, in_gate, out_gate, filter_taps):
    row_count, channels = queries.shape
    ctx = lax.axis_size("ctx")
    z_size = ctx // X_SIZE
    group_rows = X_SIZE * row_count
    per_device = channels // ctx
    z_groups = [[z * X_SIZE + x for z in range(z_size)] for x in range(X_SIZE)]
    tables = transform_tables(row_count * ctx, z_size, ctx)
    me = lax.axis_index("ctx").astype(jnp.int32)
    x_index = lax.rem(me, X_SIZE).reshape(1)

    def exchanged(x, groups=None):
        return lax.all_to_all(x, "ctx", split_axis=0, concat_axis=0, tiled=True, axis_index_groups=groups)

    def along_x(piece, k):
        pairs = [(z * X_SIZE + x, z * X_SIZE + (x + k) % X_SIZE) for z in range(z_size) for x in range(X_SIZE)]
        return lax.ppermute(piece, "ctx", pairs)

    def along_z(piece, k):
        pairs = [(i, i + X_SIZE) for i in range(ctx - X_SIZE) if i % X_SIZE != k]
        return lax.ppermute(piece, "ctx", pairs)

    def arrived(pieces):
        moved = {k: along_x(pieces[k], k) for k in NEAR_FIRST[1:]}
        return [pieces[0]] + [moved[k] for k in range(1, X_SIZE)]

    taps = filter_taps.astype(jnp.bfloat16).reshape(X_SIZE, z_size, per_device, row_count)
    taps = taps.transpose(1, 0, 2, 3).reshape(ctx, per_device, row_count)
    pieces = pieces_of(x_index, key_rows, values)
    own = arrived(pieces)
    moved = {k: along_z(own[k], k) for k in NEAR_FIRST}
    before = [moved[k] for k in range(X_SIZE)]
    _, queries, in_gate = lax.optimization_barrier((pieces[0], queries, in_gate))
    asked = pieces_of(x_index, queries, in_gate)
    both = lax.optimization_barrier((*own, *asked))
    own, asked = list(both[:X_SIZE]), list(both[X_SIZE:])
    taps, asked[0] = lax.optimization_barrier((taps, asked[0]))
    asked = arrived(asked)
    taps = exchanged(taps)

    group_first = (me // X_SIZE) * group_rows
    positions = group_first + jnp.arange(group_rows, dtype=jnp.int32)
    start = document_starts(positions, doc_lengths) - (group_first - group_rows)

    attended, gated = attention(x_index, own, before, asked, start)
    gated, taps = lax.optimization_barrier((gated, taps))
    signal = exchanged(gated.reshape(z_size, per_device, group_rows), z_groups)
    spectra = transform_taps(taps, tables)
    spectra, attended = lax.optimization_barrier((spectra, attended))
    attended = arrived([attended[k] for k in range(X_SIZE)])
    mixed = convolve(signal, spectra, tables, ctx)
    mixed, *attended = lax.optimization_barrier((mixed, *attended))
    returned = exchanged(mixed)
    return assembled(x_index, attended), finish(returned, out_gate)


def solution(mesh):
    return jax.shard_map(
        body,
        mesh=mesh,
        in_specs=(
            P(("dp", "ctx"), "tp"),
            P(("dp", "ctx"), "tp"),
            P(("dp", "ctx"), "tp"),
            P("dp"),
            P(("dp", "ctx"), "tp"),
            P(("dp", "ctx"), "tp"),
            P(("dp", "tp"), "ctx"),
        ),
        out_specs=(P(("dp", "ctx"), "tp"), P(("dp", "ctx"), "tp")),
        check_vma=False,
    )
```

```python
import functools
import math

import jax
import jax.numpy as jnp
import ml_dtypes
import numpy as np
from jax import lax
from jax.experimental import pallas as pl
from jax.experimental.pallas import tpu as pltpu
from jax.sharding import PartitionSpec as P

HEAD_DIM = 128
X_SIZE = 4
NEAR_FIRST = (0, 1, 3, 2)
Q_BLOCK = 768
K_BLOCK = 384
LANES = 128
VMEM_LIMIT = 63 * 2**20
PAIRS = 4
masked_score = -1e30


def document_starts(positions, doc_lengths):
    order = jnp.arange(doc_lengths.shape[0], dtype=jnp.int32)
    before = order[:, None] < order[None, :]
    starts = jnp.sum(jnp.where(before, doc_lengths[:, None], 0), axis=0)
    inside = starts[None, :] <= positions[:, None]
    return jnp.max(jnp.where(inside, starts[None, :], 0), axis=1)


def pieces_kernel(x_ref, first_ref, second_ref, *rest):
    outs, (held, in_sems, out_sems) = rest[:X_SIZE], rest[X_SIZE:]
    arriving, leaving = [], []
    for k in range(X_SIZE):
        column = pl.multiple_of(lax.rem(x_ref[0] + k, X_SIZE) * HEAD_DIM, HEAD_DIM)
        for which, ref in enumerate((first_ref, second_ref)):
            copy = pltpu.make_async_copy(ref.at[:, pl.ds(column, HEAD_DIM)], held.at[k, which], in_sems.at[k, which])
            copy.start()
            arriving.append((k, which, copy))
    for k, which, copy in arriving:
        copy.wait()
        out = pltpu.make_async_copy(held.at[k, which], outs[k].at[which], out_sems.at[k, which])
        out.start()
        leaving.append(out)
    for out in leaving:
        out.wait()


def pieces_of(x_index, first, second):
    rows = first.shape[0]
    anywhere = pl.BlockSpec(memory_space=pl.ANY)
    return pl.pallas_call(
        pieces_kernel,
        name="pieces",
        in_specs=[pl.BlockSpec(memory_space=pltpu.SMEM), anywhere, anywhere],
        out_specs=[anywhere] * X_SIZE,
        out_shape=[jax.ShapeDtypeStruct((2, rows, HEAD_DIM), jnp.bfloat16)] * X_SIZE,
        scratch_shapes=[
            pltpu.VMEM((X_SIZE, 2, rows, HEAD_DIM), jnp.bfloat16),
            pltpu.SemaphoreType.DMA((X_SIZE, 2)),
            pltpu.SemaphoreType.DMA((X_SIZE, 2)),
        ],
    )(x_index, first, second)


def attention_kernel(lo_ref, mid_ref, x_ref, start_ref, *rest):
    own, before, asked = rest[:X_SIZE], rest[X_SIZE : 2 * X_SIZE], rest[2 * X_SIZE : 3 * X_SIZE]
    out_ref, gated_ref, keys, values, values_t, queries_all, gate_all, weighted_ref, sems = rest[3 * X_SIZE :]
    step = pl.program_id(0)
    group = queries_all.shape[0]
    piece = group // X_SIZE
    group_blocks = group // K_BLOCK
    piece_blocks = piece // K_BLOCK

    def copies_of(k, chosen, sources):
        at = pl.multiple_of(lax.rem(x_ref[0] + X_SIZE - k, X_SIZE) * piece, piece)
        early, late = pl.ds(at, piece), pl.ds(at + group, piece)
        targets = (keys.at[early], values.at[early], keys.at[late], values.at[late], queries_all.at[early], gate_all.at[early])
        return [pltpu.make_async_copy(sources[n // 2].at[n % 2], targets[n], sems.at[k, n]) for n in chosen]

    def reached(k):
        position = lax.rem(x_ref[0] + X_SIZE - k, X_SIZE)
        return jnp.logical_and(position > 0, (position + 1) * piece_blocks > lo_ref[0])

    def turn(block, _):
        rows = values[pl.ds(pl.multiple_of(block * K_BLOCK, K_BLOCK), K_BLOCK)]
        values_t[block] = rows.T
        return 0

    @pl.when(step == 0)
    def _():
        for k in range(X_SIZE):
            sources = (before[k], own[k], asked[k])

            @pl.when(reached(k))
            def _():
                for copy in copies_of(k, (0, 1), sources):
                    copy.start()

            for copy in copies_of(k, (2, 3, 4, 5), sources):
                copy.start()
        for k in range(X_SIZE):

            @pl.when(reached(k))
            def _():
                for copy in copies_of(k, (0, 1), (before[k], own[k], asked[k])):
                    copy.wait()

        lax.fori_loop(lo_ref[0], group_blocks, turn, 0)

    now = lax.rem(x_ref[0] + X_SIZE - step, X_SIZE)
    for copy in copies_of(now, (2, 3, 4, 5), (before[0], own[0], asked[0])):
        copy.wait()
    first = group + step * Q_BLOCK
    diagonal = first // K_BLOCK
    last = (first + Q_BLOCK - 1) // K_BLOCK
    lax.fori_loop(diagonal, last + 1, turn, 0)

    here = pl.ds(pl.multiple_of(step * Q_BLOCK, Q_BLOCK), Q_BLOCK)
    queries = queries_all[here].T
    start = start_ref[0]
    query_index = first + lax.broadcasted_iota(jnp.int32, (1, Q_BLOCK), 1)
    key_offset = lax.broadcasted_iota(jnp.int32, (K_BLOCK, 1), 0)
    factor = math.log2(math.e) / math.sqrt(HEAD_DIM)
    weighted_ref[...] = jnp.zeros_like(weighted_ref)

    def visit(kind, block, carried):
        top, total = carried
        key_rows = keys[pl.ds(pl.multiple_of(block * K_BLOCK, K_BLOCK), K_BLOCK)]
        scores = jnp.dot(key_rows, queries, preferred_element_type=jnp.float32) * factor
        index = block * K_BLOCK + key_offset
        if kind == "before":
            scores = jnp.where(index >= start, scores, masked_score)
        if kind == "diagonal":
            scores = jnp.where((index >= start) & (index <= query_index), scores, masked_score)
        new_top = jnp.maximum(top, jnp.max(scores, axis=0, keepdims=True))
        rescale = jnp.exp2(top - new_top)
        weight = jnp.exp2(scores - new_top)
        total = total * rescale + jnp.sum(weight, axis=0, keepdims=True)
        weighted_ref[...] = weighted_ref[...] * rescale + jnp.dot(
            values_t[block], weight.astype(jnp.bfloat16), preferred_element_type=jnp.float32
        )
        return new_top, total

    middle = jnp.minimum(mid_ref[step], diagonal)
    carried = (
        jnp.full((1, Q_BLOCK), masked_score, jnp.float32),
        jnp.zeros((1, Q_BLOCK), jnp.float32),
    )
    carried = lax.fori_loop(lo_ref[step], middle, functools.partial(visit, "before"), carried)
    carried = lax.fori_loop(middle, diagonal, functools.partial(visit, "inside"), carried)
    _, total = lax.fori_loop(diagonal, last + 1, functools.partial(visit, "diagonal"), carried)
    rounded = (weighted_ref[...] * (1.0 / total)).astype(jnp.bfloat16)
    out_ref[0] = rounded.T
    gated = rounded.astype(jnp.float32) * gate_all[here].T.astype(jnp.float32)
    gated_ref[...] = gated.astype(jnp.bfloat16)


def attention(x_index, own, before, asked, start):
    rows = X_SIZE * own[0].shape[1]
    steps = rows // Q_BLOCK
    lo = start[::Q_BLOCK] // K_BLOCK
    middle = start[Q_BLOCK - 1 :: Q_BLOCK] // K_BLOCK + 1
    anywhere = pl.BlockSpec(memory_space=pl.ANY)
    return pl.pallas_call(
        attention_kernel,
        name="attention",
        grid_spec=pltpu.PrefetchScalarGridSpec(
            num_scalar_prefetch=3,
            grid=(steps,),
            in_specs=[pl.BlockSpec((1, 1, Q_BLOCK), lambda i, *_: (i, 0, 0))] + [anywhere] * (3 * X_SIZE),
            out_specs=[
                pl.BlockSpec((1, Q_BLOCK, HEAD_DIM), lambda i, lo, mid, x: (lax.rem(i - x[0] + X_SIZE, X_SIZE), 0, 0)),
                pl.BlockSpec((HEAD_DIM, Q_BLOCK), lambda i, *_: (0, i)),
            ],
            scratch_shapes=[
                pltpu.VMEM((2 * rows, HEAD_DIM), jnp.bfloat16),
                pltpu.VMEM((2 * rows, HEAD_DIM), jnp.bfloat16),
                pltpu.VMEM((2 * rows // K_BLOCK, HEAD_DIM, K_BLOCK), jnp.bfloat16),
                pltpu.VMEM((rows, HEAD_DIM), jnp.bfloat16),
                pltpu.VMEM((rows, HEAD_DIM), jnp.bfloat16),
                pltpu.VMEM((HEAD_DIM, Q_BLOCK), jnp.float32),
                pltpu.SemaphoreType.DMA((X_SIZE, 6)),
            ],
        ),
        out_shape=[
            jax.ShapeDtypeStruct((X_SIZE, rows // X_SIZE, HEAD_DIM), jnp.bfloat16),
            jax.ShapeDtypeStruct((HEAD_DIM, rows), jnp.bfloat16),
        ],
        compiler_params=pltpu.CompilerParams(vmem_limit_bytes=VMEM_LIMIT),
        cost_estimate=pl.CostEstimate(
            flops=16 * 10**9, bytes_accessed=10 * rows * HEAD_DIM, transcendentals=rows * 1536
        ),
    )(lo, middle, x_index, start.reshape(steps, 1, Q_BLOCK), *own, *before, *asked)


def high_low(table):
    high = table.astype(np.float32).astype(ml_dtypes.bfloat16)
    low = (table - high.astype(np.float64)).astype(np.float32).astype(ml_dtypes.bfloat16)
    return np.stack((high, low))


def transform_tables(length, senders, tap_senders):
    outer = length // LANES
    k1 = np.arange(outer)
    per_sender = outer // senders
    a_signal = (np.arange(senders)[None, :] * per_sender + np.arange(per_sender)[:, None]).reshape(-1)
    per_tap = outer // tap_senders
    a_tap = (np.arange(tap_senders)[None, :] * per_tap + np.arange(per_tap)[:, None]).reshape(-1)
    b = np.arange(LANES)

    def angles(a):
        return 2.0 * np.pi * ((4 * k1[:, None] + 1) * a[None, :] % (4 * outer)) / (4 * outer)

    def forward(a):
        angle = angles(a)
        return high_low(np.concatenate((np.cos(angle), -np.sin(angle)), axis=0))

    twist = 2.0 * np.pi * ((4 * k1[:, None] + 1) * b[None, :] % (4 * length)) / (4 * length)
    inner = 2.0 * np.pi * (b[:, None] * b[None, :] % LANES) / LANES
    cos, sin = np.cos(inner), np.sin(inner)
    back = angles(a_tap).T
    return dict(
        signal=forward(a_signal),
        taps=forward(a_tap),
        twist=np.stack((np.cos(twist), -np.sin(twist))).astype(np.float32),
        inner=high_low(np.block([[cos, -sin], [sin, cos]])),
        inner_back=high_low(np.block([[cos, sin], [-sin, cos]])),
        back=high_low(np.concatenate((np.cos(back), -np.sin(back)), axis=1) / length),
    )


def table_dot(table_ref, right):
    return jnp.dot(table_ref[0], right, preferred_element_type=jnp.float32) + jnp.dot(
        table_ref[1], right, preferred_element_type=jnp.float32
    )


def dot_table(left, table_ref):
    return jnp.dot(left, table_ref[0], preferred_element_type=jnp.float32) + jnp.dot(
        left, table_ref[1], preferred_element_type=jnp.float32
    )


def spread(source_ref, spread_ref):
    rows = spread_ref.shape[1]
    for j in range(spread_ref.shape[0]):
        part = source_ref[:, :, j * LANES : (j + 1) * LANES]
        spread_ref[j] = part.reshape(rows, LANES).astype(jnp.float32)


def channel_rows(spread_ref, channel, channels):
    senders = spread_ref.shape[1] // channels
    pair = []
    for c in (channel, channel + 1):
        parts = [spread_ref[j, pl.ds(c, senders, stride=channels), :] for j in range(spread_ref.shape[0])]
        pair.append(jnp.concatenate(parts, axis=0).astype(jnp.bfloat16))
    return jnp.concatenate(pair, axis=1)


def spectra_of(pairs, outer_ref, twist_ref, inner_ref):
    outer = twist_ref.shape[1]
    turned = []
    for rows in pairs:
        section = table_dot(outer_ref, rows)
        for lane in (0, LANES):
            real, imag = section[:outer, lane : lane + LANES], section[outer:, lane : lane + LANES]
            turned_real = real * twist_ref[0] - imag * twist_ref[1]
            turned_imag = real * twist_ref[1] + imag * twist_ref[0]
            turned.append(jnp.concatenate((turned_real.astype(jnp.bfloat16), turned_imag.astype(jnp.bfloat16)), axis=1))
    return dot_table(jnp.concatenate(turned, axis=0), inner_ref)


def taps_kernel(taps_ref, outer_ref, twist_ref, inner_ref, out_ref, spread_ref):
    step = pl.program_id(0)
    channels = taps_ref.shape[1]

    @pl.when(step == 0)
    def _():
        spread(taps_ref, spread_ref)

    first = step * 2 * PAIRS
    pairs = [channel_rows(spread_ref, first + 2 * pair, channels) for pair in range(PAIRS)]
    out_ref[...] = spectra_of(pairs, outer_ref, twist_ref, inner_ref)


def conv_kernel(
    signal_ref, taps_ref, outer_ref, twist_ref, inner_ref, inner_back_ref, back_ref, out_ref, spread_ref, result_ref
):
    step = pl.program_id(0)
    channels = signal_ref.shape[1]
    receivers = out_ref.shape[0]
    outer = twist_ref.shape[1]

    @pl.when(step == 0)
    def _():
        spread(signal_ref, spread_ref)

    first = step * 2 * PAIRS
    pairs = [channel_rows(spread_ref, first + 2 * pair, channels) for pair in range(PAIRS)]
    signal = spectra_of(pairs, outer_ref, twist_ref, inner_ref)
    sig_real, sig_imag = signal[:, :LANES], signal[:, LANES:]
    tap_real, tap_imag = taps_ref[:, :LANES], taps_ref[:, LANES:]
    prod_real = sig_real * tap_real - sig_imag * tap_imag
    prod_imag = sig_real * tap_imag + sig_imag * tap_real
    prod = jnp.concatenate((prod_real.astype(jnp.bfloat16), prod_imag.astype(jnp.bfloat16)), axis=1)
    turned = dot_table(prod, inner_back_ref)
    for pair in range(PAIRS):
        channel = first + 2 * pair
        both = []
        for row in (2 * pair * outer, (2 * pair + 1) * outer):
            real, imag = turned[row : row + outer, :LANES], turned[row : row + outer, LANES:]
            back_real = real * twist_ref[0] + imag * twist_ref[1]
            back_imag = imag * twist_ref[0] - real * twist_ref[1]
            both.append(jnp.concatenate((back_real.astype(jnp.bfloat16), back_imag.astype(jnp.bfloat16)), axis=0))
        rows = table_dot(back_ref, jnp.concatenate(both, axis=1))
        for n in range(2):
            for j in range(result_ref.shape[0]):
                part = rows[j * receivers : (j + 1) * receivers, n * LANES : (n + 1) * LANES]
                result_ref[j, pl.ds(channel + n, receivers, stride=channels), :] = part

    @pl.when(step == pl.num_programs(0) - 1)
    def _():
        for j in range(result_ref.shape[0]):
            part = result_ref[j].reshape(receivers, channels, LANES)
            out_ref[:, :, j * LANES : (j + 1) * LANES] = part.astype(jnp.bfloat16)


def whole(array):
    return pl.BlockSpec(array.shape, lambda i: (0,) * array.ndim)


def transform_taps(taps, tables):
    senders, channels, rows = taps.shape
    outer = tables["twist"].shape[1]
    operands = (taps, tables["taps"], tables["twist"], tables["inner"])
    return pl.pallas_call(
        taps_kernel,
        name="taps_spectrum",
        grid=(channels // (2 * PAIRS),),
        in_specs=[whole(x) for x in operands],
        out_specs=pl.BlockSpec((PAIRS * 2 * outer, 2 * LANES), lambda i: (i, 0)),
        out_shape=jax.ShapeDtypeStruct((channels * outer, 2 * LANES), jnp.float32),
        scratch_shapes=[pltpu.VMEM((rows // LANES, senders * channels, LANES), jnp.float32)],
        compiler_params=pltpu.CompilerParams(vmem_limit_bytes=VMEM_LIMIT),
        cost_estimate=pl.CostEstimate(flops=5 * 10**9, bytes_accessed=4 * 2**20, transcendentals=0),
    )(*operands)


def convolve(signal, spectra, tables, receivers):
    senders, channels, rows = signal.shape
    out_rows = senders * rows // receivers
    outer = tables["twist"].shape[1]
    operands = [tables[n] for n in ("signal", "twist", "inner", "inner_back", "back")]
    return pl.pallas_call(
        conv_kernel,
        name="convolution",
        grid=(channels // (2 * PAIRS),),
        in_specs=[whole(signal), pl.BlockSpec((PAIRS * 2 * outer, 2 * LANES), lambda i: (i, 0))]
        + [whole(x) for x in operands],
        out_specs=pl.BlockSpec((receivers, channels, out_rows), lambda i: (0, 0, 0)),
        out_shape=jax.ShapeDtypeStruct((receivers, channels, out_rows), jnp.bfloat16),
        scratch_shapes=[
            pltpu.VMEM((rows // LANES, senders * channels, LANES), jnp.float32),
            pltpu.VMEM((out_rows // LANES, receivers * channels, LANES), jnp.float32),
        ],
        compiler_params=pltpu.CompilerParams(vmem_limit_bytes=VMEM_LIMIT),
        cost_estimate=pl.CostEstimate(flops=7 * 10**9, bytes_accessed=5 * 2**20, transcendentals=0),
    )(signal, spectra, *operands)


def assemble_kernel(x_ref, *rest):
    pieces, (out, held, in_sems, out_sems) = rest[:X_SIZE], rest[X_SIZE:]
    arriving = [pltpu.make_async_copy(pieces[k], held.at[k], in_sems.at[k]) for k in range(X_SIZE)]
    for copy in arriving:
        copy.start()
    leaving = []
    for k, copy in enumerate(arriving):
        column = pl.multiple_of(lax.rem(x_ref[0] + X_SIZE - k, X_SIZE) * HEAD_DIM, HEAD_DIM)
        copy.wait()
        out_copy = pltpu.make_async_copy(held.at[k], out.at[:, pl.ds(column, HEAD_DIM)], out_sems.at[k])
        out_copy.start()
        leaving.append(out_copy)
    for copy in leaving:
        copy.wait()


def assembled(x_index, pieces):
    rows = pieces[0].shape[0]
    anywhere = pl.BlockSpec(memory_space=pl.ANY)
    return pl.pallas_call(
        assemble_kernel,
        name="assemble",
        in_specs=[pl.BlockSpec(memory_space=pltpu.SMEM)] + [anywhere] * X_SIZE,
        out_specs=anywhere,
        out_shape=jax.ShapeDtypeStruct((rows, X_SIZE * HEAD_DIM), jnp.bfloat16),
        scratch_shapes=[
            pltpu.VMEM((X_SIZE, rows, HEAD_DIM), jnp.bfloat16),
            pltpu.SemaphoreType.DMA((X_SIZE,)),
            pltpu.SemaphoreType.DMA((X_SIZE,)),
        ],
        cost_estimate=pl.CostEstimate(flops=2 * 10**9, bytes_accessed=2**20, transcendentals=0),
    )(x_index, *pieces)


def finish_kernel(mixed_ref, gate_ref, hyena_ref):
    mixed = mixed_ref[...].reshape(HEAD_DIM, mixed_ref.shape[3]).T
    hyena_ref[...] = (gate_ref[...].astype(jnp.float32) * mixed.astype(jnp.float32)).astype(jnp.bfloat16)


def finish(returned, out_gate):
    rows, channels = out_gate.shape
    z_size = returned.shape[0] // X_SIZE
    returned = returned.reshape(z_size, X_SIZE, returned.shape[1], rows)
    by_columns = pl.BlockSpec((rows, HEAD_DIM), lambda i: (0, i))
    return pl.pallas_call(
        finish_kernel,
        name="finish",
        grid=(channels // HEAD_DIM,),
        in_specs=[pl.BlockSpec((z_size, 1, returned.shape[2], rows), lambda i: (0, i, 0, 0)), by_columns],
        out_specs=by_columns,
        out_shape=jax.ShapeDtypeStruct((rows, channels), jnp.bfloat16),
        compiler_params=pltpu.CompilerParams(vmem_limit_bytes=16 * 2**20),
    )(returned, out_gate)


def body(queries, key_rows, values, doc_lengths, in_gate, out_gate, filter_taps):
    row_count, channels = queries.shape
    ctx = lax.axis_size("ctx")
    z_size = ctx // X_SIZE
    group_rows = X_SIZE * row_count
    per_device = channels // ctx
    z_groups = [[z * X_SIZE + x for z in range(z_size)] for x in range(X_SIZE)]
    tables = transform_tables(row_count * ctx, z_size, ctx)
    me = lax.axis_index("ctx").astype(jnp.int32)
    x_index = lax.rem(me, X_SIZE).reshape(1)

    def exchanged(x, groups=None):
        return lax.all_to_all(x, "ctx", split_axis=0, concat_axis=0, tiled=True, axis_index_groups=groups)

    def along_x(piece, k):
        pairs = [(z * X_SIZE + x, z * X_SIZE + (x + k) % X_SIZE) for z in range(z_size) for x in range(X_SIZE)]
        return lax.ppermute(piece, "ctx", pairs)

    def along_z(piece, k):
        pairs = [(i, i + X_SIZE) for i in range(ctx - X_SIZE) if i % X_SIZE != k]
        return lax.ppermute(piece, "ctx", pairs)

    def arrived(pieces):
        moved = {k: along_x(pieces[k], k) for k in NEAR_FIRST[1:]}
        return [pieces[0]] + [moved[k] for k in range(1, X_SIZE)]

    taps = filter_taps.astype(jnp.bfloat16).reshape(X_SIZE, z_size, per_device, row_count)
    taps = taps.transpose(1, 0, 2, 3).reshape(ctx, per_device, row_count)
    pieces = pieces_of(x_index, key_rows, values)
    own = arrived(pieces)
    moved = {k: along_z(own[k], k) for k in NEAR_FIRST}
    before = [moved[k] for k in range(X_SIZE)]
    _, queries, in_gate = lax.optimization_barrier((pieces[0], queries, in_gate))
    asked = pieces_of(x_index, queries, in_gate)
    both = lax.optimization_barrier((*own, *asked, before[0], before[1]))
    own, asked = list(both[:X_SIZE]), list(both[X_SIZE : 2 * X_SIZE])
    before[0], before[1] = both[2 * X_SIZE :]
    taps, asked[0] = lax.optimization_barrier((taps, asked[0]))
    asked = arrived(asked)
    taps = exchanged(taps)

    group_first = (me // X_SIZE) * group_rows
    positions = group_first + jnp.arange(group_rows, dtype=jnp.int32)
    start = document_starts(positions, doc_lengths) - (group_first - group_rows)

    attended, gated = attention(x_index, own, before, asked, start)
    gated, taps = lax.optimization_barrier((gated, taps))
    signal = exchanged(gated.reshape(z_size, per_device, group_rows), z_groups)
    spectra = transform_taps(taps, tables)
    spectra, attended = lax.optimization_barrier((spectra, attended))
    attended = arrived([attended[k] for k in range(X_SIZE)])
    mixed = convolve(signal, spectra, tables, ctx)
    mixed, *attended = lax.optimization_barrier((mixed, *attended))
    returned = exchanged(mixed)
    return assembled(x_index, attended), finish(returned, out_gate)


def solution(mesh):
    return jax.shard_map(
        body,
        mesh=mesh,
        in_specs=(
            P(("dp", "ctx"), "tp"),
            P(("dp", "ctx"), "tp"),
            P(("dp", "ctx"), "tp"),
            P("dp"),
            P(("dp", "ctx"), "tp"),
            P(("dp", "ctx"), "tp"),
            P(("dp", "tp"), "ctx"),
        ),
        out_specs=(P(("dp", "ctx"), "tp"), P(("dp", "ctx"), "tp")),
        check_vma=False,
    )
```

```python
import functools
import math

import jax
import jax.numpy as jnp
import ml_dtypes
import numpy as np
from jax import lax
from jax.experimental import pallas as pl
from jax.experimental.pallas import tpu as pltpu
from jax.sharding import PartitionSpec as P

HEAD_DIM = 128
X_SIZE = 4
Q_BLOCK = 768
K_BLOCK = 384
LANES = 128
VMEM_LIMIT = 63 * 2**20
PAIRS = 4
masked_score = -1e30


def document_starts(positions, doc_lengths):
    order = jnp.arange(doc_lengths.shape[0], dtype=jnp.int32)
    before = order[:, None] < order[None, :]
    starts = jnp.sum(jnp.where(before, doc_lengths[:, None], 0), axis=0)
    inside = starts[None, :] <= positions[:, None]
    return jnp.max(jnp.where(inside, starts[None, :], 0), axis=1)


def pieces_kernel(x_ref, first_ref, second_ref, *rest):
    outs, (held, in_sems, out_sems) = rest[:X_SIZE], rest[X_SIZE:]
    arriving, leaving = [], []
    for k in range(X_SIZE):
        column = pl.multiple_of(lax.rem(x_ref[0] + k, X_SIZE) * HEAD_DIM, HEAD_DIM)
        for which, ref in enumerate((first_ref, second_ref)):
            copy = pltpu.make_async_copy(ref.at[:, pl.ds(column, HEAD_DIM)], held.at[k, which], in_sems.at[k, which])
            copy.start()
            arriving.append((k, which, copy))
    for k, which, copy in arriving:
        copy.wait()
        out = pltpu.make_async_copy(held.at[k, which], outs[k].at[which], out_sems.at[k, which])
        out.start()
        leaving.append(out)
    for out in leaving:
        out.wait()


def pieces_of(x_index, first, second):
    rows = first.shape[0]
    anywhere = pl.BlockSpec(memory_space=pl.ANY)
    return pl.pallas_call(
        pieces_kernel,
        name="pieces",
        in_specs=[pl.BlockSpec(memory_space=pltpu.SMEM), anywhere, anywhere],
        out_specs=[anywhere] * X_SIZE,
        out_shape=[jax.ShapeDtypeStruct((2, rows, HEAD_DIM), jnp.bfloat16)] * X_SIZE,
        scratch_shapes=[
            pltpu.VMEM((X_SIZE, 2, rows, HEAD_DIM), jnp.bfloat16),
            pltpu.SemaphoreType.DMA((X_SIZE, 2)),
            pltpu.SemaphoreType.DMA((X_SIZE, 2)),
        ],
    )(x_index, first, second)


def attention_kernel(lo_ref, mid_ref, x_ref, start_ref, *rest):
    own, before, asked = rest[:X_SIZE], rest[X_SIZE : 2 * X_SIZE], rest[2 * X_SIZE : 3 * X_SIZE]
    out_ref, gated_ref, keys, values, values_t, queries_all, gate_all, weighted_ref, sems = rest[3 * X_SIZE :]
    step = pl.program_id(0)
    group = queries_all.shape[0]
    piece = group // X_SIZE
    group_blocks = group // K_BLOCK
    piece_blocks = piece // K_BLOCK

    def copies_of(k, chosen, sources):
        at = pl.multiple_of(lax.rem(x_ref[0] + X_SIZE - k, X_SIZE) * piece, piece)
        early, late = pl.ds(at, piece), pl.ds(at + group, piece)
        targets = (keys.at[early], values.at[early], keys.at[late], values.at[late], queries_all.at[early], gate_all.at[early])
        return [pltpu.make_async_copy(sources[n // 2].at[n % 2], targets[n], sems.at[k, n]) for n in chosen]

    def reached(k):
        position = lax.rem(x_ref[0] + X_SIZE - k, X_SIZE)
        return jnp.logical_and(position > 0, (position + 1) * piece_blocks > lo_ref[0])

    def turn(block, _):
        rows = values[pl.ds(pl.multiple_of(block * K_BLOCK, K_BLOCK), K_BLOCK)]
        values_t[block] = rows.T
        return 0

    @pl.when(step == 0)
    def _():
        for k in range(X_SIZE):
            sources = (before[k], own[k], asked[k])

            @pl.when(reached(k))
            def _():
                for copy in copies_of(k, (0, 1), sources):
                    copy.start()

            for copy in copies_of(k, (2, 3, 4, 5), sources):
                copy.start()
        for k in range(X_SIZE):

            @pl.when(reached(k))
            def _():
                for copy in copies_of(k, (0, 1), (before[k], own[k], asked[k])):
                    copy.wait()

        lax.fori_loop(lo_ref[0], group_blocks, turn, 0)

    now = lax.rem(x_ref[0] + X_SIZE - step, X_SIZE)
    for copy in copies_of(now, (2, 3, 4, 5), (before[0], own[0], asked[0])):
        copy.wait()
    first = group + step * Q_BLOCK
    diagonal = first // K_BLOCK
    last = (first + Q_BLOCK - 1) // K_BLOCK
    lax.fori_loop(diagonal, last + 1, turn, 0)

    here = pl.ds(pl.multiple_of(step * Q_BLOCK, Q_BLOCK), Q_BLOCK)
    queries = queries_all[here].T
    start = start_ref[0]
    query_index = first + lax.broadcasted_iota(jnp.int32, (1, Q_BLOCK), 1)
    key_offset = lax.broadcasted_iota(jnp.int32, (K_BLOCK, 1), 0)
    factor = math.log2(math.e) / math.sqrt(HEAD_DIM)
    weighted_ref[...] = jnp.zeros_like(weighted_ref)

    def visit(kind, block, carried):
        top, total = carried
        key_rows = keys[pl.ds(pl.multiple_of(block * K_BLOCK, K_BLOCK), K_BLOCK)]
        scores = jnp.dot(key_rows, queries, preferred_element_type=jnp.float32) * factor
        index = block * K_BLOCK + key_offset
        if kind == "before":
            scores = jnp.where(index >= start, scores, masked_score)
        if kind == "diagonal":
            scores = jnp.where((index >= start) & (index <= query_index), scores, masked_score)
        new_top = jnp.maximum(top, jnp.max(scores, axis=0, keepdims=True))
        rescale = jnp.exp2(top - new_top)
        weight = jnp.exp2(scores - new_top)
        total = total * rescale + jnp.sum(weight, axis=0, keepdims=True)
        weighted_ref[...] = weighted_ref[...] * rescale + jnp.dot(
            values_t[block], weight.astype(jnp.bfloat16), preferred_element_type=jnp.float32
        )
        return new_top, total

    middle = jnp.minimum(mid_ref[step], diagonal)
    carried = (
        jnp.full((1, Q_BLOCK), masked_score, jnp.float32),
        jnp.zeros((1, Q_BLOCK), jnp.float32),
    )
    carried = lax.fori_loop(lo_ref[step], middle, functools.partial(visit, "before"), carried)
    carried = lax.fori_loop(middle, diagonal, functools.partial(visit, "inside"), carried)
    _, total = lax.fori_loop(diagonal, last + 1, functools.partial(visit, "diagonal"), carried)
    rounded = (weighted_ref[...] * (1.0 / total)).astype(jnp.bfloat16)
    out_ref[0] = rounded.T
    gated = rounded.astype(jnp.float32) * gate_all[here].T.astype(jnp.float32)
    gated_ref[...] = gated.astype(jnp.bfloat16)


def attention(x_index, own, before, asked, start):
    rows = X_SIZE * own[0].shape[1]
    steps = rows // Q_BLOCK
    lo = start[::Q_BLOCK] // K_BLOCK
    middle = start[Q_BLOCK - 1 :: Q_BLOCK] // K_BLOCK + 1
    anywhere = pl.BlockSpec(memory_space=pl.ANY)
    return pl.pallas_call(
        attention_kernel,
        name="attention",
        grid_spec=pltpu.PrefetchScalarGridSpec(
            num_scalar_prefetch=3,
            grid=(steps,),
            in_specs=[pl.BlockSpec((1, 1, Q_BLOCK), lambda i, *_: (i, 0, 0))] + [anywhere] * (3 * X_SIZE),
            out_specs=[
                pl.BlockSpec((1, Q_BLOCK, HEAD_DIM), lambda i, lo, mid, x: (lax.rem(i - x[0] + X_SIZE, X_SIZE), 0, 0)),
                pl.BlockSpec((HEAD_DIM, Q_BLOCK), lambda i, *_: (0, i)),
            ],
            scratch_shapes=[
                pltpu.VMEM((2 * rows, HEAD_DIM), jnp.bfloat16),
                pltpu.VMEM((2 * rows, HEAD_DIM), jnp.bfloat16),
                pltpu.VMEM((2 * rows // K_BLOCK, HEAD_DIM, K_BLOCK), jnp.bfloat16),
                pltpu.VMEM((rows, HEAD_DIM), jnp.bfloat16),
                pltpu.VMEM((rows, HEAD_DIM), jnp.bfloat16),
                pltpu.VMEM((HEAD_DIM, Q_BLOCK), jnp.float32),
                pltpu.SemaphoreType.DMA((X_SIZE, 6)),
            ],
        ),
        out_shape=[
            jax.ShapeDtypeStruct((X_SIZE, rows // X_SIZE, HEAD_DIM), jnp.bfloat16),
            jax.ShapeDtypeStruct((HEAD_DIM, rows), jnp.bfloat16),
        ],
        compiler_params=pltpu.CompilerParams(vmem_limit_bytes=VMEM_LIMIT),
        cost_estimate=pl.CostEstimate(
            flops=16 * 10**9, bytes_accessed=10 * rows * HEAD_DIM, transcendentals=rows * 1536
        ),
    )(lo, middle, x_index, start.reshape(steps, 1, Q_BLOCK), *own, *before, *asked)


def high_low(table):
    high = table.astype(np.float32).astype(ml_dtypes.bfloat16)
    low = (table - high.astype(np.float64)).astype(np.float32).astype(ml_dtypes.bfloat16)
    return np.stack((high, low))


def transform_tables(length, senders, tap_senders):
    outer = length // LANES
    k1 = np.arange(outer)
    per_sender = outer // senders
    a_signal = (np.arange(senders)[None, :] * per_sender + np.arange(per_sender)[:, None]).reshape(-1)
    per_tap = outer // tap_senders
    a_tap = (np.arange(tap_senders)[None, :] * per_tap + np.arange(per_tap)[:, None]).reshape(-1)
    b = np.arange(LANES)

    def angles(a):
        return 2.0 * np.pi * ((4 * k1[:, None] + 1) * a[None, :] % (4 * outer)) / (4 * outer)

    def forward(a):
        angle = angles(a)
        return high_low(np.concatenate((np.cos(angle), -np.sin(angle)), axis=0))

    twist = 2.0 * np.pi * ((4 * k1[:, None] + 1) * b[None, :] % (4 * length)) / (4 * length)
    inner = 2.0 * np.pi * (b[:, None] * b[None, :] % LANES) / LANES
    cos, sin = np.cos(inner), np.sin(inner)
    back = angles(a_tap).T
    return dict(
        signal=forward(a_signal),
        taps=forward(a_tap),
        twist=np.stack((np.cos(twist), -np.sin(twist))).astype(np.float32),
        inner=high_low(np.block([[cos, -sin], [sin, cos]])),
        inner_back=high_low(np.block([[cos, sin], [-sin, cos]])),
        back=high_low(np.concatenate((np.cos(back), -np.sin(back)), axis=1) / length),
    )


def table_dot(table_ref, right):
    return jnp.dot(table_ref[0], right, preferred_element_type=jnp.float32) + jnp.dot(
        table_ref[1], right, preferred_element_type=jnp.float32
    )


def dot_table(left, table_ref):
    return jnp.dot(left, table_ref[0], preferred_element_type=jnp.float32) + jnp.dot(
        left, table_ref[1], preferred_element_type=jnp.float32
    )


def spread(source_ref, spread_ref):
    rows = spread_ref.shape[1]
    for j in range(spread_ref.shape[0]):
        part = source_ref[:, :, j * LANES : (j + 1) * LANES]
        spread_ref[j] = part.reshape(rows, LANES).astype(jnp.float32)


def channel_rows(spread_ref, channel, channels):
    senders = spread_ref.shape[1] // channels
    pair = []
    for c in (channel, channel + 1):
        parts = [spread_ref[j, pl.ds(c, senders, stride=channels), :] for j in range(spread_ref.shape[0])]
        pair.append(jnp.concatenate(parts, axis=0).astype(jnp.bfloat16))
    return jnp.concatenate(pair, axis=1)


def spectra_of(pairs, outer_ref, twist_ref, inner_ref):
    outer = twist_ref.shape[1]
    turned = []
    for rows in pairs:
        section = table_dot(outer_ref, rows)
        for lane in (0, LANES):
            real, imag = section[:outer, lane : lane + LANES], section[outer:, lane : lane + LANES]
            turned_real = real * twist_ref[0] - imag * twist_ref[1]
            turned_imag = real * twist_ref[1] + imag * twist_ref[0]
            turned.append(jnp.concatenate((turned_real.astype(jnp.bfloat16), turned_imag.astype(jnp.bfloat16)), axis=1))
    return dot_table(jnp.concatenate(turned, axis=0), inner_ref)


def taps_kernel(taps_ref, outer_ref, twist_ref, inner_ref, out_ref, spread_ref):
    step = pl.program_id(0)
    channels = taps_ref.shape[1]

    @pl.when(step == 0)
    def _():
        spread(taps_ref, spread_ref)

    first = step * 2 * PAIRS
    pairs = [channel_rows(spread_ref, first + 2 * pair, channels) for pair in range(PAIRS)]
    out_ref[...] = spectra_of(pairs, outer_ref, twist_ref, inner_ref)


def conv_kernel(
    signal_ref, taps_ref, outer_ref, twist_ref, inner_ref, inner_back_ref, back_ref, out_ref, spread_ref, result_ref
):
    step = pl.program_id(0)
    channels = signal_ref.shape[1]
    receivers = out_ref.shape[0]
    outer = twist_ref.shape[1]

    @pl.when(step == 0)
    def _():
        spread(signal_ref, spread_ref)

    first = step * 2 * PAIRS
    pairs = [channel_rows(spread_ref, first + 2 * pair, channels) for pair in range(PAIRS)]
    signal = spectra_of(pairs, outer_ref, twist_ref, inner_ref)
    sig_real, sig_imag = signal[:, :LANES], signal[:, LANES:]
    tap_real, tap_imag = taps_ref[:, :LANES], taps_ref[:, LANES:]
    prod_real = sig_real * tap_real - sig_imag * tap_imag
    prod_imag = sig_real * tap_imag + sig_imag * tap_real
    prod = jnp.concatenate((prod_real.astype(jnp.bfloat16), prod_imag.astype(jnp.bfloat16)), axis=1)
    turned = dot_table(prod, inner_back_ref)
    for pair in range(PAIRS):
        channel = first + 2 * pair
        both = []
        for row in (2 * pair * outer, (2 * pair + 1) * outer):
            real, imag = turned[row : row + outer, :LANES], turned[row : row + outer, LANES:]
            back_real = real * twist_ref[0] + imag * twist_ref[1]
            back_imag = imag * twist_ref[0] - real * twist_ref[1]
            both.append(jnp.concatenate((back_real.astype(jnp.bfloat16), back_imag.astype(jnp.bfloat16)), axis=0))
        rows = table_dot(back_ref, jnp.concatenate(both, axis=1))
        for n in range(2):
            for j in range(result_ref.shape[0]):
                part = rows[j * receivers : (j + 1) * receivers, n * LANES : (n + 1) * LANES]
                result_ref[j, pl.ds(channel + n, receivers, stride=channels), :] = part

    @pl.when(step == pl.num_programs(0) - 1)
    def _():
        for j in range(result_ref.shape[0]):
            part = result_ref[j].reshape(receivers, channels, LANES)
            out_ref[:, :, j * LANES : (j + 1) * LANES] = part.astype(jnp.bfloat16)


def whole(array):
    return pl.BlockSpec(array.shape, lambda i: (0,) * array.ndim)


def transform_taps(taps, tables):
    senders, channels, rows = taps.shape
    outer = tables["twist"].shape[1]
    operands = (taps, tables["taps"], tables["twist"], tables["inner"])
    return pl.pallas_call(
        taps_kernel,
        name="taps_spectrum",
        grid=(channels // (2 * PAIRS),),
        in_specs=[whole(x) for x in operands],
        out_specs=pl.BlockSpec((PAIRS * 2 * outer, 2 * LANES), lambda i: (i, 0)),
        out_shape=jax.ShapeDtypeStruct((channels * outer, 2 * LANES), jnp.float32),
        scratch_shapes=[pltpu.VMEM((rows // LANES, senders * channels, LANES), jnp.float32)],
        compiler_params=pltpu.CompilerParams(vmem_limit_bytes=VMEM_LIMIT),
        cost_estimate=pl.CostEstimate(flops=5 * 10**9, bytes_accessed=4 * 2**20, transcendentals=0),
    )(*operands)


def convolve(signal, spectra, tables, receivers):
    senders, channels, rows = signal.shape
    out_rows = senders * rows // receivers
    outer = tables["twist"].shape[1]
    operands = [tables[n] for n in ("signal", "twist", "inner", "inner_back", "back")]
    return pl.pallas_call(
        conv_kernel,
        name="convolution",
        grid=(channels // (2 * PAIRS),),
        in_specs=[whole(signal), pl.BlockSpec((PAIRS * 2 * outer, 2 * LANES), lambda i: (i, 0))]
        + [whole(x) for x in operands],
        out_specs=pl.BlockSpec((receivers, channels, out_rows), lambda i: (0, 0, 0)),
        out_shape=jax.ShapeDtypeStruct((receivers, channels, out_rows), jnp.bfloat16),
        scratch_shapes=[
            pltpu.VMEM((rows // LANES, senders * channels, LANES), jnp.float32),
            pltpu.VMEM((out_rows // LANES, receivers * channels, LANES), jnp.float32),
        ],
        compiler_params=pltpu.CompilerParams(vmem_limit_bytes=VMEM_LIMIT),
        cost_estimate=pl.CostEstimate(flops=7 * 10**9, bytes_accessed=5 * 2**20, transcendentals=0),
    )(signal, spectra, *operands)


def assemble_kernel(x_ref, *rest):
    pieces, (out, held, in_sems, out_sems) = rest[:X_SIZE], rest[X_SIZE:]
    arriving = [pltpu.make_async_copy(pieces[k], held.at[k], in_sems.at[k]) for k in range(X_SIZE)]
    for copy in arriving:
        copy.start()
    leaving = []
    for k, copy in enumerate(arriving):
        column = pl.multiple_of(lax.rem(x_ref[0] + X_SIZE - k, X_SIZE) * HEAD_DIM, HEAD_DIM)
        copy.wait()
        out_copy = pltpu.make_async_copy(held.at[k], out.at[:, pl.ds(column, HEAD_DIM)], out_sems.at[k])
        out_copy.start()
        leaving.append(out_copy)
    for copy in leaving:
        copy.wait()


def assembled(x_index, pieces):
    rows = pieces[0].shape[0]
    anywhere = pl.BlockSpec(memory_space=pl.ANY)
    return pl.pallas_call(
        assemble_kernel,
        name="assemble",
        in_specs=[pl.BlockSpec(memory_space=pltpu.SMEM)] + [anywhere] * X_SIZE,
        out_specs=anywhere,
        out_shape=jax.ShapeDtypeStruct((rows, X_SIZE * HEAD_DIM), jnp.bfloat16),
        scratch_shapes=[
            pltpu.VMEM((X_SIZE, rows, HEAD_DIM), jnp.bfloat16),
            pltpu.SemaphoreType.DMA((X_SIZE,)),
            pltpu.SemaphoreType.DMA((X_SIZE,)),
        ],
        cost_estimate=pl.CostEstimate(flops=2 * 10**9, bytes_accessed=2**20, transcendentals=0),
    )(x_index, *pieces)


def finish_kernel(mixed_ref, gate_ref, hyena_ref):
    mixed = mixed_ref[...].reshape(HEAD_DIM, mixed_ref.shape[3]).T
    hyena_ref[...] = (gate_ref[...].astype(jnp.float32) * mixed.astype(jnp.float32)).astype(jnp.bfloat16)


def finish(returned, out_gate):
    rows, channels = out_gate.shape
    z_size = returned.shape[0] // X_SIZE
    returned = returned.reshape(z_size, X_SIZE, returned.shape[1], rows)
    by_columns = pl.BlockSpec((rows, HEAD_DIM), lambda i: (0, i))
    return pl.pallas_call(
        finish_kernel,
        name="finish",
        grid=(channels // HEAD_DIM,),
        in_specs=[pl.BlockSpec((z_size, 1, returned.shape[2], rows), lambda i: (0, i, 0, 0)), by_columns],
        out_specs=by_columns,
        out_shape=jax.ShapeDtypeStruct((rows, channels), jnp.bfloat16),
        compiler_params=pltpu.CompilerParams(vmem_limit_bytes=16 * 2**20),
    )(returned, out_gate)


def body(queries, key_rows, values, doc_lengths, in_gate, out_gate, filter_taps):
    row_count, channels = queries.shape
    ctx = lax.axis_size("ctx")
    z_size = ctx // X_SIZE
    group_rows = X_SIZE * row_count
    per_device = channels // ctx
    z_groups = [[z * X_SIZE + x for z in range(z_size)] for x in range(X_SIZE)]
    tables = transform_tables(row_count * ctx, z_size, ctx)
    me = lax.axis_index("ctx").astype(jnp.int32)
    x_index = lax.rem(me, X_SIZE).reshape(1)

    def exchanged(x, groups=None):
        return lax.all_to_all(x, "ctx", split_axis=0, concat_axis=0, tiled=True, axis_index_groups=groups)

    def along_x(piece, k):
        pairs = [(z * X_SIZE + x, z * X_SIZE + (x + k) % X_SIZE) for z in range(z_size) for x in range(X_SIZE)]
        return lax.ppermute(piece, "ctx", pairs)

    def along_z(piece, k):
        pairs = [(i, i + X_SIZE) for i in range(ctx - X_SIZE) if i % X_SIZE != k]
        return lax.ppermute(piece, "ctx", pairs)

    def arrived(pieces):
        return [pieces[0]] + [along_x(pieces[k], k) for k in range(1, X_SIZE)]

    taps = filter_taps.astype(jnp.bfloat16).reshape(X_SIZE, z_size, per_device, row_count)
    taps = taps.transpose(1, 0, 2, 3).reshape(ctx, per_device, row_count)
    own = arrived(pieces_of(x_index, key_rows, values))
    before = [along_z(own[k], k) for k in range(X_SIZE)]
    own[1], queries, in_gate = lax.optimization_barrier((own[1], queries, in_gate))
    asked = pieces_of(x_index, queries, in_gate)
    taps, *_ = lax.optimization_barrier((taps, *own, *asked))
    asked = arrived(asked)
    taps = exchanged(taps)

    group_first = (me // X_SIZE) * group_rows
    positions = group_first + jnp.arange(group_rows, dtype=jnp.int32)
    start = document_starts(positions, doc_lengths) - (group_first - group_rows)

    attended, gated = attention(x_index, own, before, asked, start)
    gated, taps = lax.optimization_barrier((gated, taps))
    signal = exchanged(gated.reshape(z_size, per_device, group_rows), z_groups)
    spectra = transform_taps(taps, tables)
    spectra, attended = lax.optimization_barrier((spectra, attended))
    attended = arrived([attended[k] for k in range(X_SIZE)])
    mixed = convolve(signal, spectra, tables, ctx)
    mixed, *attended = lax.optimization_barrier((mixed, *attended))
    returned = exchanged(mixed)
    return assembled(x_index, attended), finish(returned, out_gate)


def solution(mesh):
    return jax.shard_map(
        body,
        mesh=mesh,
        in_specs=(
            P(("dp", "ctx"), "tp"),
            P(("dp", "ctx"), "tp"),
            P(("dp", "ctx"), "tp"),
            P("dp"),
            P(("dp", "ctx"), "tp"),
            P(("dp", "ctx"), "tp"),
            P(("dp", "tp"), "ctx"),
        ),
        out_specs=(P(("dp", "ctx"), "tp"), P(("dp", "ctx"), "tp")),
        check_vma=False,
    )
```

```python
import functools
import math

import jax
import jax.numpy as jnp
import ml_dtypes
import numpy as np
from jax import lax
from jax.experimental import pallas as pl
from jax.experimental.pallas import tpu as pltpu
from jax.sharding import PartitionSpec as P

HEAD_DIM = 128
X_SIZE = 4
Q_BLOCK = 768
K_BLOCK = 384
LANES = 128
VMEM_LIMIT = 63 * 2**20
PAIRS = 4
masked_score = -1e30


def document_starts(positions, doc_lengths):
    order = jnp.arange(doc_lengths.shape[0], dtype=jnp.int32)
    before = order[:, None] < order[None, :]
    starts = jnp.sum(jnp.where(before, doc_lengths[:, None], 0), axis=0)
    inside = starts[None, :] <= positions[:, None]
    return jnp.max(jnp.where(inside, starts[None, :], 0), axis=1)


def pieces_kernel(x_ref, first_ref, second_ref, *rest):
    outs, (held, in_sems, out_sems) = rest[:X_SIZE], rest[X_SIZE:]
    arriving, leaving = [], []
    for k in range(X_SIZE):
        column = pl.multiple_of(lax.rem(x_ref[0] + k, X_SIZE) * HEAD_DIM, HEAD_DIM)
        for which, ref in enumerate((first_ref, second_ref)):
            copy = pltpu.make_async_copy(ref.at[:, pl.ds(column, HEAD_DIM)], held.at[k, which], in_sems.at[k, which])
            copy.start()
            arriving.append((k, which, copy))
    for k, which, copy in arriving:
        copy.wait()
        out = pltpu.make_async_copy(held.at[k, which], outs[k].at[which], out_sems.at[k, which])
        out.start()
        leaving.append(out)
    for out in leaving:
        out.wait()


def pieces_of(x_index, first, second):
    rows = first.shape[0]
    anywhere = pl.BlockSpec(memory_space=pl.ANY)
    return pl.pallas_call(
        pieces_kernel,
        name="pieces",
        in_specs=[pl.BlockSpec(memory_space=pltpu.SMEM), anywhere, anywhere],
        out_specs=[anywhere] * X_SIZE,
        out_shape=[jax.ShapeDtypeStruct((2, rows, HEAD_DIM), jnp.bfloat16)] * X_SIZE,
        scratch_shapes=[
            pltpu.VMEM((X_SIZE, 2, rows, HEAD_DIM), jnp.bfloat16),
            pltpu.SemaphoreType.DMA((X_SIZE, 2)),
            pltpu.SemaphoreType.DMA((X_SIZE, 2)),
        ],
    )(x_index, first, second)


def attention_kernel(lo_ref, mid_ref, x_ref, start_ref, *rest):
    own, before, asked = rest[:X_SIZE], rest[X_SIZE : 2 * X_SIZE], rest[2 * X_SIZE : 3 * X_SIZE]
    out_ref, gated_ref, keys, values, values_t, queries_all, gate_all, weighted_ref, sems = rest[3 * X_SIZE :]
    step = pl.program_id(0)
    group = queries_all.shape[0]
    piece = group // X_SIZE
    group_blocks = group // K_BLOCK
    piece_blocks = piece // K_BLOCK

    def copies_of(k, chosen, sources):
        at = pl.multiple_of(lax.rem(x_ref[0] + X_SIZE - k, X_SIZE) * piece, piece)
        early, late = pl.ds(at, piece), pl.ds(at + group, piece)
        targets = (keys.at[early], values.at[early], keys.at[late], values.at[late], queries_all.at[early], gate_all.at[early])
        return [pltpu.make_async_copy(sources[n // 2].at[n % 2], targets[n], sems.at[k, n]) for n in chosen]

    def reached(k):
        position = lax.rem(x_ref[0] + X_SIZE - k, X_SIZE)
        return jnp.logical_and(position > 0, (position + 1) * piece_blocks > lo_ref[0])

    def turn(block, _):
        rows = values[pl.ds(pl.multiple_of(block * K_BLOCK, K_BLOCK), K_BLOCK)]
        values_t[block] = rows.T
        return 0

    @pl.when(step == 0)
    def _():
        for k in range(X_SIZE):
            sources = (before[k], own[k], asked[k])

            @pl.when(reached(k))
            def _():
                for copy in copies_of(k, (0, 1), sources):
                    copy.start()

            for copy in copies_of(k, (2, 3, 4, 5), sources):
                copy.start()
        for k in range(X_SIZE):

            @pl.when(reached(k))
            def _():
                for copy in copies_of(k, (0, 1), (before[k], own[k], asked[k])):
                    copy.wait()

        lax.fori_loop(lo_ref[0], group_blocks, turn, 0)

    now = lax.rem(x_ref[0] + X_SIZE - step, X_SIZE)
    for copy in copies_of(now, (2, 3, 4, 5), (before[0], own[0], asked[0])):
        copy.wait()
    first = group + step * Q_BLOCK
    diagonal = first // K_BLOCK
    last = (first + Q_BLOCK - 1) // K_BLOCK
    lax.fori_loop(diagonal, last + 1, turn, 0)

    here = pl.ds(pl.multiple_of(step * Q_BLOCK, Q_BLOCK), Q_BLOCK)
    queries = queries_all[here].T
    start = start_ref[0]
    query_index = first + lax.broadcasted_iota(jnp.int32, (1, Q_BLOCK), 1)
    key_offset = lax.broadcasted_iota(jnp.int32, (K_BLOCK, 1), 0)
    factor = math.log2(math.e) / math.sqrt(HEAD_DIM)
    weighted_ref[...] = jnp.zeros_like(weighted_ref)

    def visit(kind, block, carried):
        top, total = carried
        key_rows = keys[pl.ds(pl.multiple_of(block * K_BLOCK, K_BLOCK), K_BLOCK)]
        scores = jnp.dot(key_rows, queries, preferred_element_type=jnp.float32) * factor
        index = block * K_BLOCK + key_offset
        if kind == "before":
            scores = jnp.where(index >= start, scores, masked_score)
        if kind == "diagonal":
            scores = jnp.where((index >= start) & (index <= query_index), scores, masked_score)
        new_top = jnp.maximum(top, jnp.max(scores, axis=0, keepdims=True))
        rescale = jnp.exp2(top - new_top)
        weight = jnp.exp2(scores - new_top)
        total = total * rescale + jnp.sum(weight, axis=0, keepdims=True)
        weighted_ref[...] = weighted_ref[...] * rescale + jnp.dot(
            values_t[block], weight.astype(jnp.bfloat16), preferred_element_type=jnp.float32
        )
        return new_top, total

    middle = jnp.minimum(mid_ref[step], diagonal)
    carried = (
        jnp.full((1, Q_BLOCK), masked_score, jnp.float32),
        jnp.zeros((1, Q_BLOCK), jnp.float32),
    )
    carried = lax.fori_loop(lo_ref[step], middle, functools.partial(visit, "before"), carried)
    carried = lax.fori_loop(middle, diagonal, functools.partial(visit, "inside"), carried)
    _, total = lax.fori_loop(diagonal, last + 1, functools.partial(visit, "diagonal"), carried)
    rounded = (weighted_ref[...] * (1.0 / total)).astype(jnp.bfloat16)
    out_ref[0] = rounded.T
    gated = rounded.astype(jnp.float32) * gate_all[here].T.astype(jnp.float32)
    gated_ref[...] = gated.astype(jnp.bfloat16)


def attention(x_index, own, before, asked, start):
    rows = X_SIZE * own[0].shape[1]
    steps = rows // Q_BLOCK
    lo = start[::Q_BLOCK] // K_BLOCK
    middle = start[Q_BLOCK - 1 :: Q_BLOCK] // K_BLOCK + 1
    anywhere = pl.BlockSpec(memory_space=pl.ANY)
    return pl.pallas_call(
        attention_kernel,
        name="attention",
        grid_spec=pltpu.PrefetchScalarGridSpec(
            num_scalar_prefetch=3,
            grid=(steps,),
            in_specs=[pl.BlockSpec((1, 1, Q_BLOCK), lambda i, *_: (i, 0, 0))] + [anywhere] * (3 * X_SIZE),
            out_specs=[
                pl.BlockSpec((1, Q_BLOCK, HEAD_DIM), lambda i, lo, mid, x: (lax.rem(i - x[0] + X_SIZE, X_SIZE), 0, 0)),
                pl.BlockSpec((HEAD_DIM, Q_BLOCK), lambda i, *_: (0, i)),
            ],
            scratch_shapes=[
                pltpu.VMEM((2 * rows, HEAD_DIM), jnp.bfloat16),
                pltpu.VMEM((2 * rows, HEAD_DIM), jnp.bfloat16),
                pltpu.VMEM((2 * rows // K_BLOCK, HEAD_DIM, K_BLOCK), jnp.bfloat16),
                pltpu.VMEM((rows, HEAD_DIM), jnp.bfloat16),
                pltpu.VMEM((rows, HEAD_DIM), jnp.bfloat16),
                pltpu.VMEM((HEAD_DIM, Q_BLOCK), jnp.float32),
                pltpu.SemaphoreType.DMA((X_SIZE, 6)),
            ],
        ),
        out_shape=[
            jax.ShapeDtypeStruct((X_SIZE, rows // X_SIZE, HEAD_DIM), jnp.bfloat16),
            jax.ShapeDtypeStruct((HEAD_DIM, rows), jnp.bfloat16),
        ],
        compiler_params=pltpu.CompilerParams(vmem_limit_bytes=VMEM_LIMIT),
        cost_estimate=pl.CostEstimate(
            flops=16 * 10**9, bytes_accessed=10 * rows * HEAD_DIM, transcendentals=rows * 1536
        ),
    )(lo, middle, x_index, start.reshape(steps, 1, Q_BLOCK), *own, *before, *asked)


def high_low(table):
    high = table.astype(np.float32).astype(ml_dtypes.bfloat16)
    low = (table - high.astype(np.float64)).astype(np.float32).astype(ml_dtypes.bfloat16)
    return np.stack((high, low))


def transform_tables(length, senders, tap_senders):
    outer = length // LANES
    k1 = np.arange(outer)
    per_sender = outer // senders
    a_signal = (np.arange(senders)[None, :] * per_sender + np.arange(per_sender)[:, None]).reshape(-1)
    per_tap = outer // tap_senders
    a_tap = (np.arange(tap_senders)[None, :] * per_tap + np.arange(per_tap)[:, None]).reshape(-1)
    b = np.arange(LANES)

    def angles(a):
        return 2.0 * np.pi * ((4 * k1[:, None] + 1) * a[None, :] % (4 * outer)) / (4 * outer)

    def forward(a):
        angle = angles(a)
        return high_low(np.concatenate((np.cos(angle), -np.sin(angle)), axis=0))

    twist = 2.0 * np.pi * ((4 * k1[:, None] + 1) * b[None, :] % (4 * length)) / (4 * length)
    inner = 2.0 * np.pi * (b[:, None] * b[None, :] % LANES) / LANES
    cos, sin = np.cos(inner), np.sin(inner)
    back = angles(a_tap).T
    return dict(
        signal=forward(a_signal),
        taps=forward(a_tap),
        twist=np.stack((np.cos(twist), -np.sin(twist))).astype(np.float32),
        inner=high_low(np.block([[cos, -sin], [sin, cos]])),
        inner_back=high_low(np.block([[cos, sin], [-sin, cos]])),
        back=high_low(np.concatenate((np.cos(back), -np.sin(back)), axis=1) / length),
    )


def table_dot(table_ref, right):
    return jnp.dot(table_ref[0], right, preferred_element_type=jnp.float32) + jnp.dot(
        table_ref[1], right, preferred_element_type=jnp.float32
    )


def dot_table(left, table_ref):
    return jnp.dot(left, table_ref[0], preferred_element_type=jnp.float32) + jnp.dot(
        left, table_ref[1], preferred_element_type=jnp.float32
    )


def spread(source_ref, spread_ref):
    rows = spread_ref.shape[1]
    for j in range(spread_ref.shape[0]):
        part = source_ref[:, :, j * LANES : (j + 1) * LANES]
        spread_ref[j] = part.reshape(rows, LANES).astype(jnp.float32)


def channel_rows(spread_ref, channel, channels):
    senders = spread_ref.shape[1] // channels
    pair = []
    for c in (channel, channel + 1):
        parts = [spread_ref[j, pl.ds(c, senders, stride=channels), :] for j in range(spread_ref.shape[0])]
        pair.append(jnp.concatenate(parts, axis=0).astype(jnp.bfloat16))
    return jnp.concatenate(pair, axis=1)


def spectra_of(pairs, outer_ref, twist_ref, inner_ref):
    outer = twist_ref.shape[1]
    turned = []
    for rows in pairs:
        section = table_dot(outer_ref, rows)
        for lane in (0, LANES):
            real, imag = section[:outer, lane : lane + LANES], section[outer:, lane : lane + LANES]
            turned_real = real * twist_ref[0] - imag * twist_ref[1]
            turned_imag = real * twist_ref[1] + imag * twist_ref[0]
            turned.append(jnp.concatenate((turned_real.astype(jnp.bfloat16), turned_imag.astype(jnp.bfloat16)), axis=1))
    return dot_table(jnp.concatenate(turned, axis=0), inner_ref)


def taps_kernel(taps_ref, outer_ref, twist_ref, inner_ref, out_ref, spread_ref):
    step = pl.program_id(0)
    channels = taps_ref.shape[1]

    @pl.when(step == 0)
    def _():
        spread(taps_ref, spread_ref)

    first = step * 2 * PAIRS
    pairs = [channel_rows(spread_ref, first + 2 * pair, channels) for pair in range(PAIRS)]
    out_ref[...] = spectra_of(pairs, outer_ref, twist_ref, inner_ref)


def conv_kernel(
    signal_ref, taps_ref, outer_ref, twist_ref, inner_ref, inner_back_ref, back_ref, out_ref, spread_ref, result_ref
):
    step = pl.program_id(0)
    channels = signal_ref.shape[1]
    receivers = out_ref.shape[0]
    outer = twist_ref.shape[1]

    @pl.when(step == 0)
    def _():
        spread(signal_ref, spread_ref)

    first = step * 2 * PAIRS
    pairs = [channel_rows(spread_ref, first + 2 * pair, channels) for pair in range(PAIRS)]
    signal = spectra_of(pairs, outer_ref, twist_ref, inner_ref)
    sig_real, sig_imag = signal[:, :LANES], signal[:, LANES:]
    tap_real, tap_imag = taps_ref[:, :LANES], taps_ref[:, LANES:]
    prod_real = sig_real * tap_real - sig_imag * tap_imag
    prod_imag = sig_real * tap_imag + sig_imag * tap_real
    prod = jnp.concatenate((prod_real.astype(jnp.bfloat16), prod_imag.astype(jnp.bfloat16)), axis=1)
    turned = dot_table(prod, inner_back_ref)
    for pair in range(PAIRS):
        channel = first + 2 * pair
        both = []
        for row in (2 * pair * outer, (2 * pair + 1) * outer):
            real, imag = turned[row : row + outer, :LANES], turned[row : row + outer, LANES:]
            back_real = real * twist_ref[0] + imag * twist_ref[1]
            back_imag = imag * twist_ref[0] - real * twist_ref[1]
            both.append(jnp.concatenate((back_real.astype(jnp.bfloat16), back_imag.astype(jnp.bfloat16)), axis=0))
        rows = table_dot(back_ref, jnp.concatenate(both, axis=1))
        for n in range(2):
            for j in range(result_ref.shape[0]):
                part = rows[j * receivers : (j + 1) * receivers, n * LANES : (n + 1) * LANES]
                result_ref[j, pl.ds(channel + n, receivers, stride=channels), :] = part

    @pl.when(step == pl.num_programs(0) - 1)
    def _():
        for j in range(result_ref.shape[0]):
            part = result_ref[j].reshape(receivers, channels, LANES)
            out_ref[:, :, j * LANES : (j + 1) * LANES] = part.astype(jnp.bfloat16)


def whole(array):
    return pl.BlockSpec(array.shape, lambda i: (0,) * array.ndim)


def transform_taps(taps, tables):
    senders, channels, rows = taps.shape
    outer = tables["twist"].shape[1]
    operands = (taps, tables["taps"], tables["twist"], tables["inner"])
    return pl.pallas_call(
        taps_kernel,
        name="taps_spectrum",
        grid=(channels // (2 * PAIRS),),
        in_specs=[whole(x) for x in operands],
        out_specs=pl.BlockSpec((PAIRS * 2 * outer, 2 * LANES), lambda i: (i, 0)),
        out_shape=jax.ShapeDtypeStruct((channels * outer, 2 * LANES), jnp.float32),
        scratch_shapes=[pltpu.VMEM((rows // LANES, senders * channels, LANES), jnp.float32)],
        compiler_params=pltpu.CompilerParams(vmem_limit_bytes=VMEM_LIMIT),
        cost_estimate=pl.CostEstimate(flops=5 * 10**9, bytes_accessed=4 * 2**20, transcendentals=0),
    )(*operands)


def convolve(signal, spectra, tables, receivers):
    senders, channels, rows = signal.shape
    out_rows = senders * rows // receivers
    outer = tables["twist"].shape[1]
    operands = [tables[n] for n in ("signal", "twist", "inner", "inner_back", "back")]
    return pl.pallas_call(
        conv_kernel,
        name="convolution",
        grid=(channels // (2 * PAIRS),),
        in_specs=[whole(signal), pl.BlockSpec((PAIRS * 2 * outer, 2 * LANES), lambda i: (i, 0))]
        + [whole(x) for x in operands],
        out_specs=pl.BlockSpec((receivers, channels, out_rows), lambda i: (0, 0, 0)),
        out_shape=jax.ShapeDtypeStruct((receivers, channels, out_rows), jnp.bfloat16),
        scratch_shapes=[
            pltpu.VMEM((rows // LANES, senders * channels, LANES), jnp.float32),
            pltpu.VMEM((out_rows // LANES, receivers * channels, LANES), jnp.float32),
        ],
        compiler_params=pltpu.CompilerParams(vmem_limit_bytes=VMEM_LIMIT),
        cost_estimate=pl.CostEstimate(flops=7 * 10**9, bytes_accessed=5 * 2**20, transcendentals=0),
    )(signal, spectra, *operands)


def assemble_kernel(x_ref, *rest):
    pieces, (out, held, in_sems, out_sems) = rest[:X_SIZE], rest[X_SIZE:]
    arriving = [pltpu.make_async_copy(pieces[k], held.at[k], in_sems.at[k]) for k in range(X_SIZE)]
    for copy in arriving:
        copy.start()
    leaving = []
    for k, copy in enumerate(arriving):
        column = pl.multiple_of(lax.rem(x_ref[0] + X_SIZE - k, X_SIZE) * HEAD_DIM, HEAD_DIM)
        copy.wait()
        out_copy = pltpu.make_async_copy(held.at[k], out.at[:, pl.ds(column, HEAD_DIM)], out_sems.at[k])
        out_copy.start()
        leaving.append(out_copy)
    for copy in leaving:
        copy.wait()


def assembled(x_index, pieces):
    rows = pieces[0].shape[0]
    anywhere = pl.BlockSpec(memory_space=pl.ANY)
    return pl.pallas_call(
        assemble_kernel,
        name="assemble",
        in_specs=[pl.BlockSpec(memory_space=pltpu.SMEM)] + [anywhere] * X_SIZE,
        out_specs=anywhere,
        out_shape=jax.ShapeDtypeStruct((rows, X_SIZE * HEAD_DIM), jnp.bfloat16),
        scratch_shapes=[
            pltpu.VMEM((X_SIZE, rows, HEAD_DIM), jnp.bfloat16),
            pltpu.SemaphoreType.DMA((X_SIZE,)),
            pltpu.SemaphoreType.DMA((X_SIZE,)),
        ],
        cost_estimate=pl.CostEstimate(flops=2 * 10**9, bytes_accessed=2**20, transcendentals=0),
    )(x_index, *pieces)


def finish_kernel(mixed_ref, gate_ref, hyena_ref):
    mixed = mixed_ref[...].reshape(HEAD_DIM, mixed_ref.shape[3]).T
    hyena_ref[...] = (gate_ref[...].astype(jnp.float32) * mixed.astype(jnp.float32)).astype(jnp.bfloat16)


def finish(returned, out_gate):
    rows, channels = out_gate.shape
    z_size = returned.shape[0] // X_SIZE
    returned = returned.reshape(z_size, X_SIZE, returned.shape[1], rows)
    by_columns = pl.BlockSpec((rows, HEAD_DIM), lambda i: (0, i))
    return pl.pallas_call(
        finish_kernel,
        name="finish",
        grid=(channels // HEAD_DIM,),
        in_specs=[pl.BlockSpec((z_size, 1, returned.shape[2], rows), lambda i: (0, i, 0, 0)), by_columns],
        out_specs=by_columns,
        out_shape=jax.ShapeDtypeStruct((rows, channels), jnp.bfloat16),
        compiler_params=pltpu.CompilerParams(vmem_limit_bytes=16 * 2**20),
    )(returned, out_gate)


def body(queries, key_rows, values, doc_lengths, in_gate, out_gate, filter_taps):
    row_count, channels = queries.shape
    ctx = lax.axis_size("ctx")
    z_size = ctx // X_SIZE
    group_rows = X_SIZE * row_count
    per_device = channels // ctx
    z_groups = [[z * X_SIZE + x for z in range(z_size)] for x in range(X_SIZE)]
    tables = transform_tables(row_count * ctx, z_size, ctx)
    me = lax.axis_index("ctx").astype(jnp.int32)
    x_index = lax.rem(me, X_SIZE).reshape(1)

    def exchanged(x, groups=None):
        return lax.all_to_all(x, "ctx", split_axis=0, concat_axis=0, tiled=True, axis_index_groups=groups)

    def along_x(piece, k):
        pairs = [(z * X_SIZE + x, z * X_SIZE + (x + k) % X_SIZE) for z in range(z_size) for x in range(X_SIZE)]
        return lax.ppermute(piece, "ctx", pairs)

    def along_z(piece, k):
        pairs = [(i, i + X_SIZE) for i in range(ctx - X_SIZE) if i % X_SIZE != k]
        return lax.ppermute(piece, "ctx", pairs)

    def arrived(pieces):
        return [pieces[0]] + [along_x(pieces[k], k) for k in range(1, X_SIZE)]

    taps = filter_taps.astype(jnp.bfloat16).reshape(X_SIZE, z_size, per_device, row_count)
    taps = taps.transpose(1, 0, 2, 3).reshape(ctx, per_device, row_count)
    own = arrived(pieces_of(x_index, key_rows, values))
    before = [along_z(own[k], k) for k in range(X_SIZE)]
    own[1], queries, in_gate = lax.optimization_barrier((own[1], queries, in_gate))
    asked = pieces_of(x_index, queries, in_gate)
    asked = arrived(asked)
    taps, *here = lax.optimization_barrier((taps, *before, *asked))
    before, asked = here[:X_SIZE], here[X_SIZE:]
    taps = exchanged(taps)

    group_first = (me // X_SIZE) * group_rows
    positions = group_first + jnp.arange(group_rows, dtype=jnp.int32)
    start = document_starts(positions, doc_lengths) - (group_first - group_rows)

    attended, gated = attention(x_index, own, before, asked, start)
    gated, taps = lax.optimization_barrier((gated, taps))
    signal = exchanged(gated.reshape(z_size, per_device, group_rows), z_groups)
    spectra = transform_taps(taps, tables)
    spectra, attended = lax.optimization_barrier((spectra, attended))
    attended = arrived([attended[k] for k in range(X_SIZE)])
    mixed = convolve(signal, spectra, tables, ctx)
    mixed, *attended = lax.optimization_barrier((mixed, *attended))
    returned = exchanged(mixed)
    return assembled(x_index, attended), finish(returned, out_gate)


def solution(mesh):
    return jax.shard_map(
        body,
        mesh=mesh,
        in_specs=(
            P(("dp", "ctx"), "tp"),
            P(("dp", "ctx"), "tp"),
            P(("dp", "ctx"), "tp"),
            P("dp"),
            P(("dp", "ctx"), "tp"),
            P(("dp", "ctx"), "tp"),
            P(("dp", "tp"), "ctx"),
        ),
        out_specs=(P(("dp", "ctx"), "tp"), P(("dp", "ctx"), "tp")),
        check_vma=False,
    )
```

```python
import functools
import math

import jax
import jax.numpy as jnp
import ml_dtypes
import numpy as np
from jax import lax
from jax.experimental import pallas as pl
from jax.experimental.pallas import tpu as pltpu
from jax.sharding import PartitionSpec as P

HEAD_DIM = 128
X_SIZE = 4
Q_BLOCK = 768
K_BLOCK = 384
LANES = 128
VMEM_LIMIT = 63 * 2**20
PAIRS = 4
masked_score = -1e30


def document_starts(positions, doc_lengths):
    order = jnp.arange(doc_lengths.shape[0], dtype=jnp.int32)
    before = order[:, None] < order[None, :]
    starts = jnp.sum(jnp.where(before, doc_lengths[:, None], 0), axis=0)
    inside = starts[None, :] <= positions[:, None]
    return jnp.max(jnp.where(inside, starts[None, :], 0), axis=1)


def pieces_kernel(x_ref, first_ref, second_ref, *rest):
    outs, (held, in_sems, out_sems) = rest[:X_SIZE], rest[X_SIZE:]
    arriving, leaving = [], []
    for k in range(X_SIZE):
        column = pl.multiple_of(lax.rem(x_ref[0] + k, X_SIZE) * HEAD_DIM, HEAD_DIM)
        for which, ref in enumerate((first_ref, second_ref)):
            copy = pltpu.make_async_copy(ref.at[:, pl.ds(column, HEAD_DIM)], held.at[k, which], in_sems.at[k, which])
            copy.start()
            arriving.append((k, which, copy))
    for k, which, copy in arriving:
        copy.wait()
        out = pltpu.make_async_copy(held.at[k, which], outs[k].at[which], out_sems.at[k, which])
        out.start()
        leaving.append(out)
    for out in leaving:
        out.wait()


def pieces_of(x_index, first, second):
    rows = first.shape[0]
    anywhere = pl.BlockSpec(memory_space=pl.ANY)
    return pl.pallas_call(
        pieces_kernel,
        name="pieces",
        in_specs=[pl.BlockSpec(memory_space=pltpu.SMEM), anywhere, anywhere],
        out_specs=[anywhere] * X_SIZE,
        out_shape=[jax.ShapeDtypeStruct((2, rows, HEAD_DIM), jnp.bfloat16)] * X_SIZE,
        scratch_shapes=[
            pltpu.VMEM((X_SIZE, 2, rows, HEAD_DIM), jnp.bfloat16),
            pltpu.SemaphoreType.DMA((X_SIZE, 2)),
            pltpu.SemaphoreType.DMA((X_SIZE, 2)),
        ],
    )(x_index, first, second)


def attention_kernel(lo_ref, mid_ref, x_ref, start_ref, *rest):
    own, before, asked = rest[:X_SIZE], rest[X_SIZE : 2 * X_SIZE], rest[2 * X_SIZE : 3 * X_SIZE]
    out_ref, gated_ref, keys, values, values_t, queries_all, gate_all, weighted_ref, sems = rest[3 * X_SIZE :]
    step = pl.program_id(0)
    group = queries_all.shape[0]
    piece = group // X_SIZE
    group_blocks = group // K_BLOCK
    piece_blocks = piece // K_BLOCK

    def copies_of(k, chosen, sources):
        at = pl.multiple_of(lax.rem(x_ref[0] + X_SIZE - k, X_SIZE) * piece, piece)
        early, late = pl.ds(at, piece), pl.ds(at + group, piece)
        targets = (keys.at[early], values.at[early], keys.at[late], values.at[late], queries_all.at[early], gate_all.at[early])
        return [pltpu.make_async_copy(sources[n // 2].at[n % 2], targets[n], sems.at[k, n]) for n in chosen]

    def reached(k):
        position = lax.rem(x_ref[0] + X_SIZE - k, X_SIZE)
        return jnp.logical_and(position > 0, (position + 1) * piece_blocks > lo_ref[0])

    def turn(block, _):
        rows = values[pl.ds(pl.multiple_of(block * K_BLOCK, K_BLOCK), K_BLOCK)]
        values_t[block] = rows.T
        return 0

    @pl.when(step == 0)
    def _():
        for k in range(X_SIZE):
            sources = (before[k], own[k], asked[k])

            @pl.when(reached(k))
            def _():
                for copy in copies_of(k, (0, 1), sources):
                    copy.start()

            for copy in copies_of(k, (2, 3, 4, 5), sources):
                copy.start()
        for k in range(X_SIZE):

            @pl.when(reached(k))
            def _():
                for copy in copies_of(k, (0, 1), (before[k], own[k], asked[k])):
                    copy.wait()

        lax.fori_loop(lo_ref[0], group_blocks, turn, 0)

    now = lax.rem(x_ref[0] + X_SIZE - step, X_SIZE)
    for copy in copies_of(now, (2, 3, 4, 5), (before[0], own[0], asked[0])):
        copy.wait()
    first = group + step * Q_BLOCK
    diagonal = first // K_BLOCK
    last = (first + Q_BLOCK - 1) // K_BLOCK
    lax.fori_loop(diagonal, last + 1, turn, 0)

    here = pl.ds(pl.multiple_of(step * Q_BLOCK, Q_BLOCK), Q_BLOCK)
    queries = queries_all[here].T
    start = start_ref[0]
    query_index = first + lax.broadcasted_iota(jnp.int32, (1, Q_BLOCK), 1)
    key_offset = lax.broadcasted_iota(jnp.int32, (K_BLOCK, 1), 0)
    factor = math.log2(math.e) / math.sqrt(HEAD_DIM)
    weighted_ref[...] = jnp.zeros_like(weighted_ref)

    def visit(kind, block, carried):
        top, total = carried
        key_rows = keys[pl.ds(pl.multiple_of(block * K_BLOCK, K_BLOCK), K_BLOCK)]
        scores = jnp.dot(key_rows, queries, preferred_element_type=jnp.float32) * factor
        index = block * K_BLOCK + key_offset
        if kind == "before":
            scores = jnp.where(index >= start, scores, masked_score)
        if kind == "diagonal":
            scores = jnp.where((index >= start) & (index <= query_index), scores, masked_score)
        new_top = jnp.maximum(top, jnp.max(scores, axis=0, keepdims=True))
        rescale = jnp.exp2(top - new_top)
        weight = jnp.exp2(scores - new_top)
        total = total * rescale + jnp.sum(weight, axis=0, keepdims=True)
        weighted_ref[...] = weighted_ref[...] * rescale + jnp.dot(
            values_t[block], weight.astype(jnp.bfloat16), preferred_element_type=jnp.float32
        )
        return new_top, total

    middle = jnp.minimum(mid_ref[step], diagonal)
    carried = (
        jnp.full((1, Q_BLOCK), masked_score, jnp.float32),
        jnp.zeros((1, Q_BLOCK), jnp.float32),
    )
    carried = lax.fori_loop(lo_ref[step], middle, functools.partial(visit, "before"), carried)
    carried = lax.fori_loop(middle, diagonal, functools.partial(visit, "inside"), carried)
    _, total = lax.fori_loop(diagonal, last + 1, functools.partial(visit, "diagonal"), carried)
    rounded = (weighted_ref[...] * (1.0 / total)).astype(jnp.bfloat16)
    out_ref[0] = rounded.T
    gated = rounded.astype(jnp.float32) * gate_all[here].T.astype(jnp.float32)
    gated_ref[...] = gated.astype(jnp.bfloat16)


def attention(x_index, own, before, asked, start):
    rows = X_SIZE * own[0].shape[1]
    steps = rows // Q_BLOCK
    lo = start[::Q_BLOCK] // K_BLOCK
    middle = start[Q_BLOCK - 1 :: Q_BLOCK] // K_BLOCK + 1
    anywhere = pl.BlockSpec(memory_space=pl.ANY)
    return pl.pallas_call(
        attention_kernel,
        name="attention",
        grid_spec=pltpu.PrefetchScalarGridSpec(
            num_scalar_prefetch=3,
            grid=(steps,),
            in_specs=[pl.BlockSpec((1, 1, Q_BLOCK), lambda i, *_: (i, 0, 0))] + [anywhere] * (3 * X_SIZE),
            out_specs=[
                pl.BlockSpec((1, Q_BLOCK, HEAD_DIM), lambda i, lo, mid, x: (lax.rem(i - x[0] + X_SIZE, X_SIZE), 0, 0)),
                pl.BlockSpec((HEAD_DIM, Q_BLOCK), lambda i, *_: (0, i)),
            ],
            scratch_shapes=[
                pltpu.VMEM((2 * rows, HEAD_DIM), jnp.bfloat16),
                pltpu.VMEM((2 * rows, HEAD_DIM), jnp.bfloat16),
                pltpu.VMEM((2 * rows // K_BLOCK, HEAD_DIM, K_BLOCK), jnp.bfloat16),
                pltpu.VMEM((rows, HEAD_DIM), jnp.bfloat16),
                pltpu.VMEM((rows, HEAD_DIM), jnp.bfloat16),
                pltpu.VMEM((HEAD_DIM, Q_BLOCK), jnp.float32),
                pltpu.SemaphoreType.DMA((X_SIZE, 6)),
            ],
        ),
        out_shape=[
            jax.ShapeDtypeStruct((X_SIZE, rows // X_SIZE, HEAD_DIM), jnp.bfloat16),
            jax.ShapeDtypeStruct((HEAD_DIM, rows), jnp.bfloat16),
        ],
        compiler_params=pltpu.CompilerParams(vmem_limit_bytes=VMEM_LIMIT),
        cost_estimate=pl.CostEstimate(
            flops=16 * 10**9, bytes_accessed=10 * rows * HEAD_DIM, transcendentals=rows * 1536
        ),
    )(lo, middle, x_index, start.reshape(steps, 1, Q_BLOCK), *own, *before, *asked)


def high_low(table):
    high = table.astype(np.float32).astype(ml_dtypes.bfloat16)
    low = (table - high.astype(np.float64)).astype(np.float32).astype(ml_dtypes.bfloat16)
    return np.stack((high, low))


def transform_tables(length, senders, tap_senders):
    outer = length // LANES
    k1 = np.arange(outer)
    per_sender = outer // senders
    a_signal = (np.arange(senders)[None, :] * per_sender + np.arange(per_sender)[:, None]).reshape(-1)
    per_tap = outer // tap_senders
    a_tap = (np.arange(tap_senders)[None, :] * per_tap + np.arange(per_tap)[:, None]).reshape(-1)
    b = np.arange(LANES)

    def angles(a):
        return 2.0 * np.pi * ((4 * k1[:, None] + 1) * a[None, :] % (4 * outer)) / (4 * outer)

    def forward(a):
        angle = angles(a)
        return high_low(np.concatenate((np.cos(angle), -np.sin(angle)), axis=0))

    twist = 2.0 * np.pi * ((4 * k1[:, None] + 1) * b[None, :] % (4 * length)) / (4 * length)
    inner = 2.0 * np.pi * (b[:, None] * b[None, :] % LANES) / LANES
    cos, sin = np.cos(inner), np.sin(inner)
    back = angles(a_tap).T
    return dict(
        signal=forward(a_signal),
        taps=forward(a_tap),
        twist=np.stack((np.cos(twist), -np.sin(twist))).astype(np.float32),
        inner=high_low(np.block([[cos, -sin], [sin, cos]])),
        inner_back=high_low(np.block([[cos, sin], [-sin, cos]])),
        back=high_low(np.concatenate((np.cos(back), -np.sin(back)), axis=1) / length),
    )


def table_dot(table_ref, right):
    return jnp.dot(table_ref[0], right, preferred_element_type=jnp.float32) + jnp.dot(
        table_ref[1], right, preferred_element_type=jnp.float32
    )


def dot_table(left, table_ref):
    return jnp.dot(left, table_ref[0], preferred_element_type=jnp.float32) + jnp.dot(
        left, table_ref[1], preferred_element_type=jnp.float32
    )


def spread(source_ref, spread_ref):
    rows = spread_ref.shape[1]
    for j in range(spread_ref.shape[0]):
        part = source_ref[:, :, j * LANES : (j + 1) * LANES]
        spread_ref[j] = part.reshape(rows, LANES).astype(jnp.float32)


def channel_rows(spread_ref, channel, channels):
    senders = spread_ref.shape[1] // channels
    pair = []
    for c in (channel, channel + 1):
        parts = [spread_ref[j, pl.ds(c, senders, stride=channels), :] for j in range(spread_ref.shape[0])]
        pair.append(jnp.concatenate(parts, axis=0).astype(jnp.bfloat16))
    return jnp.concatenate(pair, axis=1)


def spectra_of(pairs, outer_ref, twist_ref, inner_ref):
    outer = twist_ref.shape[1]
    turned = []
    for rows in pairs:
        section = table_dot(outer_ref, rows)
        for lane in (0, LANES):
            real, imag = section[:outer, lane : lane + LANES], section[outer:, lane : lane + LANES]
            turned_real = real * twist_ref[0] - imag * twist_ref[1]
            turned_imag = real * twist_ref[1] + imag * twist_ref[0]
            turned.append(jnp.concatenate((turned_real.astype(jnp.bfloat16), turned_imag.astype(jnp.bfloat16)), axis=1))
    return dot_table(jnp.concatenate(turned, axis=0), inner_ref)


def taps_kernel(taps_ref, outer_ref, twist_ref, inner_ref, out_ref, spread_ref):
    step = pl.program_id(0)
    channels = taps_ref.shape[1]

    @pl.when(step == 0)
    def _():
        spread(taps_ref, spread_ref)

    first = step * 2 * PAIRS
    pairs = [channel_rows(spread_ref, first + 2 * pair, channels) for pair in range(PAIRS)]
    out_ref[...] = spectra_of(pairs, outer_ref, twist_ref, inner_ref)


def conv_kernel(
    signal_ref, taps_ref, outer_ref, twist_ref, inner_ref, inner_back_ref, back_ref, out_ref, spread_ref, result_ref
):
    step = pl.program_id(0)
    channels = signal_ref.shape[1]
    receivers = out_ref.shape[0]
    outer = twist_ref.shape[1]

    @pl.when(step == 0)
    def _():
        spread(signal_ref, spread_ref)

    first = step * 2 * PAIRS
    pairs = [channel_rows(spread_ref, first + 2 * pair, channels) for pair in range(PAIRS)]
    signal = spectra_of(pairs, outer_ref, twist_ref, inner_ref)
    sig_real, sig_imag = signal[:, :LANES], signal[:, LANES:]
    tap_real, tap_imag = taps_ref[:, :LANES], taps_ref[:, LANES:]
    prod_real = sig_real * tap_real - sig_imag * tap_imag
    prod_imag = sig_real * tap_imag + sig_imag * tap_real
    prod = jnp.concatenate((prod_real.astype(jnp.bfloat16), prod_imag.astype(jnp.bfloat16)), axis=1)
    turned = dot_table(prod, inner_back_ref)
    for pair in range(PAIRS):
        channel = first + 2 * pair
        both = []
        for row in (2 * pair * outer, (2 * pair + 1) * outer):
            real, imag = turned[row : row + outer, :LANES], turned[row : row + outer, LANES:]
            back_real = real * twist_ref[0] + imag * twist_ref[1]
            back_imag = imag * twist_ref[0] - real * twist_ref[1]
            both.append(jnp.concatenate((back_real.astype(jnp.bfloat16), back_imag.astype(jnp.bfloat16)), axis=0))
        rows = table_dot(back_ref, jnp.concatenate(both, axis=1))
        for n in range(2):
            for j in range(result_ref.shape[0]):
                part = rows[j * receivers : (j + 1) * receivers, n * LANES : (n + 1) * LANES]
                result_ref[j, pl.ds(channel + n, receivers, stride=channels), :] = part

    @pl.when(step == pl.num_programs(0) - 1)
    def _():
        for j in range(result_ref.shape[0]):
            part = result_ref[j].reshape(receivers, channels, LANES)
            out_ref[:, :, j * LANES : (j + 1) * LANES] = part.astype(jnp.bfloat16)


def whole(array):
    return pl.BlockSpec(array.shape, lambda i: (0,) * array.ndim)


def transform_taps(taps, tables):
    senders, channels, rows = taps.shape
    outer = tables["twist"].shape[1]
    operands = (taps, tables["taps"], tables["twist"], tables["inner"])
    return pl.pallas_call(
        taps_kernel,
        name="taps_spectrum",
        grid=(channels // (2 * PAIRS),),
        in_specs=[whole(x) for x in operands],
        out_specs=pl.BlockSpec((PAIRS * 2 * outer, 2 * LANES), lambda i: (i, 0)),
        out_shape=jax.ShapeDtypeStruct((channels * outer, 2 * LANES), jnp.float32),
        scratch_shapes=[pltpu.VMEM((rows // LANES, senders * channels, LANES), jnp.float32)],
        compiler_params=pltpu.CompilerParams(vmem_limit_bytes=VMEM_LIMIT),
        cost_estimate=pl.CostEstimate(flops=5 * 10**9, bytes_accessed=4 * 2**20, transcendentals=0),
    )(*operands)


def convolve(signal, spectra, tables, receivers):
    senders, channels, rows = signal.shape
    out_rows = senders * rows // receivers
    outer = tables["twist"].shape[1]
    operands = [tables[n] for n in ("signal", "twist", "inner", "inner_back", "back")]
    return pl.pallas_call(
        conv_kernel,
        name="convolution",
        grid=(channels // (2 * PAIRS),),
        in_specs=[whole(signal), pl.BlockSpec((PAIRS * 2 * outer, 2 * LANES), lambda i: (i, 0))]
        + [whole(x) for x in operands],
        out_specs=pl.BlockSpec((receivers, channels, out_rows), lambda i: (0, 0, 0)),
        out_shape=jax.ShapeDtypeStruct((receivers, channels, out_rows), jnp.bfloat16),
        scratch_shapes=[
            pltpu.VMEM((rows // LANES, senders * channels, LANES), jnp.float32),
            pltpu.VMEM((out_rows // LANES, receivers * channels, LANES), jnp.float32),
        ],
        compiler_params=pltpu.CompilerParams(vmem_limit_bytes=VMEM_LIMIT),
        cost_estimate=pl.CostEstimate(flops=7 * 10**9, bytes_accessed=5 * 2**20, transcendentals=0),
    )(signal, spectra, *operands)


def assemble_kernel(x_ref, *rest):
    pieces, (out, held, in_sems, out_sems) = rest[:X_SIZE], rest[X_SIZE:]
    arriving = [pltpu.make_async_copy(pieces[k], held.at[k], in_sems.at[k]) for k in range(X_SIZE)]
    for copy in arriving:
        copy.start()
    leaving = []
    for k, copy in enumerate(arriving):
        column = pl.multiple_of(lax.rem(x_ref[0] + X_SIZE - k, X_SIZE) * HEAD_DIM, HEAD_DIM)
        copy.wait()
        out_copy = pltpu.make_async_copy(held.at[k], out.at[:, pl.ds(column, HEAD_DIM)], out_sems.at[k])
        out_copy.start()
        leaving.append(out_copy)
    for copy in leaving:
        copy.wait()


def assembled(x_index, pieces):
    rows = pieces[0].shape[0]
    anywhere = pl.BlockSpec(memory_space=pl.ANY)
    return pl.pallas_call(
        assemble_kernel,
        name="assemble",
        in_specs=[pl.BlockSpec(memory_space=pltpu.SMEM)] + [anywhere] * X_SIZE,
        out_specs=anywhere,
        out_shape=jax.ShapeDtypeStruct((rows, X_SIZE * HEAD_DIM), jnp.bfloat16),
        scratch_shapes=[
            pltpu.VMEM((X_SIZE, rows, HEAD_DIM), jnp.bfloat16),
            pltpu.SemaphoreType.DMA((X_SIZE,)),
            pltpu.SemaphoreType.DMA((X_SIZE,)),
        ],
        cost_estimate=pl.CostEstimate(flops=2 * 10**9, bytes_accessed=2**20, transcendentals=0),
    )(x_index, *pieces)


def finish_kernel(mixed_ref, gate_ref, hyena_ref):
    mixed = mixed_ref[...].reshape(HEAD_DIM, mixed_ref.shape[3]).T
    hyena_ref[...] = (gate_ref[...].astype(jnp.float32) * mixed.astype(jnp.float32)).astype(jnp.bfloat16)


def finish(returned, out_gate):
    rows, channels = out_gate.shape
    z_size = returned.shape[0] // X_SIZE
    returned = returned.reshape(z_size, X_SIZE, returned.shape[1], rows)
    by_columns = pl.BlockSpec((rows, HEAD_DIM), lambda i: (0, i))
    return pl.pallas_call(
        finish_kernel,
        name="finish",
        grid=(channels // HEAD_DIM,),
        in_specs=[pl.BlockSpec((z_size, 1, returned.shape[2], rows), lambda i: (0, i, 0, 0)), by_columns],
        out_specs=by_columns,
        out_shape=jax.ShapeDtypeStruct((rows, channels), jnp.bfloat16),
        compiler_params=pltpu.CompilerParams(vmem_limit_bytes=16 * 2**20),
    )(returned, out_gate)


def body(queries, key_rows, values, doc_lengths, in_gate, out_gate, filter_taps):
    row_count, channels = queries.shape
    ctx = lax.axis_size("ctx")
    z_size = ctx // X_SIZE
    group_rows = X_SIZE * row_count
    per_device = channels // ctx
    z_groups = [[z * X_SIZE + x for z in range(z_size)] for x in range(X_SIZE)]
    tables = transform_tables(row_count * ctx, z_size, ctx)
    me = lax.axis_index("ctx").astype(jnp.int32)
    x_index = lax.rem(me, X_SIZE).reshape(1)

    def exchanged(x, groups=None):
        return lax.all_to_all(x, "ctx", split_axis=0, concat_axis=0, tiled=True, axis_index_groups=groups)

    def along_x(piece, k):
        pairs = [(z * X_SIZE + x, z * X_SIZE + (x + k) % X_SIZE) for z in range(z_size) for x in range(X_SIZE)]
        return lax.ppermute(piece, "ctx", pairs)

    def along_z(piece, k):
        pairs = [(i, i + X_SIZE) for i in range(ctx - X_SIZE) if i % X_SIZE != k]
        return lax.ppermute(piece, "ctx", pairs)

    def arrived(pieces):
        return [pieces[0]] + [along_x(pieces[k], k) for k in range(1, X_SIZE)]

    taps = filter_taps.astype(jnp.bfloat16).reshape(X_SIZE, z_size, per_device, row_count)
    taps = taps.transpose(1, 0, 2, 3).reshape(ctx, per_device, row_count)
    own = arrived(pieces_of(x_index, key_rows, values))
    before = [along_z(own[k], k) for k in range(X_SIZE)]
    own[1], queries, in_gate = lax.optimization_barrier((own[1], queries, in_gate))
    asked = pieces_of(x_index, queries, in_gate)
    asked = list(asked)
    before[0], before[1], asked[2], asked[3] = lax.optimization_barrier((before[0], before[1], asked[2], asked[3]))
    taps, *_ = lax.optimization_barrier((taps, *own, *asked))
    asked = arrived(asked)
    taps = exchanged(taps)

    group_first = (me // X_SIZE) * group_rows
    positions = group_first + jnp.arange(group_rows, dtype=jnp.int32)
    start = document_starts(positions, doc_lengths) - (group_first - group_rows)

    attended, gated = attention(x_index, own, before, asked, start)
    gated, taps = lax.optimization_barrier((gated, taps))
    signal = exchanged(gated.reshape(z_size, per_device, group_rows), z_groups)
    spectra = transform_taps(taps, tables)
    spectra, attended = lax.optimization_barrier((spectra, attended))
    attended = arrived([attended[k] for k in range(X_SIZE)])
    mixed = convolve(signal, spectra, tables, ctx)
    mixed, *attended = lax.optimization_barrier((mixed, *attended))
    returned = exchanged(mixed)
    return assembled(x_index, attended), finish(returned, out_gate)


def solution(mesh):
    return jax.shard_map(
        body,
        mesh=mesh,
        in_specs=(
            P(("dp", "ctx"), "tp"),
            P(("dp", "ctx"), "tp"),
            P(("dp", "ctx"), "tp"),
            P("dp"),
            P(("dp", "ctx"), "tp"),
            P(("dp", "ctx"), "tp"),
            P(("dp", "tp"), "ctx"),
        ),
        out_specs=(P(("dp", "ctx"), "tp"), P(("dp", "ctx"), "tp")),
        check_vma=False,
    )
```

```python
import functools
import math

import jax
import jax.numpy as jnp
import ml_dtypes
import numpy as np
from jax import lax
from jax.experimental import pallas as pl
from jax.experimental.pallas import tpu as pltpu
from jax.sharding import PartitionSpec as P

HEAD_DIM = 128
X_SIZE = 4
Q_BLOCK = 768
K_BLOCK = 384
LANES = 128
VMEM_LIMIT = 63 * 2**20
PAIRS = 4
masked_score = -1e30


def document_starts(positions, doc_lengths):
    order = jnp.arange(doc_lengths.shape[0], dtype=jnp.int32)
    before = order[:, None] < order[None, :]
    starts = jnp.sum(jnp.where(before, doc_lengths[:, None], 0), axis=0)
    inside = starts[None, :] <= positions[:, None]
    return jnp.max(jnp.where(inside, starts[None, :], 0), axis=1)


def pieces_kernel(x_ref, first_ref, second_ref, *rest):
    outs, (held, in_sems, out_sems) = rest[:X_SIZE], rest[X_SIZE:]
    arriving, leaving = [], []
    for k in range(X_SIZE):
        column = pl.multiple_of(lax.rem(x_ref[0] + k, X_SIZE) * HEAD_DIM, HEAD_DIM)
        for which, ref in enumerate((first_ref, second_ref)):
            copy = pltpu.make_async_copy(ref.at[:, pl.ds(column, HEAD_DIM)], held.at[k, which], in_sems.at[k, which])
            copy.start()
            arriving.append((k, which, copy))
    for k, which, copy in arriving:
        copy.wait()
        out = pltpu.make_async_copy(held.at[k, which], outs[k].at[which], out_sems.at[k, which])
        out.start()
        leaving.append(out)
    for out in leaving:
        out.wait()


def pieces_of(x_index, first, second):
    rows = first.shape[0]
    anywhere = pl.BlockSpec(memory_space=pl.ANY)
    return pl.pallas_call(
        pieces_kernel,
        name="pieces",
        in_specs=[pl.BlockSpec(memory_space=pltpu.SMEM), anywhere, anywhere],
        out_specs=[anywhere] * X_SIZE,
        out_shape=[jax.ShapeDtypeStruct((2, rows, HEAD_DIM), jnp.bfloat16)] * X_SIZE,
        scratch_shapes=[
            pltpu.VMEM((X_SIZE, 2, rows, HEAD_DIM), jnp.bfloat16),
            pltpu.SemaphoreType.DMA((X_SIZE, 2)),
            pltpu.SemaphoreType.DMA((X_SIZE, 2)),
        ],
    )(x_index, first, second)


def attention_kernel(lo_ref, mid_ref, x_ref, start_ref, *rest):
    own, before, asked = rest[:X_SIZE], rest[X_SIZE : 2 * X_SIZE], rest[2 * X_SIZE : 3 * X_SIZE]
    out_ref, gated_ref, keys, values, values_t, queries_all, gate_all, weighted_ref, sems = rest[3 * X_SIZE :]
    step = pl.program_id(0)
    group = queries_all.shape[0]
    piece = group // X_SIZE
    group_blocks = group // K_BLOCK
    piece_blocks = piece // K_BLOCK

    def copies_of(k, chosen, sources):
        at = pl.multiple_of(lax.rem(x_ref[0] + X_SIZE - k, X_SIZE) * piece, piece)
        early, late = pl.ds(at, piece), pl.ds(at + group, piece)
        targets = (keys.at[early], values.at[early], keys.at[late], values.at[late], queries_all.at[early], gate_all.at[early])
        return [pltpu.make_async_copy(sources[n // 2].at[n % 2], targets[n], sems.at[k, n]) for n in chosen]

    def reached(k):
        position = lax.rem(x_ref[0] + X_SIZE - k, X_SIZE)
        return jnp.logical_and(position > 0, (position + 1) * piece_blocks > lo_ref[0])

    def turn(block, _):
        rows = values[pl.ds(pl.multiple_of(block * K_BLOCK, K_BLOCK), K_BLOCK)]
        values_t[block] = rows.T
        return 0

    @pl.when(step == 0)
    def _():
        for k in range(X_SIZE):
            sources = (before[k], own[k], asked[k])

            @pl.when(reached(k))
            def _():
                for copy in copies_of(k, (0, 1), sources):
                    copy.start()

            for copy in copies_of(k, (2, 3, 4, 5), sources):
                copy.start()
        for k in range(X_SIZE):

            @pl.when(reached(k))
            def _():
                for copy in copies_of(k, (0, 1), (before[k], own[k], asked[k])):
                    copy.wait()

        lax.fori_loop(lo_ref[0], group_blocks, turn, 0)

    now = lax.rem(x_ref[0] + X_SIZE - step, X_SIZE)
    for copy in copies_of(now, (2, 3, 4, 5), (before[0], own[0], asked[0])):
        copy.wait()
    first = group + step * Q_BLOCK
    diagonal = first // K_BLOCK
    last = (first + Q_BLOCK - 1) // K_BLOCK
    lax.fori_loop(diagonal, last + 1, turn, 0)

    here = pl.ds(pl.multiple_of(step * Q_BLOCK, Q_BLOCK), Q_BLOCK)
    queries = queries_all[here].T
    start = start_ref[0]
    query_index = first + lax.broadcasted_iota(jnp.int32, (1, Q_BLOCK), 1)
    key_offset = lax.broadcasted_iota(jnp.int32, (K_BLOCK, 1), 0)
    factor = math.log2(math.e) / math.sqrt(HEAD_DIM)
    weighted_ref[...] = jnp.zeros_like(weighted_ref)

    def visit(kind, block, carried):
        top, total = carried
        key_rows = keys[pl.ds(pl.multiple_of(block * K_BLOCK, K_BLOCK), K_BLOCK)]
        scores = jnp.dot(key_rows, queries, preferred_element_type=jnp.float32) * factor
        index = block * K_BLOCK + key_offset
        if kind == "before":
            scores = jnp.where(index >= start, scores, masked_score)
        if kind == "diagonal":
            scores = jnp.where((index >= start) & (index <= query_index), scores, masked_score)
        new_top = jnp.maximum(top, jnp.max(scores, axis=0, keepdims=True))
        rescale = jnp.exp2(top - new_top)
        weight = jnp.exp2(scores - new_top)
        total = total * rescale + jnp.sum(weight, axis=0, keepdims=True)
        weighted_ref[...] = weighted_ref[...] * rescale + jnp.dot(
            values_t[block], weight.astype(jnp.bfloat16), preferred_element_type=jnp.float32
        )
        return new_top, total

    middle = jnp.minimum(mid_ref[step], diagonal)
    carried = (
        jnp.full((1, Q_BLOCK), masked_score, jnp.float32),
        jnp.zeros((1, Q_BLOCK), jnp.float32),
    )
    carried = lax.fori_loop(lo_ref[step], middle, functools.partial(visit, "before"), carried)
    carried = lax.fori_loop(middle, diagonal, functools.partial(visit, "inside"), carried)
    _, total = lax.fori_loop(diagonal, last + 1, functools.partial(visit, "diagonal"), carried)
    rounded = (weighted_ref[...] * (1.0 / total)).astype(jnp.bfloat16)
    out_ref[0] = rounded.T
    gated = rounded.astype(jnp.float32) * gate_all[here].T.astype(jnp.float32)
    gated_ref[...] = gated.astype(jnp.bfloat16)


def attention(x_index, own, before, asked, start):
    rows = X_SIZE * own[0].shape[1]
    steps = rows // Q_BLOCK
    lo = start[::Q_BLOCK] // K_BLOCK
    middle = start[Q_BLOCK - 1 :: Q_BLOCK] // K_BLOCK + 1
    anywhere = pl.BlockSpec(memory_space=pl.ANY)
    return pl.pallas_call(
        attention_kernel,
        name="attention",
        grid_spec=pltpu.PrefetchScalarGridSpec(
            num_scalar_prefetch=3,
            grid=(steps,),
            in_specs=[pl.BlockSpec((1, 1, Q_BLOCK), lambda i, *_: (i, 0, 0))] + [anywhere] * (3 * X_SIZE),
            out_specs=[
                pl.BlockSpec((1, Q_BLOCK, HEAD_DIM), lambda i, lo, mid, x: (lax.rem(i - x[0] + X_SIZE, X_SIZE), 0, 0)),
                pl.BlockSpec((HEAD_DIM, Q_BLOCK), lambda i, *_: (0, i)),
            ],
            scratch_shapes=[
                pltpu.VMEM((2 * rows, HEAD_DIM), jnp.bfloat16),
                pltpu.VMEM((2 * rows, HEAD_DIM), jnp.bfloat16),
                pltpu.VMEM((2 * rows // K_BLOCK, HEAD_DIM, K_BLOCK), jnp.bfloat16),
                pltpu.VMEM((rows, HEAD_DIM), jnp.bfloat16),
                pltpu.VMEM((rows, HEAD_DIM), jnp.bfloat16),
                pltpu.VMEM((HEAD_DIM, Q_BLOCK), jnp.float32),
                pltpu.SemaphoreType.DMA((X_SIZE, 6)),
            ],
        ),
        out_shape=[
            jax.ShapeDtypeStruct((X_SIZE, rows // X_SIZE, HEAD_DIM), jnp.bfloat16),
            jax.ShapeDtypeStruct((HEAD_DIM, rows), jnp.bfloat16),
        ],
        compiler_params=pltpu.CompilerParams(vmem_limit_bytes=VMEM_LIMIT),
        cost_estimate=pl.CostEstimate(
            flops=16 * 10**9, bytes_accessed=10 * rows * HEAD_DIM, transcendentals=rows * 1536
        ),
    )(lo, middle, x_index, start.reshape(steps, 1, Q_BLOCK), *own, *before, *asked)


def high_low(table):
    high = table.astype(np.float32).astype(ml_dtypes.bfloat16)
    low = (table - high.astype(np.float64)).astype(np.float32).astype(ml_dtypes.bfloat16)
    return np.stack((high, low))


def transform_tables(length, senders, tap_senders):
    outer = length // LANES
    k1 = np.arange(outer)
    per_sender = outer // senders
    a_signal = (np.arange(senders)[None, :] * per_sender + np.arange(per_sender)[:, None]).reshape(-1)
    per_tap = outer // tap_senders
    a_tap = (np.arange(tap_senders)[None, :] * per_tap + np.arange(per_tap)[:, None]).reshape(-1)
    b = np.arange(LANES)

    def angles(a):
        return 2.0 * np.pi * ((4 * k1[:, None] + 1) * a[None, :] % (4 * outer)) / (4 * outer)

    def forward(a):
        angle = angles(a)
        return high_low(np.concatenate((np.cos(angle), -np.sin(angle)), axis=0))

    twist = 2.0 * np.pi * ((4 * k1[:, None] + 1) * b[None, :] % (4 * length)) / (4 * length)
    inner = 2.0 * np.pi * (b[:, None] * b[None, :] % LANES) / LANES
    cos, sin = np.cos(inner), np.sin(inner)
    back = angles(a_tap).T
    return dict(
        signal=forward(a_signal),
        taps=forward(a_tap),
        twist=np.stack((np.cos(twist), -np.sin(twist))).astype(np.float32),
        inner=high_low(np.block([[cos, -sin], [sin, cos]])),
        inner_back=high_low(np.block([[cos, sin], [-sin, cos]])),
        back=high_low(np.concatenate((np.cos(back), -np.sin(back)), axis=1) / length),
    )


def table_dot(table_ref, right):
    return jnp.dot(table_ref[0], right, preferred_element_type=jnp.float32) + jnp.dot(
        table_ref[1], right, preferred_element_type=jnp.float32
    )


def dot_table(left, table_ref):
    return jnp.dot(left, table_ref[0], preferred_element_type=jnp.float32) + jnp.dot(
        left, table_ref[1], preferred_element_type=jnp.float32
    )


def spread(source_ref, spread_ref):
    rows = spread_ref.shape[1]
    for j in range(spread_ref.shape[0]):
        part = source_ref[:, :, j * LANES : (j + 1) * LANES]
        spread_ref[j] = part.reshape(rows, LANES).astype(jnp.float32)


def channel_rows(spread_ref, channel, channels):
    senders = spread_ref.shape[1] // channels
    pair = []
    for c in (channel, channel + 1):
        parts = [spread_ref[j, pl.ds(c, senders, stride=channels), :] for j in range(spread_ref.shape[0])]
        pair.append(jnp.concatenate(parts, axis=0).astype(jnp.bfloat16))
    return jnp.concatenate(pair, axis=1)


def spectra_of(pairs, outer_ref, twist_ref, inner_ref):
    outer = twist_ref.shape[1]
    turned = []
    for rows in pairs:
        section = table_dot(outer_ref, rows)
        for lane in (0, LANES):
            real, imag = section[:outer, lane : lane + LANES], section[outer:, lane : lane + LANES]
            turned_real = real * twist_ref[0] - imag * twist_ref[1]
            turned_imag = real * twist_ref[1] + imag * twist_ref[0]
            turned.append(jnp.concatenate((turned_real.astype(jnp.bfloat16), turned_imag.astype(jnp.bfloat16)), axis=1))
    return dot_table(jnp.concatenate(turned, axis=0), inner_ref)


def taps_kernel(taps_ref, outer_ref, twist_ref, inner_ref, out_ref, spread_ref):
    step = pl.program_id(0)
    channels = taps_ref.shape[1]

    @pl.when(step == 0)
    def _():
        spread(taps_ref, spread_ref)

    first = step * 2 * PAIRS
    pairs = [channel_rows(spread_ref, first + 2 * pair, channels) for pair in range(PAIRS)]
    out_ref[...] = spectra_of(pairs, outer_ref, twist_ref, inner_ref)


def conv_kernel(
    signal_ref, taps_ref, outer_ref, twist_ref, inner_ref, inner_back_ref, back_ref, out_ref, spread_ref, result_ref
):
    step = pl.program_id(0)
    channels = signal_ref.shape[1]
    receivers = out_ref.shape[0]
    outer = twist_ref.shape[1]

    @pl.when(step == 0)
    def _():
        spread(signal_ref, spread_ref)

    first = step * 2 * PAIRS
    pairs = [channel_rows(spread_ref, first + 2 * pair, channels) for pair in range(PAIRS)]
    signal = spectra_of(pairs, outer_ref, twist_ref, inner_ref)
    sig_real, sig_imag = signal[:, :LANES], signal[:, LANES:]
    tap_real, tap_imag = taps_ref[:, :LANES], taps_ref[:, LANES:]
    prod_real = sig_real * tap_real - sig_imag * tap_imag
    prod_imag = sig_real * tap_imag + sig_imag * tap_real
    prod = jnp.concatenate((prod_real.astype(jnp.bfloat16), prod_imag.astype(jnp.bfloat16)), axis=1)
    turned = dot_table(prod, inner_back_ref)
    for pair in range(PAIRS):
        channel = first + 2 * pair
        both = []
        for row in (2 * pair * outer, (2 * pair + 1) * outer):
            real, imag = turned[row : row + outer, :LANES], turned[row : row + outer, LANES:]
            back_real = real * twist_ref[0] + imag * twist_ref[1]
            back_imag = imag * twist_ref[0] - real * twist_ref[1]
            both.append(jnp.concatenate((back_real.astype(jnp.bfloat16), back_imag.astype(jnp.bfloat16)), axis=0))
        rows = table_dot(back_ref, jnp.concatenate(both, axis=1))
        for n in range(2):
            for j in range(result_ref.shape[0]):
                part = rows[j * receivers : (j + 1) * receivers, n * LANES : (n + 1) * LANES]
                result_ref[j, pl.ds(channel + n, receivers, stride=channels), :] = part

    @pl.when(step == pl.num_programs(0) - 1)
    def _():
        for j in range(result_ref.shape[0]):
            part = result_ref[j].reshape(receivers, channels, LANES)
            out_ref[:, :, j * LANES : (j + 1) * LANES] = part.astype(jnp.bfloat16)


def whole(array):
    return pl.BlockSpec(array.shape, lambda i: (0,) * array.ndim)


def transform_taps(taps, tables):
    senders, channels, rows = taps.shape
    outer = tables["twist"].shape[1]
    operands = (taps, tables["taps"], tables["twist"], tables["inner"])
    return pl.pallas_call(
        taps_kernel,
        name="taps_spectrum",
        grid=(channels // (2 * PAIRS),),
        in_specs=[whole(x) for x in operands],
        out_specs=pl.BlockSpec((PAIRS * 2 * outer, 2 * LANES), lambda i: (i, 0)),
        out_shape=jax.ShapeDtypeStruct((channels * outer, 2 * LANES), jnp.float32),
        scratch_shapes=[pltpu.VMEM((rows // LANES, senders * channels, LANES), jnp.float32)],
        compiler_params=pltpu.CompilerParams(vmem_limit_bytes=VMEM_LIMIT),
        cost_estimate=pl.CostEstimate(flops=5 * 10**9, bytes_accessed=4 * 2**20, transcendentals=0),
    )(*operands)


def convolve(signal, spectra, tables, receivers):
    senders, channels, rows = signal.shape
    out_rows = senders * rows // receivers
    outer = tables["twist"].shape[1]
    operands = [tables[n] for n in ("signal", "twist", "inner", "inner_back", "back")]
    return pl.pallas_call(
        conv_kernel,
        name="convolution",
        grid=(channels // (2 * PAIRS),),
        in_specs=[whole(signal), pl.BlockSpec((PAIRS * 2 * outer, 2 * LANES), lambda i: (i, 0))]
        + [whole(x) for x in operands],
        out_specs=pl.BlockSpec((receivers, channels, out_rows), lambda i: (0, 0, 0)),
        out_shape=jax.ShapeDtypeStruct((receivers, channels, out_rows), jnp.bfloat16),
        scratch_shapes=[
            pltpu.VMEM((rows // LANES, senders * channels, LANES), jnp.float32),
            pltpu.VMEM((out_rows // LANES, receivers * channels, LANES), jnp.float32),
        ],
        compiler_params=pltpu.CompilerParams(vmem_limit_bytes=VMEM_LIMIT),
        cost_estimate=pl.CostEstimate(flops=7 * 10**9, bytes_accessed=5 * 2**20, transcendentals=0),
    )(signal, spectra, *operands)


def assemble_kernel(x_ref, *rest):
    pieces, (out, held, in_sems, out_sems) = rest[:X_SIZE], rest[X_SIZE:]
    arriving = [pltpu.make_async_copy(pieces[k], held.at[k], in_sems.at[k]) for k in range(X_SIZE)]
    for copy in arriving:
        copy.start()
    leaving = []
    for k, copy in enumerate(arriving):
        column = pl.multiple_of(lax.rem(x_ref[0] + X_SIZE - k, X_SIZE) * HEAD_DIM, HEAD_DIM)
        copy.wait()
        out_copy = pltpu.make_async_copy(held.at[k], out.at[:, pl.ds(column, HEAD_DIM)], out_sems.at[k])
        out_copy.start()
        leaving.append(out_copy)
    for copy in leaving:
        copy.wait()


def assembled(x_index, pieces):
    rows = pieces[0].shape[0]
    anywhere = pl.BlockSpec(memory_space=pl.ANY)
    return pl.pallas_call(
        assemble_kernel,
        name="assemble",
        in_specs=[pl.BlockSpec(memory_space=pltpu.SMEM)] + [anywhere] * X_SIZE,
        out_specs=anywhere,
        out_shape=jax.ShapeDtypeStruct((rows, X_SIZE * HEAD_DIM), jnp.bfloat16),
        scratch_shapes=[
            pltpu.VMEM((X_SIZE, rows, HEAD_DIM), jnp.bfloat16),
            pltpu.SemaphoreType.DMA((X_SIZE,)),
            pltpu.SemaphoreType.DMA((X_SIZE,)),
        ],
        cost_estimate=pl.CostEstimate(flops=2 * 10**9, bytes_accessed=2**20, transcendentals=0),
    )(x_index, *pieces)


def finish_kernel(mixed_ref, gate_ref, hyena_ref):
    mixed = mixed_ref[...].reshape(HEAD_DIM, mixed_ref.shape[3]).T
    hyena_ref[...] = (gate_ref[...].astype(jnp.float32) * mixed.astype(jnp.float32)).astype(jnp.bfloat16)


def finish(returned, out_gate):
    rows, channels = out_gate.shape
    z_size = returned.shape[0] // X_SIZE
    returned = returned.reshape(z_size, X_SIZE, returned.shape[1], rows)
    by_columns = pl.BlockSpec((rows, HEAD_DIM), lambda i: (0, i))
    return pl.pallas_call(
        finish_kernel,
        name="finish",
        grid=(channels // HEAD_DIM,),
        in_specs=[pl.BlockSpec((z_size, 1, returned.shape[2], rows), lambda i: (0, i, 0, 0)), by_columns],
        out_specs=by_columns,
        out_shape=jax.ShapeDtypeStruct((rows, channels), jnp.bfloat16),
        compiler_params=pltpu.CompilerParams(vmem_limit_bytes=16 * 2**20),
    )(returned, out_gate)


def body(queries, key_rows, values, doc_lengths, in_gate, out_gate, filter_taps):
    row_count, channels = queries.shape
    ctx = lax.axis_size("ctx")
    z_size = ctx // X_SIZE
    group_rows = X_SIZE * row_count
    per_device = channels // ctx
    z_groups = [[z * X_SIZE + x for z in range(z_size)] for x in range(X_SIZE)]
    tables = transform_tables(row_count * ctx, z_size, ctx)
    me = lax.axis_index("ctx").astype(jnp.int32)
    x_index = lax.rem(me, X_SIZE).reshape(1)

    def exchanged(x, groups=None):
        return lax.all_to_all(x, "ctx", split_axis=0, concat_axis=0, tiled=True, axis_index_groups=groups)

    def along_x(piece, k):
        pairs = [(z * X_SIZE + x, z * X_SIZE + (x + k) % X_SIZE) for z in range(z_size) for x in range(X_SIZE)]
        return lax.ppermute(piece, "ctx", pairs)

    def along_z(piece, k):
        pairs = [(i, i + X_SIZE) for i in range(ctx - X_SIZE) if i % X_SIZE != k]
        return lax.ppermute(piece, "ctx", pairs)

    def arrived(pieces):
        return [pieces[0]] + [along_x(pieces[k], k) for k in range(1, X_SIZE)]

    taps = filter_taps.astype(jnp.bfloat16).reshape(X_SIZE, z_size, per_device, row_count)
    taps = taps.transpose(1, 0, 2, 3).reshape(ctx, per_device, row_count)
    own = arrived(pieces_of(x_index, key_rows, values))
    before = [along_z(own[k], k) for k in range(X_SIZE)]
    own[1], queries, in_gate = lax.optimization_barrier((own[1], queries, in_gate))
    asked = pieces_of(x_index, queries, in_gate)
    asked = arrived(asked)
    taps, asked[1], asked[3], before[0], before[1] = lax.optimization_barrier(
        (taps, asked[1], asked[3], before[0], before[1])
    )
    taps = exchanged(taps)

    group_first = (me // X_SIZE) * group_rows
    positions = group_first + jnp.arange(group_rows, dtype=jnp.int32)
    start = document_starts(positions, doc_lengths) - (group_first - group_rows)

    attended, gated = attention(x_index, own, before, asked, start)
    gated, taps = lax.optimization_barrier((gated, taps))
    signal = exchanged(gated.reshape(z_size, per_device, group_rows), z_groups)
    spectra = transform_taps(taps, tables)
    spectra, attended = lax.optimization_barrier((spectra, attended))
    attended = arrived([attended[k] for k in range(X_SIZE)])
    mixed = convolve(signal, spectra, tables, ctx)
    mixed, *attended = lax.optimization_barrier((mixed, *attended))
    returned = exchanged(mixed)
    return assembled(x_index, attended), finish(returned, out_gate)


def solution(mesh):
    return jax.shard_map(
        body,
        mesh=mesh,
        in_specs=(
            P(("dp", "ctx"), "tp"),
            P(("dp", "ctx"), "tp"),
            P(("dp", "ctx"), "tp"),
            P("dp"),
            P(("dp", "ctx"), "tp"),
            P(("dp", "ctx"), "tp"),
            P(("dp", "tp"), "ctx"),
        ),
        out_specs=(P(("dp", "ctx"), "tp"), P(("dp", "ctx"), "tp")),
        check_vma=False,
    )
```
